32 devices in a mesh: dp: 8 (over z, x), section: 4 (over y, core).
Axes of the slice: x: 2, y: 2, z: 4, core: 2. Of those that a mesh axis runs over, the one named last changes fastest.
Arguments:
- pixels: bfloat16 [8192, 192], P('dp'), may hold values from -6 to 6
- cell_mask: int32 [8192, 192], P('dp'), may hold values 0 or 1
- lead_time: float32 [16], P('dp'), may hold values from 0.1 to 1
- query: bfloat16 [1024], replicated, may hold values from -6 to 6
- w_query: bfloat16 [1024, 1024], replicated, may hold values from -0.1875 to 0.1875
- w_key: bfloat16 [1024, 1024], replicated, may hold values from -0.1875 to 0.1875
- w_value: bfloat16 [1024, 1024], replicated, may hold values from -0.1875 to 0.1875
- b_value: float32 [1024], replicated, may hold values from -4 to 4
- w_out: bfloat16 [1024, 1024], replicated, may hold values from -0.5 to 0.5
- b_out: float32 [1024], replicated, may hold values from -4 to 4
- w_embed: bfloat16 [192, 1024], replicated, may hold values from -3 to 3
- var_embed: bfloat16 [48, 1024], replicated, may hold values from -6 to 6
- pos_embed: bfloat16 [512, 1024], replicated, may hold values from -6 to 6
- w_lead: float32 [1024], replicated, may hold values from -6 to 6
- b_lead: float32 [1024], replicated, may hold values from -6 to 6
- gain_one: float32 [1024], replicated, may hold values from 0.5 to 1.5
- shift_one: float32 [1024], replicated, may hold values from -4 to 4
- w_qkv: bfloat16 [1024, 3072], replicated, may hold values from -0.1875 to 0.1875
- w_proj: bfloat16 [1024, 1024], replicated, may hold values from -2 to 2
- b_proj: float32 [1024], replicated, may hold values from -4 to 4
- gain_two: float32 [1024], replicated, may hold values from 0.5 to 1.5
- shift_two: float32 [1024], replicated, may hold values from -4 to 4
- w_up: bfloat16 [1024, 4096], replicated, may hold values from -0.1875 to 0.1875
- b_up: float32 [4096], replicated, may hold values from -4 to 4
- w_down: bfloat16 [4096, 1024], replicated, may hold values from -0.125 to 0.125
- b_down: float32 [1024], replicated, may hold values from -4 to 4
- cotangent: bfloat16 [8192, 1024], P('dp'), may hold values from -6 to 6
Outputs:
- block_out: bfloat16 [8192, 1024], P(('dp', 'section'))
- pixels_grad: float32 [8192, 192], P(('dp', 'section'))
- query_grad: float32 [1024], P('dp')
- w_query_grad: float32 [1024, 1024], P('dp')
- w_key_grad: float32 [1024, 1024], P('dp')
- w_value_grad: float32 [1024, 1024], P('dp')
- b_value_grad: float32 [1024], P('dp')
- w_out_grad: float32 [1024, 1024], P('dp')
- b_out_grad: float32 [1024], P('dp')
- w_embed_grad: float32 [192, 1024], P(None, 'dp')
- var_embed_grad: float32 [48, 1024], P(None, 'dp')
- pos_embed_grad: float32 [512, 1024], P('dp')
- w_lead_grad: float32 [1024], P('dp')
- b_lead_grad: float32 [1024], P('dp')
- gain_one_grad: float32 [1024], P('dp')
- shift_one_grad: float32 [1024], P('dp')
- w_qkv_grad: float32 [1024, 3072], P('dp')
- w_proj_grad: float32 [1024, 1024], P('dp')
- b_proj_grad: float32 [1024], P('dp')
- gain_two_grad: float32 [1024], P('dp')
- shift_two_grad: float32 [1024], P('dp')
- w_up_grad: float32 [1024, 4096], P('dp')
- b_up_grad: float32 [4096], P('dp')
- w_down_grad: float32 [4096, 1024], P(None, 'dp')
- b_down_grad: float32 [1024], P('dp')
The draws below stay inside these ranges and needn't reach their ends.
All inputs are finite; a program needn't handle non-finite values. No bound on the sum of `cell_mask` on one device may be relied on, other than what follows from the above.
Results may differ from the reference program's by a relative error of at most 0.015.
Values may be sent and summed in bfloat16 or wider, within the bound.
No kernel may reach another device: no remote copies, remote signals or barrier semaphores. Data moves between devices by JAX's collectives and lax.ppermute only.
A program may use at most 640 MiB of HBM per device.

```python
import jax
import jax.numpy as jnp
from jax import lax

D = 1024
HEADS = 16
HD = 64
FF = 4096
VARS = 48
PIX = 4
SEQ = 512
SAMPLES = 16
TOKENS = 8192


def set_ends(values, own_key, low, top_value):
    spot = [jax.random.randint(jax.random.fold_in(own_key, axis), (), 0, length) for axis, length in enumerate(values.shape)]
    widest = values.shape.index(max(values.shape))
    next_to = spot[:widest] + [(spot[widest] + 1) % values.shape[widest]] + spot[widest + 1:]
    return values.at[tuple(spot)].set(low).at[tuple(next_to)].set(top_value)


def levels(key, dims, shards, smallest, largest):
    loudness = 1.0
    for axis_at, shards_of in shards:
        steps = jax.random.uniform(jax.random.fold_in(jax.random.fold_in(key, 6), axis_at), (shards_of,), jnp.float32, smallest / len(shards), largest / len(shards))
        loudness = loudness * jnp.repeat(jnp.exp(steps), dims[axis_at] // shards_of).reshape((-1,) + (1,) * (len(dims) - 1 - axis_at))
    return loudness


def centred(stream_key, shape, width, limit, pieces=(), held_as=jnp.bfloat16):
    level = levels(stream_key, shape, pieces, -0.22, 0.18) if pieces else 1.0
    values = jax.random.normal(stream_key, shape, jnp.float32) * width * level
    return jnp.minimum(jnp.maximum(values, -limit), limit).astype(held_as)


def setup_inputs(seed: int = 0) -> dict:
    key_of = jax.random.split(jax.random.key(seed), 28)
    pixels = centred(key_of[0], (TOKENS, VARS * PIX), 1.0, 6.0, ((0, 8),))
    cell_mask = set_ends((jax.random.randint(key_of[1], (TOKENS, VARS * PIX), 0, 4) < 3).astype(jnp.int32), jax.random.fold_in(key_of[1], 1), 0, 1)
    lead_time = jnp.clip(0.1 + 0.9 * jax.random.uniform(key_of[2], (SAMPLES,), jnp.float32) ** levels(key_of[2], (SAMPLES,), ((0, 8),), -0.2, 0.2), 0.1, 1.0)
    query = centred(key_of[3], (D,), 1.0, 6.0)
    w_query = centred(key_of[4], (D, D), D ** -0.5, 0.1875)
    w_key = centred(key_of[5], (D, D), D ** -0.5, 0.1875)
    w_value = centred(key_of[6], (D, D), D ** -0.5, 0.1875)
    b_value = centred(key_of[7], (D,), 0.3, 4.0, (), jnp.float32)
    w_out = centred(key_of[8], (D, D), (D // 8) ** -0.5, 0.5)
    b_out = centred(key_of[9], (D,), 0.3, 4.0, (), jnp.float32)
    w_embed = centred(key_of[10], (VARS * PIX, D), PIX ** -0.5, 3.0)
    var_embed = centred(key_of[11], (VARS, D), 1.0, 6.0)
    pos_embed = centred(key_of[12], (SEQ, D), 0.5, 6.0)
    w_lead = centred(key_of[13], (D,), 1.0, 6.0, (), jnp.float32)
    b_lead = centred(key_of[14], (D,), 0.5, 6.0, (), jnp.float32)
    gain_one = jnp.clip(1.0 + 0.1 * jax.random.normal(key_of[15], (D,), jnp.float32), 0.5, 1.5)
    shift_one = centred(key_of[16], (D,), 0.3, 4.0, (), jnp.float32)
    w_qkv = centred(key_of[17], (D, 3 * D), D ** -0.5, 0.1875)
    w_proj = centred(key_of[18], (D, D), (max(1, 4 * D // SEQ)) ** -0.5, 2.0)
    b_proj = centred(key_of[19], (D,), 0.3, 4.0, (), jnp.float32)
    gain_two = jnp.clip(1.0 + 0.1 * jax.random.normal(key_of[20], (D,), jnp.float32), 0.5, 1.5)
    shift_two = centred(key_of[21], (D,), 0.3, 4.0, (), jnp.float32)
    w_up = centred(key_of[22], (D, FF), D ** -0.5, 0.1875)
    b_up = centred(key_of[23], (FF,), 0.3, 4.0, (), jnp.float32)
    w_down = centred(key_of[24], (FF, D), (FF // 2) ** -0.5, 0.125)
    b_down = centred(key_of[25], (D,), 0.3, 4.0, (), jnp.float32)
    cotangent = centred(key_of[26], (TOKENS, D), 1.0, 6.0, ((0, 8),))
    return dict(pixels=pixels, cell_mask=cell_mask, lead_time=lead_time, query=query, w_query=w_query, w_key=w_key, w_value=w_value, b_value=b_value, w_out=w_out, b_out=b_out, w_embed=w_embed, var_embed=var_embed, pos_embed=pos_embed, w_lead=w_lead, b_lead=b_lead, gain_one=gain_one, shift_one=shift_one, w_qkv=w_qkv, w_proj=w_proj, b_proj=b_proj, gain_two=gain_two, shift_two=shift_two, w_up=w_up, b_up=b_up, w_down=w_down, b_down=b_down, cotangent=cotangent)


highest = lax.Precision.HIGHEST
epsilon = 1e-05

@jax.custom_vjp
def low(v):
    return lax.optimization_barrier(v.astype(jnp.bfloat16)).astype(jnp.float32)

@jax.custom_vjp
def low_back(v):
    return v

def low_keep(v):
    return (low(v), None)

def low_pass(kept, grad):
    return (grad,)

def back_keep(v):
    return (v, None)

def back_low(kept, grad):
    return (low(grad),)
low.defvjp(low_keep, low_pass)
low_back.defvjp(back_keep, back_low)

def product(pattern, left_back, right_back, left_side, right_side):
    return low_back(jnp.einsum(pattern, left_side, right_side, precision=highest))

def layer_norm(value, gain, shift):
    average = lax.optimization_barrier(jnp.mean(value, axis=-1, keepdims=True))
    centered = value - average
    inv_scale = lax.rsqrt(lax.optimization_barrier(jnp.mean(centered * centered, axis=-1, keepdims=True)) + epsilon)
    return centered * inv_scale * gain + shift

def aggregate(cells_in, present_cells, query, w_query, w_key, w_value, b_value, w_out, b_out, w_embed, var_embed, pos_embed):
    row_count = cells_in.shape[0]
    block_rows = min(512, row_count)
    cell_vals = cells_in * present_cells
    present = lax.optimization_barrier(jnp.max(present_cells.reshape(row_count, VARS, PIX), axis=2))
    query_vec = jnp.dot(query[None, :], w_query, precision=highest)[0].reshape(HEADS, HD)
    probe = jnp.einsum('dhe,he->dh', w_key.reshape(D, HEADS, HD), query_vec, precision=highest)
    embed_table = jnp.concatenate([w_embed, var_embed], axis=0)
    score_coef = jnp.dot(embed_table, probe, precision=highest) * 0.125
    pixel_coef = score_coef[:VARS * PIX].reshape(VARS, PIX, HEADS)
    var_coef = jnp.transpose(score_coef[VARS * PIX:])
    value_heads = w_value.reshape(D, HEADS, HD)

    def one_block(inputs):
        cell_block, present_block, pos_block = inputs
        grid_vals = cell_block.reshape(block_rows, VARS, PIX)
        scores = jnp.einsum('tvj,vjh->thv', grid_vals, pixel_coef, precision=highest)
        scores = scores + var_coef[None] + (present_block[:, None, :] - 1.0) * 10000.0
        agg_weight = jax.nn.softmax(scores, axis=-1)
        weighted = (agg_weight[:, :, :, None] * grid_vals[:, None]).reshape(block_rows, HEADS, VARS * PIX)
        features = low(jnp.concatenate([weighted, agg_weight], axis=-1))
        mixture = low(product('thk,kd->thd', 'thd,kd->thk', 'thk,thd->kd', features, embed_table))
        per_head = product('thd,dhe->the', 'the,dhe->thd', 'thd,the->dhe', mixture, value_heads)
        per_head = low(per_head.reshape(block_rows, D) + b_value)
        return low(product('td,de->te', 'te,de->td', 'td,te->de', per_head, w_out) + b_out + pos_block)
    outputs = lax.map(jax.checkpoint(one_block), (cell_vals.reshape(-1, block_rows, VARS * PIX), present.reshape(-1, block_rows, VARS), pos_embed.reshape(-1, block_rows, D)))
    return outputs.reshape(row_count, D)

def attend(start, lead_val, w_lead, b_lead, gain_one, shift_one, w_qkv, w_proj, b_proj):
    row_count = start.shape[0]
    block_rows = min(512, row_count)
    stream = start + lead_val * w_lead + b_lead
    normed = low(layer_norm(stream, gain_one, shift_one))
    packed = low(product('td,de->te', 'te,de->td', 'td,te->de', normed, w_qkv)).reshape(row_count, 3, HEADS, HD)
    queries = packed[:, 0]
    key_rows = packed[:, 1]
    values = packed[:, 2]

    def one_block(query_block):
        logits = product('qhd,khd->hqk', 'hqk,khd->qhd', 'qhd,hqk->khd', query_block, key_rows)
        probs = low(jax.nn.softmax(logits * 0.125, axis=-1))
        return product('hqk,khd->qhd', 'qhd,khd->hqk', 'hqk,qhd->khd', probs, values)
    attended = lax.map(jax.checkpoint(one_block), queries.reshape(-1, block_rows, HEADS, HD))
    attended = low(attended.reshape(row_count, D))
    return low(stream + product('td,de->te', 'te,de->td', 'td,te->de', attended, w_proj) + b_proj)

def mlp_half(stream, gain_two, shift_two, w_up, b_up, w_down):
    normed = low(layer_norm(stream, gain_two, shift_two))
    hidden = low(jax.nn.gelu(product('td,de->te', 'te,de->td', 'td,te->de', normed, w_up) + b_up))
    return product('td,de->te', 'te,de->td', 'td,te->de', hidden, w_down)

def layer(cells_in, present_cells, lead_val, weights):
    query, w_query, w_key, w_value, b_value, w_out, b_out, w_embed, var_embed, pos_embed, w_lead, b_lead, gain_one, shift_one, w_qkv, w_proj, b_proj, gain_two, shift_two, w_up, b_up, w_down, b_down = weights
    half_units = w_up.shape[1] // 2
    start = low_back(aggregate(cells_in, present_cells, query, w_query, w_key, w_value, b_value, w_out, b_out, w_embed, var_embed, pos_embed))
    mid = low_back(attend(start, lead_val, w_lead, b_lead, gain_one, shift_one, w_qkv, w_proj, b_proj))
    part_one = low_back(low(mlp_half(mid, gain_two, shift_two, w_up[:, :half_units], b_up[:half_units], w_down[:half_units])))
    relay = low_back(mid)
    part_two = mlp_half(relay, gain_two, shift_two, w_up[:, half_units:], b_up[half_units:], w_down[half_units:])
    return relay + part_one + part_two + b_down

def reference(pixels, cell_mask, lead_time, query, w_query, w_key, w_value, b_value, w_out, b_out, w_embed, var_embed, pos_embed, w_lead, b_lead, gain_one, shift_one, w_qkv, w_proj, b_proj, gain_two, shift_two, w_up, b_up, w_down, b_down, cotangent):
    weights = tuple((item.astype(jnp.float32) for item in (query, w_query, w_key, w_value, b_value, w_out, b_out, w_embed, var_embed, pos_embed, w_lead, b_lead, gain_one, shift_one, w_qkv, w_proj, b_proj, gain_two, shift_two, w_up, b_up, w_down, b_down)))
    samples = lead_time.shape[0]
    seq_len = pixels.shape[0] // samples
    cells_all = pixels.astype(jnp.float32).reshape(samples, seq_len, VARS * PIX)
    mask_all = cell_mask.astype(jnp.float32).reshape(samples, seq_len, VARS * PIX)
    cot_all = cotangent.astype(jnp.float32).reshape(samples, seq_len, D)

    def one_sample(totals, inputs):
        cells_in, present_cells, lead_val, cot_rows = inputs
        result, pullback = jax.vjp(lambda cell_arg, weight_arg: layer(cell_arg, present_cells, lead_val, weight_arg), cells_in, weights)
        cell_grad, weight_grads = pullback(cot_rows)
        summed = tuple((first_term + second_term for first_term, second_term in zip(totals, weight_grads)))
        return (summed, (result.astype(jnp.bfloat16), cell_grad))
    blank = tuple((jnp.zeros_like(item) for item in weights))
    totals, (outputs, cell_grads) = lax.scan(one_sample, blank, (cells_all, mask_all, lead_time.astype(jnp.float32), cot_all))
    g_query, g_wq, g_wk, g_wv, g_bv, g_wo, g_bo, g_embed, g_var, g_pos, g_wlead, g_blead, g_gain1, g_shift1, g_qkv, g_proj, g_bproj, g_gain2, g_shift2, g_up, g_bup, g_down, g_bdown = totals
    return (outputs.reshape(samples * seq_len, D), cell_grads.reshape(samples * seq_len, VARS * PIX), g_query, g_wq, g_wk, g_wv, g_bv, g_wo, g_bo, g_embed, g_var, g_pos, g_wlead, g_blead, g_gain1, g_shift1, g_qkv, g_proj, g_bproj, g_gain2, g_shift2, g_up, g_bup, g_down, g_bdown)
```

```python
import jax
import jax.numpy as jnp
from jax import lax
from jax.experimental import pallas as pl
from jax.experimental.pallas import tpu as pltpu
from jax.sharding import PartitionSpec as P

D = 1024
HEADS = 16
HD = 64
VARS = 48
PIX = 4
CELLS = VARS * PIX
ROWS = CELLS + VARS
PADDED = 256

highest = lax.Precision.HIGHEST
epsilon = 1e-05
bf16 = jnp.bfloat16
f32 = jnp.float32
axes = ("dp", "section")


def dot(a, b, contract, kind=f32, precision=None):
    return lax.dot_general(
        a, b, ((contract[:1], contract[1:]), ((), ())), precision=precision, preferred_element_type=kind
    )


def vmem(mb):
    return pltpu.CompilerParams(vmem_limit_bytes=mb << 20)


def head_weights(cells, pen, coef, h):
    scores = pen + coef[CELLS:ROWS, h : h + 1]
    for j in range(PIX):
        rows = slice(j * VARS, (j + 1) * VARS)
        scores = scores + cells[rows] * coef[rows, h : h + 1]
    raised = jnp.exp(scores - jnp.max(scores, axis=0, keepdims=True))
    return raised / jnp.sum(raised, axis=0, keepdims=True)


def head_features(cells, weight):
    parts = [weight * cells[j * VARS : (j + 1) * VARS] for j in range(PIX)]
    parts = parts + [weight, jnp.zeros((PADDED - ROWS, weight.shape[1]), f32)]
    return jnp.concatenate(parts, axis=0).astype(bf16)


def load_cells(pix_ref, mask_ref, perm_ref):
    mask = mask_ref[...].astype(f32).astype(bf16)
    masked = pix_ref[...] * mask
    cells = dot(perm_ref[...], masked, (1, 1))
    seen = dot(perm_ref[...], mask, (1, 1))
    present = seen[:VARS]
    for j in range(1, PIX):
        present = jnp.maximum(present, seen[j * VARS : (j + 1) * VARS])
    return cells, seen, (present - 1.0) * 10000.0


def aggregate_kernel(pix_ref, mask_ref, perm_ref, coef_ref, tv_ref, bias_ref, out_ref):
    cells, _, pen = load_cells(pix_ref, mask_ref, perm_ref)
    coef = coef_ref[...]
    for h in range(coef.shape[1]):
        rows = slice(h * HD, (h + 1) * HD)
        features = head_features(cells, head_weights(cells, pen, coef, h))
        out_ref[rows, :] = (dot(tv_ref[rows, :], features, (1, 0)) + bias_ref[rows, :]).astype(bf16)


def aggregate_back_kernel(
    pix_ref, mask_ref, perm_ref, coef_ref, tv_ref, grad_ref, g_ref, coef_grad_ref, pix_grad_ref
):
    cells, seen, pen = load_cells(pix_ref, mask_ref, perm_ref)
    coef = coef_ref[...]
    heads = coef.shape[1]
    lane = lax.broadcasted_iota(jnp.int32, (PADDED, 128), 1)
    coef_grad = jnp.zeros((PADDED, 128), f32)
    cell_grad = [jnp.zeros((VARS, cells.shape[1]), f32) for _ in range(PIX)]
    for h in range(heads):
        rows = slice(h * HD, (h + 1) * HD)
        weight = head_weights(cells, pen, coef, h)
        features = head_features(cells, weight)
        grad = grad_ref[rows, :]
        g_ref[rows, :] = dot(grad, features, (1, 1)).astype(g_ref.dtype)
        feature_grad = dot(tv_ref[rows, :], grad, (0, 0))
        weight_grad = feature_grad[CELLS:ROWS]
        for j in range(PIX):
            part = slice(j * VARS, (j + 1) * VARS)
            weight_grad = weight_grad + feature_grad[part] * cells[part]
        score_grad = weight * (weight_grad - jnp.sum(weight * weight_grad, axis=0, keepdims=True))
        sums = []
        for j in range(PIX):
            part = slice(j * VARS, (j + 1) * VARS)
            cell_grad[j] = cell_grad[j] + feature_grad[part] * weight + score_grad * coef[part, h : h + 1]
            sums.append(jnp.sum(score_grad * cells[part], axis=1, keepdims=True))
        sums.append(jnp.sum(score_grad, axis=1, keepdims=True))
        sums.append(jnp.zeros((PADDED - ROWS, 1), f32))
        coef_grad = jnp.where(lane == h, jnp.concatenate(sums, axis=0), coef_grad)
    coef_grad_ref[...] = coef_grad
    cell_grads = (jnp.concatenate(cell_grad, axis=0) * seen).astype(bf16)
    pix_grad_ref[...] = dot(cell_grads, perm_ref[...], (0, 0)).astype(bf16)


def aggregate(pix, mask, perm, coef, tv, bias):
    return pl.pallas_call(
        aggregate_kernel,
        out_shape=jax.ShapeDtypeStruct((tv.shape[0], pix.shape[0]), bf16),
        compiler_params=vmem(48),
        cost_estimate=pl.CostEstimate(flops=2 << 28, bytes_accessed=4 << 20, transcendentals=0),
    )(pix, mask, perm, coef, tv, bias)


def aggregate_back(pix, mask, perm, coef, tv, grad):
    return pl.pallas_call(
        aggregate_back_kernel,
        out_shape=(
            jax.ShapeDtypeStruct((tv.shape[0], PADDED), bf16),
            jax.ShapeDtypeStruct((PADDED, 128), f32),
            jax.ShapeDtypeStruct(pix.shape, bf16),
        ),
        compiler_params=vmem(48),
        cost_estimate=pl.CostEstimate(flops=4 << 28, bytes_accessed=8 << 20, transcendentals=0),
    )(pix, mask, perm, coef, tv, grad)


def only_half(block, half):
    lane = lax.broadcasted_iota(jnp.int32, block.shape, 1)
    return jnp.where((lane >= HD) == (half == 1), block, jnp.zeros_like(block))


def attend_kernel(q_ref, k_ref, v_ref, out_ref, lse_ref):
    q, k, v = q_ref[...], k_ref[...], v_ref[...]
    outs, norms = [], []
    for half in range(2):
        logits = dot(only_half(q, half), k, (1, 1)) * 0.125
        top = jnp.max(logits, axis=1, keepdims=True)
        raised = jnp.exp(logits - top)
        total = jnp.sum(raised, axis=1, keepdims=True)
        outs.append(dot((raised / total).astype(bf16), v, (1, 0)))
        norms.append(top + jnp.log(total))
    lane = lax.broadcasted_iota(jnp.int32, outs[0].shape, 1)
    out_ref[...] = jnp.where(lane < HD, outs[0], outs[1]).astype(bf16)
    lse_ref[...] = jnp.where(lane < HD, norms[0], norms[1])


def attend(qkv):
    seq, width = qkv.shape[0], qkv.shape[1] // 3
    pairs = width // 128
    block = lambda shift: pl.BlockSpec((seq, 128), lambda i: (0, i + shift * pairs))
    return pl.pallas_call(
        attend_kernel,
        grid=(pairs,),
        in_specs=[block(0), block(1), block(2)],
        out_specs=[block(0), block(0)],
        out_shape=(
            jax.ShapeDtypeStruct((seq, width), bf16),
            jax.ShapeDtypeStruct((seq, width), f32),
        ),
        compiler_params=vmem(48),
        cost_estimate=pl.CostEstimate(flops=4 << 30, bytes_accessed=4 << 20, transcendentals=0),
    )(qkv, qkv, qkv)


def attend_back_kernel(q_ref, k_ref, v_ref, out_ref, lse_ref, grad_ref, dq_ref, dk_ref, dv_ref):
    q, k, v, grad = q_ref[...], k_ref[...], v_ref[...], grad_ref[...]
    product = grad.astype(f32) * out_ref[...].astype(f32)
    results = []
    for half in range(2):
        grad_half = only_half(grad, half)
        logits = dot(only_half(q, half), k, (1, 1)) * 0.125
        probs = jnp.exp(logits - lse_ref[:, half * HD : half * HD + 1])
        probs_grad = dot(grad_half, v, (1, 1))
        shift = jnp.sum(only_half(product, half), axis=1, keepdims=True)
        logits_grad = (probs * (probs_grad - shift) * 0.125).astype(bf16)
        results.append(
            (
                dot(logits_grad, k, (1, 0)),
                dot(logits_grad, q, (0, 0)),
                dot(probs.astype(bf16), grad, (0, 0)),
            )
        )
    lane = lax.broadcasted_iota(jnp.int32, q.shape, 1)
    for ref, low, high in zip((dq_ref, dk_ref, dv_ref), *results):
        ref[...] = jnp.where(lane < HD, low, high).astype(bf16)


def attend_back(qkv, out, lse, grad):
    seq, width = out.shape
    pairs = width // 128
    block = lambda shift: pl.BlockSpec((seq, 128), lambda i: (0, i + shift * pairs))
    return pl.pallas_call(
        attend_back_kernel,
        grid=(pairs,),
        in_specs=[block(0), block(1), block(2), block(0), block(0), block(0)],
        out_specs=[block(0)] * 3,
        out_shape=[jax.ShapeDtypeStruct((seq, width), bf16)] * 3,
        compiler_params=vmem(48),
        cost_estimate=pl.CostEstimate(flops=10 << 30, bytes_accessed=8 << 20, transcendentals=0),
    )(qkv, qkv, qkv, out, lse, grad)


def norm_parts(value):
    average = jnp.mean(value, axis=-1, keepdims=True)
    centered = value - average
    scale = lax.rsqrt(jnp.mean(centered * centered, axis=-1, keepdims=True) + epsilon)
    return centered * scale, scale


def norm_back(normal, scale, gain, grad):
    inner = grad * gain
    return scale * (
        inner
        - jnp.mean(inner, axis=-1, keepdims=True)
        - normal * jnp.mean(inner * normal, axis=-1, keepdims=True)
    )


def gelu_both(x):
    k = 0.7978845608028654
    t = jnp.tanh(k * (x + 0.044715 * (x * x * x)))
    value = 0.5 * x * (1.0 + t)
    slope = 0.5 * (1.0 + t) + 0.5 * x * (1.0 - t * t) * (k * (1.0 + 3 * 0.044715 * (x * x)))
    return value.astype(bf16), slope.astype(bf16)


def bit_orders(groups):
    bits = groups.bit_length() - 1
    first = list(range(bits))
    return first, first[1:] + first[:1]


def block_map(groups):
    table = []
    for order in bit_orders(groups):
        bits = len(order)
        table.append(
            [sum(1 << order[n] for n in range(bits) if j >> (bits - 1 - n) & 1) for j in range(groups)]
        )
    return table


def stage_pairs(groups, stage):
    orders = bit_orders(groups)
    return [
        (g * 4 + s, (g ^ (1 << orders[s % 2][stage])) * 4 + s) for g in range(groups) for s in range(4)
    ]


def swap_core(value):
    return lax.ppermute(value, "section", [(s, s ^ 1) for s in range(4)])


def swap_y(value):
    return lax.ppermute(value, "section", [(s, s ^ 2) for s in range(4)])


def added(kept, arrived):
    return (kept.astype(f32) + arrived.astype(f32)).astype(bf16)


def in_order(index, low_value, high_value, axis):
    first = jnp.where(index == 0, low_value, high_value)
    second = jnp.where(index == 0, high_value, low_value)
    return jnp.concatenate([first, second], axis=axis)


def local(
    pixels, cell_mask, lead_time, query, w_query, w_key, w_value, b_value, w_out, b_out, w_embed,
    var_embed, pos_embed, w_lead, b_lead, gain_one, shift_one, w_qkv, w_proj, b_proj, gain_two,
    shift_two, w_up, b_up, w_down, b_down, cotangent,
):
    groups = lax.axis_size("dp")
    me = lax.axis_index("dp")
    section = lax.axis_index("section")
    core, far = section % 2, section // 2
    seq = pixels.shape[0] // lead_time.shape[0]
    half_d, half_units = D // 2, w_up.shape[1] // 2
    quarter = half_units // 2
    half_heads = HEADS // 2
    piece = D // groups
    table_of = jnp.array(block_map(groups), jnp.int32)[core]
    blocks_of = [me ^ table_of[j] for j in range(groups)]

    def cut(value, start, length, axis):
        return lax.dynamic_slice_in_dim(value, start, length, axis)

    def own_order(value, width):
        return jnp.concatenate([cut(value, b * width, width, 1) for b in blocks_of], axis=1)

    def pieces_scattered(kept, arrived_of, first_stage=1):
        total = added(kept, arrived_of)
        stage = first_stage
        while total.shape[0] > 1:
            half = total.shape[0] // 2
            arrived = lax.ppermute(total[half:], axes, stage_pairs(groups, stage))
            total = added(total[:half], arrived)
            stage += 1
        return total[0]

    def scatter_product(left, right):
        half = left.shape[1] // 2
        sent = dot(left[:, half:], right, (0, 0), bf16)
        arrived = lax.ppermute(sent, axes, stage_pairs(groups, 0))
        kept = dot(left[:, :half], right, (0, 0), bf16)
        shape = (groups // 2, piece, right.shape[1])
        return pieces_scattered(kept.reshape(shape), arrived.reshape(shape))

    pix = cut(pixels, far * seq, seq, 0)
    mask = cut(cell_mask, far * seq, seq, 0)
    cot = cut(cotangent, far * seq, seq, 0)
    other_cot = jnp.concatenate(
        [
            cut(cotangent, (1 - far) * seq + core * (seq // 2), seq // 2, 0),
            cut(cotangent, (1 - far) * seq + (1 - core) * (seq // 2), seq // 2, 0),
        ]
    )
    lead = lead_time[far]
    value_half = cut(w_value, core * half_d, half_d, 1)
    out_half = cut(w_out, core * half_d, half_d, 0)
    qkv_half = cut(w_qkv.reshape(D, 3, D), core * half_d, half_d, 2).reshape(D, 3 * half_d)
    proj_half = cut(w_proj, core * half_d, half_d, 0)
    up_half = cut(w_up, core * half_units, half_units, 1)
    down_half = cut(w_down, core * half_units, half_units, 0)
    up_bias = cut(b_up, core * half_units, half_units, 0)
    up_quarter = cut(w_up, core * half_units + far * quarter, quarter, 1)
    down_quarter = cut(w_down, core * half_units + far * quarter, quarter, 0)
    up_bias_quarter = cut(b_up, core * half_units + far * quarter, quarter, 0)

    by_cell = jnp.transpose(w_embed.reshape(VARS, PIX, D), (1, 0, 2)).reshape(CELLS, D)
    table = jnp.concatenate([by_cell, var_embed], axis=0)
    asked = dot(query[None, :], w_query, (1, 0))[0]
    probe = jnp.sum(
        w_key.astype(f32).reshape(D, HEADS, HD) * asked.reshape(1, HEADS, HD), axis=2
    )
    coef_all = jnp.dot(table.astype(f32), probe, precision=highest) * 0.125
    coef = cut(jnp.pad(coef_all, ((0, PADDED - ROWS), (0, 0))), core * half_heads, half_heads, 1)
    table_padded = jnp.pad(table, ((0, PADDED - ROWS), (0, 0)))
    tv = dot(value_half, table_padded, (0, 1), bf16)
    cell_at = jnp.arange(CELLS)
    perm = (((cell_at % VARS) * PIX + cell_at // VARS)[:, None] == cell_at[None, :]).astype(bf16)

    value_bias = cut(b_value, core * half_d, half_d, 0)[:, None]
    per_head = aggregate(pix, mask, perm, coef, tv, value_bias)
    start_part = dot(per_head, out_half, (0, 0), bf16)
    start = added(start_part, swap_core(start_part)).astype(f32) + b_out + pos_embed
    start = start.astype(bf16).astype(f32)
    stream = start + lead * w_lead + b_lead
    normal_one, scale_one = norm_parts(stream)
    normed_one = (normal_one * gain_one + shift_one).astype(bf16)
    qkv = dot(normed_one, qkv_half, (1, 0), bf16)
    attended, lse = attend(qkv)
    proj_part = dot(attended, proj_half, (1, 0), bf16)
    mid = stream + b_proj + added(proj_part, swap_core(proj_part)).astype(f32)
    mid = mid.astype(bf16).astype(f32)
    normal_two, scale_two = norm_parts(mid)
    normed_two = (normal_two * gain_two + shift_two).astype(bf16)
    other_half = swap_y(cut(normed_two, core * (seq // 2), seq // 2, 0))
    other_normed = jnp.concatenate([other_half, swap_core(other_half)])

    hidden, slope = gelu_both(dot(normed_two, up_half, (1, 0)) + up_bias)
    hidden_grad = dot(cot, down_half, (1, 1))
    pre_grad = (hidden_grad * slope.astype(f32)).astype(bf16)
    normed_part = dot(pre_grad, up_half, (1, 1), bf16)
    normed_two_grad = added(normed_part, swap_core(normed_part)).astype(f32)

    out_part = dot(hidden, down_half, (1, 0), bf16)
    out_sent = cut(out_part, (1 - core) * (seq // 2), seq // 2, 0)
    out_kept = cut(out_part, core * (seq // 2), seq // 2, 0)
    block_out = cut(mid, core * (seq // 2), seq // 2, 0) + b_down
    block_out = (block_out + out_kept.astype(f32) + swap_core(out_sent).astype(f32)).astype(bf16)

    other_hidden, other_slope = gelu_both(dot(other_normed, up_quarter, (1, 0)) + up_bias_quarter)
    other_hidden_grad = dot(other_cot, down_quarter, (1, 1))
    other_pre_grad = (other_hidden_grad * other_slope.astype(f32)).astype(bf16)
    both_normed = own_order(jnp.concatenate([normed_two, other_normed]), piece)
    both_cot = own_order(jnp.concatenate([cot, other_cot]), piece)
    both_pre_grad = jnp.concatenate([cut(pre_grad, far * quarter, quarter, 1), other_pre_grad])
    both_hidden = jnp.concatenate([cut(hidden, far * quarter, quarter, 1), other_hidden])
    up_piece = scatter_product(both_normed, both_pre_grad)
    down_piece = scatter_product(both_cot, both_hidden)

    gain_two_grad = jnp.sum(normed_two_grad * normal_two, axis=0)
    shift_two_grad = jnp.sum(normed_two_grad, axis=0)
    mid_grad = cot.astype(f32) + norm_back(normal_two, scale_two, gain_two, normed_two_grad)
    mid_low = mid_grad.astype(bf16)
    b_proj_grad = jnp.sum(mid_grad, axis=0)
    attended_grad = dot(mid_low, proj_half, (1, 1), bf16)
    dq, dk, dv = attend_back(qkv, attended, lse, attended_grad)
    qkv_grad = jnp.concatenate([dq, dk, dv], axis=1)
    norm_one_part = dot(qkv_grad, qkv_half, (1, 1), bf16)
    normed_one_grad = added(norm_one_part, swap_core(norm_one_part)).astype(f32)
    gain_one_grad = jnp.sum(normed_one_grad * normal_one, axis=0)
    shift_one_grad = jnp.sum(normed_one_grad, axis=0)
    stream_grad = mid_low.astype(f32) + norm_back(normal_one, scale_one, gain_one, normed_one_grad)
    b_lead_grad = jnp.sum(stream_grad, axis=0)
    start_grad = stream_grad.astype(bf16)
    b_out_grad = jnp.sum(start_grad.astype(f32), axis=0)
    per_head_grad = dot(out_half, start_grad, (1, 1), bf16)
    g_part, coef_part, pix_part = aggregate_back(pix, mask, perm, coef, tv, per_head_grad)
    b_value_grad = jnp.sum(per_head_grad.astype(f32), axis=1)

    pix_sent = cut(pix_part, (1 - core) * (seq // 2), seq // 2, 0)
    pix_kept = cut(pix_part, core * (seq // 2), seq // 2, 0)
    pixels_grad = pix_kept.astype(f32) + swap_core(pix_sent).astype(f32)

    def halves_first(value):
        width = value.shape[1] // 2
        return cut(value, far * width, width, 1), cut(value, (1 - far) * width, width, 1)

    def whole_heads(value):
        return in_order(core, value, swap_core(value), 1)

    def scatter_with_y(left, right):
        half = left.shape[1] // 2
        keep, send = halves_first(right)
        arrived = swap_y(dot(left, send, (0, 0), bf16))
        total = added(dot(left, keep, (0, 0), bf16), arrived)
        shape = (groups // 2, piece, keep.shape[1])
        came = lax.ppermute(total[half:], axes, stage_pairs(groups, 0))
        return pieces_scattered(total[:half].reshape(shape), came.reshape(shape))

    all_attended = own_order(whole_heads(attended), piece)
    all_per_head = own_order(whole_heads(jnp.transpose(per_head)), piece)
    own_normed_one = own_order(normed_one, piece)
    qkv_piece = scatter_with_y(own_normed_one, qkv_grad)
    proj_piece = scatter_with_y(all_attended, cut(mid_low, core * half_d, half_d, 1))
    start_half = cut(start_grad, core * half_d, half_d, 1)
    out_piece = scatter_with_y(all_per_head, start_half)
    pos_width = half_d // 2
    pos_piece = seq // groups
    pos_keep, pos_send = halves_first(start_half)
    pos_total = added(pos_keep, swap_y(pos_send))
    pos_total = jnp.concatenate([cut(pos_total, b * pos_piece, pos_piece, 0) for b in blocks_of])
    pos_total = pos_total.reshape(groups, pos_piece, pos_width)
    pos_came = lax.ppermute(pos_total[groups // 2 :], axes, stage_pairs(groups, 0))
    pos_part = pieces_scattered(pos_total[: groups // 2], pos_came)

    rows = jnp.concatenate(
        [
            g_part.reshape(-1),
            jnp.transpose(coef_part[:, :half_heads]).reshape(-1).astype(bf16),
        ]
        + [
            v.astype(bf16)
            for v in (
                gain_one_grad, shift_one_grad, lead * b_lead_grad, b_lead_grad, b_out_grad, b_proj_grad,
                gain_two_grad, shift_two_grad, jnp.sum(cot.astype(f32), axis=0),
                b_value_grad, jnp.sum(pre_grad.astype(f32), axis=0),
            )
        ]
    ).reshape(-1, 512)
    rows = added(rows, swap_y(rows))
    for stage in range(groups.bit_length() - 1):
        rows = added(rows, lax.ppermute(rows, axes, stage_pairs(groups, stage)))
    other_rows = swap_core(rows)
    flat, other_flat = rows.reshape(-1), other_rows.reshape(-1)
    g_size, coef_size = half_d * PADDED, half_heads * PADDED

    def both_cores(offset, size):
        return in_order(core, flat[offset : offset + size], other_flat[offset : offset + size], 0)

    g_all = both_cores(0, g_size).reshape(D, PADDED)
    coef_grad = both_cores(g_size, coef_size).reshape(HEADS, PADDED).astype(f32) * 0.125
    offset = g_size + coef_size
    vectors = []
    shared = jnp.where(core == 0, flat, other_flat)[offset : offset + 9 * D].reshape(9, D)
    shared = cut(shared.astype(f32), me * piece, piece, 1)
    vectors = [shared[n] for n in range(9)]
    offset += 9 * D
    value_bias_grad = both_cores(offset, half_d).astype(f32)
    offset += half_d
    up_bias_grad = both_cores(offset, half_units).astype(f32)

    my_table = cut(table_padded, me * piece, piece, 1)
    w_value_grad = dot(my_table, g_all, (0, 1))
    my_value = cut(w_value, me * piece, piece, 0)
    my_probe = cut(probe, me * piece, piece, 0)
    table_grad = dot(g_all, my_value, (0, 1)) + dot(coef_grad, my_probe, (0, 1), f32, highest)
    embed_grad = jnp.transpose(table_grad[:CELLS].reshape(PIX, VARS, piece), (1, 0, 2)).reshape(CELLS, piece)
    var_grad = table_grad[CELLS:ROWS]
    probe_grad = dot(table_padded.astype(f32), coef_grad, (0, 1), f32, highest)
    my_probe_grad = cut(probe_grad, me * piece, piece, 0)
    w_key_grad = (my_probe_grad[:, :, None] * asked.reshape(1, HEADS, HD)).reshape(piece, D)
    asked_grad = jnp.sum(
        w_key.astype(f32).reshape(D, HEADS, HD) * probe_grad[:, :, None], axis=0
    ).reshape(D)
    my_query = cut(query, me * piece, piece, 0).astype(f32)
    w_query_grad = my_query[:, None] * asked_grad[None, :]
    query_grad = jnp.sum(cut(w_query, me * piece, piece, 0).astype(f32) * asked_grad[None, :], axis=1)

    def from_y(value):
        return in_order(far, value, swap_y(value), value.ndim - 1)

    def from_core(value, axis=1):
        return in_order(core, value, swap_core(value), axis)

    w_up_grad = from_core(from_y(up_piece)).astype(f32)
    w_down_grad = jnp.transpose(from_core(from_y(down_piece)).astype(f32))
    w_qkv_grad = from_core(from_y(qkv_piece).reshape(piece, 3, half_d), 2).reshape(piece, 3 * D).astype(f32)
    w_proj_grad = from_core(from_y(proj_piece)).astype(f32)
    w_out_grad = from_core(from_y(out_piece)).astype(f32)
    pos_grad = from_core(from_y(pos_part)).astype(f32)

    my_value_bias = cut(value_bias_grad, me * piece, piece, 0)
    up_bias_piece = up_bias_grad.shape[0] // groups
    my_up_bias = cut(up_bias_grad, me * up_bias_piece, up_bias_piece, 0)
    return (
        block_out, pixels_grad, query_grad, w_query_grad, w_key_grad, w_value_grad, my_value_bias,
        w_out_grad, vectors[4], embed_grad, var_grad, pos_grad, vectors[2], vectors[3], vectors[0],
        vectors[1], w_qkv_grad, w_proj_grad, vectors[5], vectors[6], vectors[7], w_up_grad,
        my_up_bias, w_down_grad, vectors[8],
    )


def solution(mesh):
    whole = P()
    args = (P("dp", None), P("dp", None), P("dp")) + (whole,) * 23 + (P("dp", None),)
    outs = (
        (P(axes, None),) * 2
        + (P("dp"),)
        + (P("dp", None),) * 3
        + (P("dp"), P("dp", None), P("dp"), P(None, "dp"), P(None, "dp"), P("dp", None))
        + (P("dp"),) * 4
        + (P("dp", None),) * 2
        + (P("dp"),) * 3
        + (P("dp", None), P("dp"), P(None, "dp"), P("dp"))
    )
    return jax.shard_map(local, mesh=mesh, in_specs=args, out_specs=outs, check_vma=False)
```

```python
import functools

import jax
import jax.numpy as jnp
from jax import lax
from jax.experimental import pallas as pl
from jax.experimental.pallas import tpu as pltpu
from jax.sharding import PartitionSpec as P

D = 1024
HEADS = 16
HD = 64
VARS = 48
PIX = 4
CELLS = VARS * PIX
ROWS = CELLS + VARS
PADDED = 256
OWN_HEADS = HEADS // 2
HALF = D // 2
QUARTER = D // 4
LANES = 128
SMALL_ROWS = 160

highest = lax.Precision.HIGHEST
epsilon = 1e-05
bf16 = jnp.bfloat16
f32 = jnp.float32
axes = ("dp", "section")


def dot(a, b, contract, kind=f32, precision=None):
    return lax.dot_general(
        a, b, ((contract[:1], contract[1:]), ((), ())), precision=precision, preferred_element_type=kind
    )


def call(body, scalars, ins, outs, scratch=(), us=2, mb=24, after=()):
    arrays, in_specs = [], []
    for item in list(ins) + [(x, pl.ANY) for x in after]:
        array, space = item if isinstance(item, tuple) else (item, pltpu.VMEM)
        in_specs.append(pl.BlockSpec(memory_space=space))
        arrays.append(array)
    count = len(ins)

    def unread(s, *refs):
        body(s, *refs[:count], *refs[count + len(after) :])

    return pl.pallas_call(
        unread if after else body,
        in_specs=[pl.BlockSpec(memory_space=pltpu.SMEM)] + in_specs,
        out_specs=[pl.BlockSpec(memory_space=pltpu.HBM if len(item) > 2 else pltpu.VMEM) for item in outs],
        out_shape=[
            pltpu.HBM(*item[:2]) if len(item) > 2 else jax.ShapeDtypeStruct(*item) for item in outs
        ],
        scratch_shapes=list(scratch) + [pltpu.SemaphoreType.DMA((24,))],
        compiler_params=pltpu.CompilerParams(vmem_limit_bytes=mb << 20),
        cost_estimate=pl.CostEstimate(flops=int(us * 1e7), bytes_accessed=1 << 12, transcendentals=0),
    )(scalars, *arrays)


def remote(array):
    return pltpu.with_memory_space_constraint(array, pltpu.HBM), pltpu.HBM


def scalar(array):
    return array, pltpu.SMEM


class Moves:
    def __init__(self, sems):
        self.sems, self.count = sems, 0

    def start(self, source, place):
        copy = pltpu.make_async_copy(source, place, self.sems.at[self.count])
        self.count += 1
        copy.start()
        return copy


def wait(*copies):
    for copy in copies:
        copy.wait()


def part_of(start, size):
    return pl.ds(pl.multiple_of(start * size, size), size)


def cell_order():
    row = lax.broadcasted_iota(jnp.int32, (CELLS, CELLS), 0)
    column = lax.broadcasted_iota(jnp.int32, (CELLS, CELLS), 1)
    cell = sum((row >= n * VARS).astype(jnp.int32) for n in range(1, PIX))
    return ((row - cell * VARS) * PIX + cell == column).astype(f32).astype(bf16)


def in_three(value):
    high = value.astype(bf16).astype(f32)
    middle = (value - high).astype(bf16).astype(f32)
    return jnp.concatenate([high, middle, value - high - middle], axis=0).astype(bf16)


def summed_rows(value, rows):
    return value[:rows] + value[rows : 2 * rows] + value[2 * rows :]


def head_weights(cells, pen, coef, h):
    scores = pen + coef[CELLS:ROWS, h : h + 1]
    for j in range(PIX):
        rows = slice(j * VARS, (j + 1) * VARS)
        scores = scores + cells[rows] * coef[rows, h : h + 1]
    raised = jnp.exp(scores - jnp.max(scores, axis=0, keepdims=True))
    return raised / jnp.sum(raised, axis=0, keepdims=True)


def head_features(cells, weight):
    parts = [weight * cells[j * VARS : (j + 1) * VARS] for j in range(PIX)]
    parts = parts + [weight, jnp.ones((PADDED - ROWS, weight.shape[1]), f32)]
    return jnp.concatenate(parts, axis=0).astype(bf16)


def load_cells(pix_ref, mask_ref, perm):
    mask = mask_ref[...].astype(f32).astype(bf16)
    masked = pix_ref[...] * mask
    cells = dot(perm, masked, (1, 0))
    seen = dot(perm, mask, (1, 0))
    present = seen[:VARS]
    for j in range(1, PIX):
        present = jnp.maximum(present, seen[j * VARS : (j + 1) * VARS])
    return cells, seen, (present - 1.0) * 10000.0


def start_kernel(
    s, pix_hbm, mask_hbm, query_ref, w_query_hbm, w_key_hbm, w_value_hbm, b_value_ref, w_out_hbm, embed_hbm, var_hbm,
    part_ref, per_head_hbm, coef_ref, tv_hbm, table_hbm, probe_ref,
    w_query_ref, w_key_ref, w_value_ref, w_out_ref, per_head_ref, tv_ref, table_ref, pix_ref, mask_ref, embed_ref, var_ref,
    sems,
):
    half = part_of(s[0], HALF)
    seq = part_ref.shape[0]
    moves = Moves(sems)
    sample = part_of(s[1], seq)
    tables = [moves.start(embed_hbm, embed_ref), moves.start(var_hbm, var_ref)]
    pixels = [moves.start(pix_hbm.at[:, sample], pix_ref), moves.start(mask_hbm.at[:, sample], mask_ref)]
    copies = [
        moves.start(w_query_hbm.at[:, half], w_query_ref),
        moves.start(w_key_hbm.at[:, half], w_key_ref),
        moves.start(w_value_hbm.at[:, half], w_value_ref),
        moves.start(w_out_hbm.at[half, :], w_out_ref),
    ]
    perm = cell_order()
    wait(*tables)
    table = jnp.concatenate(
        [
            dot(perm, embed_ref[...], (1, 0)),
            var_ref[...].astype(f32),
            jnp.zeros((PADDED - ROWS, D), f32),
        ]
    ).astype(bf16)
    table_ref[...] = table
    saved = [moves.start(table_ref, table_hbm)]
    wait(*pixels)
    cells, _, pen = load_cells(pix_ref, mask_ref, perm)
    wait(*copies[:3])
    asked = dot(query_ref[...], w_query_ref[...], (1, 0))
    row = lax.broadcasted_iota(jnp.int32, (OWN_HEADS, HALF), 0)
    lane = lax.broadcasted_iota(jnp.int32, (OWN_HEADS, HALF), 1)
    by_head = jnp.where((lane >= row * HD) & (lane < (row + 1) * HD), asked, 0.0)
    probe = summed_rows(dot(in_three(by_head), w_key_ref[...], (1, 1)), OWN_HEADS)
    asked_row = jnp.concatenate([jnp.broadcast_to(asked, (8, HALF)), jnp.zeros((8, HALF), f32)], axis=1)
    probe_ref[...] = jnp.concatenate([probe, asked_row], axis=0)
    coef3 = dot(table, in_three(probe), (1, 1)) * 0.125
    coef = coef3[:, :OWN_HEADS] + coef3[:, OWN_HEADS : 2 * OWN_HEADS] + coef3[:, 2 * OWN_HEADS :]
    coef_ref[...] = coef
    tv = jnp.transpose(dot(table, w_value_ref[...], (1, 0))).astype(bf16)
    lane = lax.broadcasted_iota(jnp.int32, tv.shape, 1)
    tv = jnp.where(lane < ROWS, tv, jnp.zeros_like(tv))
    tv_ref[...] = tv
    saved.append(moves.start(tv_ref, tv_hbm))
    bias = b_value_ref[:, half]
    for h in range(OWN_HEADS):
        rows = slice(h * HD, (h + 1) * HD)
        features = head_features(cells, head_weights(cells, pen, coef, h))
        column = jnp.transpose(jnp.broadcast_to(bias[:, rows], (8, HD)))[:, :1]
        per_head_ref[rows, :] = (dot(tv[rows], features, (1, 0)) + column).astype(bf16)
    saved.append(moves.start(per_head_ref, per_head_hbm))
    wait(copies[3])
    part_ref[...] = dot(per_head_ref[...], w_out_ref[...], (0, 0)).astype(bf16)
    wait(*saved)


def norm_parts(value):
    average = jnp.mean(value, axis=-1, keepdims=True)
    centered = value - average
    scale = lax.rsqrt(jnp.mean(centered * centered, axis=-1, keepdims=True) + epsilon)
    return centered * scale, scale


def norm_back(normal, scale, gain, grad):
    inner = grad * gain
    return scale * (
        inner
        - jnp.mean(inner, axis=-1, keepdims=True)
        - normal * jnp.mean(inner * normal, axis=-1, keepdims=True)
    )


def gelu_both(x):
    k = 0.7978845608028654
    square = x * x
    t = jnp.tanh(x * (k + k * 0.044715 * square))
    gate = 0.5 + 0.5 * t
    slope = gate + (0.5 * x) * (1.0 - t * t) * (k + 3 * k * 0.044715 * square)
    return x * gate, slope


def total(first_ref, second_ref):
    return first_ref[...].astype(f32) + second_ref[...].astype(f32)


def column_sums(value):
    return jnp.sum(value, axis=0, keepdims=True)


def only_half(block, half):
    lane = lax.broadcasted_iota(jnp.int32, block.shape, 1)
    return jnp.where((lane >= HD) if half else (lane < HD), block, jnp.zeros_like(block))


def joined(low, high):
    lane = lax.broadcasted_iota(jnp.int32, low.shape, 1)
    return jnp.where(lane < HD, low, high)


def pair_columns(pair, part=0):
    return pl.ds(pl.multiple_of(part * HALF + pair * LANES, LANES), LANES)


def fetch_heads(moves, s, w_qkv_hbm, w_ref):
    return [moves.start(w_qkv_hbm.at[:, part_of(2 * n + s[0], HALF)], w_ref.at[n]) for n in range(3)]


def attend_kernel(
    s, own_ref, came_ref, pos_ref, lead_ref, w_lead_ref, b_lead_ref, b_out_ref, gain_ref, shift_ref, w_qkv_hbm,
    w_proj_hbm,
    start_ref, part_ref, start_hbm, normed_hbm, qkv_hbm, lse_hbm, out_hbm,
    w_ref, w_proj_ref, normed_ref, qkv_ref, lse_ref, out_ref, sems,
):
    moves = Moves(sems)
    copies = fetch_heads(moves, s, w_qkv_hbm, w_ref)
    proj_copy = moves.start(w_proj_hbm.at[part_of(s[0], HALF), :], w_proj_ref)
    start = (total(own_ref, came_ref) + b_out_ref[...] + pos_ref[...].astype(f32)).astype(bf16)
    start_ref[...] = start
    saved = [moves.start(start_ref, start_hbm)]
    stream = start.astype(f32) + lead_ref[s[1]] * w_lead_ref[...] + b_lead_ref[...]
    normal, _ = norm_parts(stream)
    normed = (normal * gain_ref[...] + shift_ref[...]).astype(bf16)
    normed_ref[...] = normed
    saved.append(moves.start(normed_ref, normed_hbm))
    wait(*copies)
    for n in range(3):
        qkv_ref[:, n * HALF : (n + 1) * HALF] = dot(normed, w_ref[n], (1, 0)).astype(bf16)
    saved.append(moves.start(qkv_ref, qkv_hbm))

    def one_pair(pair, carried):
        q, k, v = (qkv_ref[:, pair_columns(pair, part)] for part in range(3))
        lane = lax.broadcasted_iota(jnp.int32, v.shape, 1)
        outs, weights, norms = [], [], []
        for half in range(2):
            mine = (lane >= HD) if half else (lane < HD)
            logits = dot(only_half(q * jnp.asarray(0.125, bf16), half), k, (1, 1))
            top = jnp.max(logits, axis=1, keepdims=True)
            raised = jnp.exp(logits - top).astype(bf16)
            both = dot(raised, jnp.where(mine, v, jnp.ones_like(v)), (1, 0))
            outs.append(both)
            weights.append(pltpu.roll(both, HD, 1))
            norms.append(jnp.broadcast_to(top, both.shape))
        weight = joined(*weights)
        out_ref[:, pair_columns(pair)] = (joined(*outs) / weight).astype(bf16)
        lse_ref[pair] = joined(*norms) + jnp.log(weight)
        return carried

    lax.fori_loop(0, OWN_HEADS // 2, one_pair, 0)
    saved.append(moves.start(lse_ref, lse_hbm))
    saved.append(moves.start(out_ref, out_hbm))
    wait(proj_copy)
    part_ref[...] = dot(out_ref[...], w_proj_ref[...], (1, 0)).astype(bf16)
    wait(*saved)


def middle_kernel(
    s, start_ref, lead_ref, w_lead_ref, b_lead_ref, b_proj_ref, own_ref, came_ref, gain_ref, shift_ref,
    normed_ref, half_ref, mid_hbm, normed_hbm, mid_ref, sems,
):
    moves = Moves(sems)
    stream = start_ref[...].astype(f32) + lead_ref[s[1]] * w_lead_ref[...] + b_lead_ref[...]
    mid = (stream + b_proj_ref[...] + total(own_ref, came_ref)).astype(bf16)
    mid_ref[...] = mid
    saved = [moves.start(mid_ref, mid_hbm)]
    normal, _ = norm_parts(mid.astype(f32))
    normed_ref[...] = (normal * gain_ref[...] + shift_ref[...]).astype(bf16)
    saved.append(moves.start(normed_ref, normed_hbm))
    half_ref[...] = normed_ref[part_of(s[0], half_ref.shape[0]), :]
    wait(*saved)


def mlp_kernel(
    s, normed_ref, cot_hbm, w_up_hbm, b_up_ref, w_down_hbm, sums_ref, part_ref, hidden_hbm, pre_grad_hbm,
    hidden_ref, pre_grad_ref, w_up_ref, w_down_ref, cot_ref, sems,
):
    width = w_up_ref.shape[2]
    moves = Moves(sems)
    ups, downs, saved = [], [], []
    for n in range(2):
        place = part_of(2 * s[0] + n, width)
        ups.append(moves.start(w_up_hbm.at[:, place], w_up_ref.at[n]))
        if n == 0:
            cot_copy = moves.start(cot_hbm.at[part_of(s[1], cot_ref.shape[0]), :], cot_ref)
        downs.append(moves.start(w_down_hbm.at[place, :], w_down_ref.at[n]))
    wait(cot_copy)
    back = None
    for n in range(2):
        columns = slice(n * width, (n + 1) * width)
        wait(ups[n], downs[n])
        pre = dot(normed_ref[...], w_up_ref[n], (1, 0)) + b_up_ref[:, part_of(2 * s[0] + n, width)]
        hidden_grad = dot(cot_ref[...], w_down_ref[n], (1, 1))
        hidden, slope = gelu_both(pre)
        hidden_ref[n] = hidden.astype(bf16)
        pre_grad = hidden_grad * slope
        sums_ref[:, columns] = column_sums(pre_grad)
        low = pre_grad.astype(bf16)
        pre_grad_ref[n] = low
        term = dot(low, w_up_ref[n], (1, 1))
        back = term if back is None else back + term
        saved.append(moves.start(hidden_ref.at[n], hidden_hbm.at[n]))
        saved.append(moves.start(pre_grad_ref.at[n], pre_grad_hbm.at[n]))
    part_ref[...] = back.astype(bf16)
    wait(*saved)


def out_kernel(
    s, hidden_hbm, w_down_hbm, mid_hbm, b_down_ref, sent_ref, kept_ref, total_ref, hidden_ref, w_down_ref, mid_ref, sems
):
    width = w_down_ref.shape[1]
    rows = sent_ref.shape[0]
    moves = Moves(sems)
    copies = []
    for n in range(2):
        copies.append(moves.start(hidden_hbm.at[n], hidden_ref.at[n]))
        copies.append(moves.start(w_down_hbm.at[part_of(2 * s[0] + n, width), :], w_down_ref.at[n]))
    mid_copy = moves.start(mid_hbm.at[part_of(s[0], rows), :], mid_ref)
    wait(*copies[:2])
    result = dot(hidden_ref[0], w_down_ref[0], (1, 0))
    wait(*copies[2:])
    total_ref[...] = result + dot(hidden_ref[1], w_down_ref[1], (1, 0))
    wait(mid_copy)
    sent_ref[...] = total_ref[part_of(1 - s[0], rows), :].astype(bf16)
    kept_ref[...] = total_ref[part_of(s[0], rows), :] + mid_ref[...].astype(f32) + b_down_ref[...]


def attend_back_kernel(
    s, own_ref, came_ref, mid_hbm, cot_hbm, gain_ref, qkv_hbm, out_hbm, lse_hbm, w_proj_hbm, w_qkv_hbm,
    part_one_ref, part_two_ref, sums_ref, keep_hbm, send_hbm, mid_grad_hbm,
    mid_ref, cot_ref, qkv_ref, out_ref, lse_ref, w_ref, w_proj_ref, grad_ref, back_ref, keep_ref, send_ref, mid_grad_ref,
    sems,
):
    seq = own_ref.shape[0]
    moves = Moves(sems)
    first = [moves.start(mid_hbm, mid_ref), moves.start(cot_hbm.at[part_of(s[1], seq), :], cot_ref)]
    proj_copy = moves.start(w_proj_hbm.at[part_of(s[0], HALF), :], w_proj_ref)
    copies = [
        moves.start(qkv_hbm, qkv_ref), moves.start(out_hbm, out_ref), moves.start(lse_hbm, lse_ref)
    ]
    heads = fetch_heads(moves, s, w_qkv_hbm, w_ref)
    grad = total(own_ref, came_ref)
    wait(*first)
    cot = cot_ref[...].astype(f32)
    normal, scale = norm_parts(mid_ref[...].astype(f32))
    mid_grad = cot + norm_back(normal, scale, gain_ref[...], grad)
    sums_ref[...] = jnp.concatenate(
        [column_sums(grad * normal), column_sums(grad), column_sums(mid_grad), column_sums(cot), jnp.zeros((4, D), f32)]
    )
    low = mid_grad.astype(bf16)
    mid_grad_ref[...] = low
    saved = [moves.start(mid_grad_ref, mid_grad_hbm)]
    wait(proj_copy, *copies)
    grad_ref[...] = dot(low, w_proj_ref[...], (1, 1)).astype(bf16)

    def one_pair(pair, carried):
        q, k, v = (qkv_ref[:, pair_columns(pair, part)] for part in range(3))
        out_grad = grad_ref[:, pair_columns(pair)]
        weighted = out_grad.astype(f32) * out_ref[:, pair_columns(pair)].astype(f32)
        norms = lse_ref[pair]
        results = []
        for half in range(2):
            logits = dot(only_half(q * jnp.asarray(0.125, bf16), half), k, (1, 1))
            probs = jnp.exp(logits - norms[:, half * HD : half * HD + 1])
            probs_grad = dot(only_half(out_grad, half), v, (1, 1))
            shift = jnp.sum(only_half(weighted, half), axis=1, keepdims=True)
            logits_grad = (probs * (probs_grad - shift)).astype(bf16)
            results.append(
                (
                    dot(logits_grad, k, (1, 0)) * 0.125,
                    dot(logits_grad, q, (0, 0)) * 0.125,
                    dot(probs.astype(bf16), out_grad, (0, 0)),
                )
            )
        for part, (low_head, high_head) in enumerate(zip(*results)):
            back_ref[:, pair_columns(pair, part)] = joined(low_head, high_head).astype(bf16)
        return carried

    lax.fori_loop(0, OWN_HEADS // 2, one_pair, 0)
    for part in range(3):
        columns = slice(part * QUARTER, (part + 1) * QUARTER)
        mine = pl.multiple_of(part * HALF + s[1] * QUARTER, LANES)
        theirs = pl.multiple_of(part * HALF + (1 - s[1]) * QUARTER, LANES)
        keep_ref[:, columns] = back_ref[:, pl.ds(mine, QUARTER)]
        send_ref[:, columns] = back_ref[:, pl.ds(theirs, QUARTER)]
    saved += [moves.start(keep_ref, keep_hbm), moves.start(send_ref, send_hbm)]
    wait(*heads)
    back = None
    for n in range(3):
        term = dot(back_ref[:, n * HALF : (n + 1) * HALF], w_ref[n], (1, 1))
        back = term if back is None else back + term
    part_one_ref[...] = back[: seq // 2].astype(bf16)
    part_two_ref[...] = back[seq // 2 :].astype(bf16)
    wait(*saved)


def start_back_kernel(
    s, own_one_ref, own_two_ref, came_one_ref, came_two_ref, start_hbm, lead_ref, w_lead_ref, b_lead_ref, gain_ref, mid_grad_hbm, w_out_hbm, pix_hbm,
    mask_hbm, coef_ref, tv_hbm, sums_ref, up_sums_ref,
    pix_keep_ref, pix_send_ref, side_hbm, small_ref,
    held_ref, w_out_ref, start_ref, mid_grad_ref, tv_ref, start_grad_ref, side_ref, pix_ref, mask_ref, sems,
):
    moves = Moves(sems)
    first = [moves.start(start_hbm, start_ref), moves.start(mid_grad_hbm, mid_grad_ref)]
    seq = 2 * own_one_ref.shape[0]
    sample = part_of(s[1], seq)
    copies = [
        moves.start(w_out_hbm.at[part_of(s[0], HALF), :], w_out_ref), moves.start(tv_hbm, tv_ref),
        moves.start(pix_hbm.at[:, sample], pix_ref), moves.start(mask_hbm.at[:, sample], mask_ref),
    ]
    grad = jnp.concatenate([total(own_one_ref, came_one_ref), total(own_two_ref, came_two_ref)], axis=0)
    lead = lead_ref[s[1]]
    wait(*first)
    stream = start_ref[...].astype(f32) + lead * w_lead_ref[...] + b_lead_ref[...]
    normal, scale = norm_parts(stream)
    stream_grad = mid_grad_ref[...].astype(f32) + norm_back(normal, scale, gain_ref[...], grad)
    start_grad = stream_grad.astype(bf16)
    start_grad_ref[...] = start_grad
    for side in range(2):
        side_ref[:, side * QUARTER : (side + 1) * QUARTER] = start_grad_ref[:, quarter_columns(s, side)]
    saved = [moves.start(side_ref, side_hbm)]
    lead_sum = column_sums(stream_grad)
    vectors = [
        sums_ref[0:4, :],
        column_sums(grad * normal),
        column_sums(grad),
        lead_sum,
        lead * lead_sum,
        column_sums(start_grad.astype(f32)),
        up_sums_ref[:, :D],
        up_sums_ref[:, D:],
        jnp.zeros((SMALL_ROWS - 136 - 11, D), f32),
    ]
    wait(*copies)
    per_head_grad = dot(w_out_ref[...], start_grad, (1, 1)).astype(bf16)

    cells, seen, pen = load_cells(pix_ref, mask_ref, cell_order())
    coef = coef_ref[...]
    tv = tv_ref[...]
    lane = lax.broadcasted_iota(jnp.int32, (PADDED, LANES), 1)
    coef_grad = jnp.zeros((PADDED, LANES), f32)
    cell_grad = [jnp.zeros((VARS, cells.shape[1]), f32) for _ in range(PIX)]
    for h in range(OWN_HEADS):
        rows = slice(h * HD, (h + 1) * HD)
        weight = head_weights(cells, pen, coef, h)
        features = head_features(cells, weight)
        head_grad = per_head_grad[rows]
        small_rows = slice((h % 2) * HD, (h % 2 + 1) * HD)
        small_ref[small_rows, (h // 2) * PADDED : (h // 2 + 1) * PADDED] = dot(head_grad, features, (1, 1)).astype(bf16)
        feature_grad = dot(tv[rows], head_grad, (0, 0))
        weight_grad = feature_grad[CELLS:ROWS]
        for j in range(PIX):
            part = slice(j * VARS, (j + 1) * VARS)
            weight_grad = weight_grad + feature_grad[part] * cells[part]
        score_grad = weight * (weight_grad - jnp.sum(weight * weight_grad, axis=0, keepdims=True))
        sums = []
        for j in range(PIX):
            part = slice(j * VARS, (j + 1) * VARS)
            cell_grad[j] = cell_grad[j] + feature_grad[part] * weight + score_grad * coef[part, h : h + 1]
            sums.append(jnp.sum(score_grad * cells[part], axis=1, keepdims=True))
        sums.append(jnp.sum(score_grad, axis=1, keepdims=True))
        sums.append(jnp.zeros((PADDED - ROWS, 1), f32))
        coef_grad = jnp.where(lane == h, jnp.concatenate(sums, axis=0), coef_grad)
    coef_rows = jnp.transpose(coef_grad)[:OWN_HEADS]
    coef_rows = jnp.concatenate([coef_rows, jnp.zeros((OWN_HEADS, D - PADDED), f32)], axis=1)
    small_ref[LANES:, :] = jnp.concatenate([coef_rows] + vectors, axis=0).astype(bf16)
    cell_grads = (jnp.concatenate(cell_grad, axis=0) * seen).astype(bf16)
    held_ref[...] = dot(cell_order(), cell_grads, (0, 0))
    columns = pix_keep_ref.shape[1]
    pix_keep_ref[...] = held_ref[:, part_of(s[0], columns)]
    pix_send_ref[...] = held_ref[:, part_of(1 - s[0], columns)].astype(bf16)
    wait(*saved)


def quarter_columns(s, side):
    far = s[1] if side == 0 else 1 - s[1]
    return pl.ds(pl.multiple_of(s[0] * HALF + far * QUARTER, QUARTER), QUARTER)


def mlp_grads_kernel(
    s, normed_hbm, first_hbm, second_hbm, cot_hbm, w_up_hbm, b_up_ref, w_down_hbm, pre_grad_hbm, hidden_hbm,
    up_send_hbm, up_keep_hbm, down_send_hbm, down_keep_hbm,
    normed_ref, cot_ref, w_up_ref, w_down_ref, pre_grad_ref, hidden_ref, sum_ref, sems, *, piece, groups,
):
    width = w_up_ref.shape[1]
    rows = first_hbm.shape[0]
    seq = 2 * rows
    place = part_of(2 * s[0] + s[1], width)
    moves = Moves(sems)
    own, one, two = pl.ds(0, seq), pl.ds(seq, rows), pl.ds(seq + rows, rows)
    first = [
        moves.start(w_up_hbm.at[:, place], w_up_ref),
        moves.start(first_hbm, normed_ref.at[one, :]),
        moves.start(second_hbm, normed_ref.at[two, :]),
        moves.start(cot_hbm.at[part_of((1 - s[1]) * 2 + s[0], rows), :], cot_ref.at[one, :]),
        moves.start(cot_hbm.at[part_of((1 - s[1]) * 2 + (1 - s[0]), rows), :], cot_ref.at[two, :]),
        moves.start(w_down_hbm.at[place, :], w_down_ref),
    ]
    then = [
        moves.start(cot_hbm.at[part_of(s[1], seq), :], cot_ref.at[own, :]),
        moves.start(normed_hbm, normed_ref.at[own, :]),
        moves.start(hidden_hbm.at[s[1]], hidden_ref.at[own, :]),
        moves.start(pre_grad_hbm.at[s[1]], pre_grad_ref.at[own, :]),
    ]
    wait(*first)
    pre = dot(normed_ref[seq:, :], w_up_ref[...], (1, 0)) + b_up_ref[:, place]
    hidden_grad = dot(cot_ref[seq:, :], w_down_ref[...], (1, 1))
    hidden, slope = gelu_both(pre)
    hidden_ref[seq:, :] = hidden.astype(bf16)
    pre_grad_ref[seq:, :] = (hidden_grad * slope).astype(bf16)
    wait(*then)
    half = groups // 2 * piece
    outs = ((up_send_hbm, up_keep_hbm), (down_send_hbm, down_keep_hbm))
    saved = []
    for n, (left_ref, right_ref) in enumerate(((normed_ref, pre_grad_ref), (cot_ref, hidden_ref))):
        left = chosen(left_ref, [s[3 + n * groups + b] for b in range(groups)], piece)
        sum_ref[n] = dot(left, right_ref[...], (0, 0)).astype(bf16)
        send_hbm, keep_hbm = outs[n]
        saved.append(moves.start(sum_ref.at[n, half:, :], send_hbm))
        saved.append(moves.start(sum_ref.at[n, :half, :], keep_hbm))
    wait(*saved)


def chosen(ref, blocks, piece):
    return jnp.concatenate([ref[:, part_of(b, piece)] for b in blocks], axis=1)


def head_grads_kernel(
    s, normed_hbm, keep_hbm, send_hbm, attended_hbm, attended_far_hbm, mid_grad_hbm, one_send, one_keep, two_send, two_keep,
    normed_ref, right_ref, attended_ref, mid_ref, sems, *, piece, groups,
):
    moves = Moves(sems)
    copies = [
        moves.start(normed_hbm, normed_ref), moves.start(send_hbm, right_ref.at[1]), moves.start(keep_hbm, right_ref.at[0])
    ]
    then = [
        moves.start(attended_hbm, attended_ref.at[s[0]]),
        moves.start(attended_far_hbm, attended_ref.at[1 - s[0]]),
        moves.start(mid_grad_hbm.at[:, quarter_columns(s, 0)], mid_ref.at[:, :QUARTER]),
        moves.start(mid_grad_hbm.at[:, quarter_columns(s, 1)], mid_ref.at[:, QUARTER:]),
    ]
    blocks = [s[3 + n] for n in range(groups)]
    wait(*copies)
    left = chosen(normed_ref, blocks, piece)
    both_qk = 2 * QUARTER
    one_send[...] = dot(left, right_ref[1, :, :both_qk], (0, 0)).astype(bf16)
    one_keep[...] = dot(left, right_ref[0, :, :both_qk], (0, 0)).astype(bf16)
    wait(*then)
    features = jnp.concatenate([attended_ref[b >> 2, :, part_of(b & 3, piece)] for b in blocks], axis=1)
    half = two_keep.shape[0]
    for side in range(2):
        quarter = slice(side * QUARTER, (side + 1) * QUARTER)
        value = dot(left, right_ref[side, :, both_qk:], (0, 0)).astype(bf16)
        proj = dot(features, mid_ref[:, quarter], (0, 0)).astype(bf16)
        for ref, part in ((two_keep, slice(0, half)), (two_send, slice(half, 2 * half))):
            ref[:, side * both_qk : side * both_qk + QUARTER] = value[part]
            ref[:, side * both_qk + QUARTER : (side + 1) * both_qk] = proj[part]


def side_grads_kernel(
    s, head_hbm, head_far_hbm, start_hbm, small_ref, sent_ref, kept_ref, head_ref, start_ref, pos_ref, sems, *, piece, groups
):
    moves = Moves(sems)
    seq = start_ref.shape[0]
    wait(
        moves.start(head_hbm, head_ref.at[s[0]]),
        moves.start(head_far_hbm, head_ref.at[1 - s[0]]),
        moves.start(start_hbm, start_ref),
    )
    pos_ref[...] = start_ref[...].astype(f32)
    width = QUARTER + LANES
    blocks = [s[3 + n] for n in range(groups)]
    per_head = jnp.concatenate([head_ref[b >> 2, part_of(b & 3, piece), :] for b in blocks], axis=0)
    out = dot(per_head, start_ref[...], (1, 0)).astype(bf16)
    for side in range(2):
        quarter = slice(side * QUARTER, (side + 1) * QUARTER)
        pos = []
        for b in blocks:
            block = pos_ref[part_of(b, seq // groups), quarter]
            pos += [block[:, :LANES], block[:, LANES:]]
        columns = jnp.concatenate([out[:, quarter], jnp.concatenate(pos, axis=0).astype(bf16)], axis=1)
        if side == 0:
            kept_ref[...] = columns
        else:
            sent_ref[:width, :] = by_squares(columns)
    sent_ref[width:, :] = small_ref[...]


def by_squares(value):
    rows, columns = value.shape
    return jnp.concatenate(
        [
            jnp.concatenate(
                [value[r : r + LANES, c : c + LANES] for r in range(0, rows, LANES)], axis=1
            )
            for c in range(0, columns, LANES)
        ],
        axis=0,
    )


def both(one, two):
    return (one.astype(f32) + two.astype(f32)).astype(bf16)


def halves_kernel(s, *refs):
    count = len(refs) // 4
    for n in range(count):
        kept, came = refs[2 * n : 2 * n + 2]
        keep, send = refs[2 * count + 2 * n : 2 * count + 2 * n + 2]
        half = keep.shape[0]
        send[...] = both(kept[half:], came[half:])
        keep[...] = both(kept[:half], came[:half])


def heads_kernel(s, one_ref, one_came_ref, two_ref, two_came_ref, one_keep, one_send, two_keep, two_send, sems):
    half = one_keep.shape[0]
    one_send[...] = both(one_ref[half:], one_came_ref[half:])
    one_keep[...] = both(one_ref[:half], one_came_ref[:half])
    width = two_keep.shape[2]
    two_send[...] = both(two_ref[:, :, width:], two_came_ref[:, :, width:])
    two_keep[...] = both(two_ref[:, :, :width], two_came_ref[:, :, :width])


def sides_kernel(s, kept_ref, small_ref, came_ref, keep_ref, send_ref, sum_ref, sems):
    width = kept_ref.shape[1]
    half = keep_ref.shape[0]
    whole = both(kept_ref[...], by_squares(came_ref[:width, :]))
    keep_ref[...] = whole[:half]
    send_ref[...] = whole[half:]
    sum_ref[...] = both(small_ref[...], came_ref[width:, :])


def merge_kernel(s, one_ref, one_came_ref, two_ref, two_came_ref, side_ref, side_came_ref, keep_ref, send_ref, sems):
    half = keep_ref.shape[0]
    start = 0
    for kept, came in ((one_ref, one_came_ref), (two_ref, two_came_ref), (side_ref, side_came_ref)):
        columns = pl.ds(start, kept.shape[2])
        keep_ref[:, :, columns] = both(kept[:half], came[:half])
        send_ref[:, :, columns] = both(kept[half:], came[half:])
        start += kept.shape[2]


def last_kernel(s, *refs):
    sum_ref = refs[-2]
    start = 0
    for n in range((len(refs) - 2) // 2):
        kept, came = refs[2 * n : 2 * n + 2]
        width = kept.shape[2]
        sum_ref[:, start : start + width] = both(kept[0], came[0])
        start += width


def sum_kernel(s, kept_ref, came_ref, sum_ref, sems):
    sum_ref[...] = both(kept_ref[...], came_ref[...])


def small_kernel(
    s, own_ref, came_ref, table_hbm, probe_ref, far_probe_ref, w_value_hbm, w_key_hbm, query_ref, w_query_hbm, cut_table_ref,
    cut_probe_ref, cut_query_ref,
    embed_ref, var_ref, value_grad_ref, key_grad_ref, query_grad_ref, vector_ref, bias_ref,
    table_ref, my_value_ref, w_key_ref, my_w_query_ref, sems, *, piece,
):
    moves = Moves(sems)
    mine = pl.ds(pl.multiple_of(s[2] * piece, piece), piece)
    copies = [
        moves.start(table_hbm, table_ref),
        moves.start(w_value_hbm.at[mine, :], my_value_ref),
        moves.start(w_key_hbm, w_key_ref),
        moves.start(w_query_hbm.at[mine, :], my_w_query_ref),
    ]
    own, came = own_ref[...], came_ref[...]
    swap = s[0] == 1
    low = jnp.where(swap, came, own)
    high = jnp.where(swap, own, came)
    probes = (probe_ref[...], far_probe_ref[...])
    probe_low = jnp.where(swap, probes[1], probes[0])
    probe_high = jnp.where(swap, probes[0], probes[1])
    my_table = cut_table_ref[...]
    my_probe = cut_probe_ref[...]
    marked = (lax.broadcasted_iota(jnp.int32, (8, PADDED), 1) == ROWS).astype(f32).astype(bf16)
    wait(*copies)
    my_value = my_value_ref[...]
    table_grad = None
    for c, part in enumerate((low, high)):
        for n in range(HALF // LANES):
            g = part[:LANES, n * PADDED : (n + 1) * PADDED]
            columns = slice(c * HALF + n * LANES, c * HALF + (n + 1) * LANES)
            value_grad_ref[:, columns] = dot(my_table, g, (0, 1))
            bias_ref[:, columns] = dot(marked, g, (1, 1))
            term = dot(g, my_value[:, columns], (0, 1))
            table_grad = term if table_grad is None else table_grad + term
    coef = jnp.concatenate([low[128:136, :PADDED].astype(f32), high[128:136, :PADDED].astype(f32)], axis=0) * 0.125
    coef_low = coef.astype(bf16)
    probe3 = in_three(my_probe)
    for n in range(3):
        table_grad = table_grad + dot(coef_low, probe3[n * HEADS : (n + 1) * HEADS], (0, 0))
    by_cell = in_three(table_grad[:CELLS])
    perm = cell_order()
    embed_ref[...] = sum(dot(perm, by_cell[n * CELLS : (n + 1) * CELLS], (0, 0)) for n in range(3))
    var_ref[...] = table_grad[CELLS:ROWS]
    probe_grad = dot(coef_low, table_ref[...], (1, 0))
    my_probe_grad = dot(coef_low, my_table, (1, 0))
    row = lax.broadcasted_iota(jnp.int32, (HEADS, D), 0)
    lane = lax.broadcasted_iota(jnp.int32, (HEADS, D), 1)
    own_head = (lane >= row * HD) & (lane < (row + 1) * HD)
    asked = jnp.concatenate([probe_low[8:9, :HALF], probe_high[8:9, :HALF]], axis=1)
    key_grad_ref[...] = dot(my_probe_grad, jnp.where(own_head, asked, 0.0), (0, 0), f32, highest)
    asked_grad = summed_rows(dot(in_three(probe_grad), w_key_ref[...], (1, 0)), HEADS)
    asked_grad = column_sums(jnp.where(own_head, asked_grad, 0.0))
    my_query = jnp.broadcast_to(cut_query_ref[...].astype(f32), (8, piece))
    first_row = lax.broadcasted_iota(jnp.int32, (8, D), 0) == 0
    query_grad_ref[...] = dot(my_query, jnp.where(first_row, asked_grad, 0.0), (0, 0), f32, highest)
    vector_ref[...] = summed_rows(dot(in_three(jnp.broadcast_to(asked_grad, (8, D))), my_w_query_ref[...], (1, 1)), 8)


def four_places(s, refs, width):
    for n, ref in enumerate(refs):
        core = s[0] if n < 2 else 1 - s[0]
        far = s[1] if n % 2 == 0 else 1 - s[1]
        yield ref[...].astype(f32), pl.multiple_of((core * 2 + far) * width, width)


def mlp_final_kernel(s, one_ref, two_ref, three_ref, four_ref, up_ref, down_ref, sems):
    width = one_ref.shape[1] // 2
    for block, start in four_places(s, (one_ref, two_ref, three_ref, four_ref), width):
        up_ref[:, pl.ds(start, width)] = block[:, :width]
        down_ref[pl.ds(start, width), :] = jnp.transpose(block[:, width:])


def attend_final_kernel(s, one_ref, two_ref, three_ref, four_ref, qkv_ref, proj_ref, out_ref, pos_ref, sems):
    for block, start in four_places(s, (one_ref, two_ref, three_ref, four_ref), QUARTER):
        for n in range(3):
            place = pl.ds(pl.multiple_of(n * D + start, QUARTER), QUARTER)
            qkv_ref[:, place] = block[:, n * QUARTER : (n + 1) * QUARTER]
        place = pl.ds(start, QUARTER)
        proj_ref[:, place] = block[:, 3 * QUARTER : D]
        out_ref[:, place] = block[:, D : D + QUARTER]
        rows = pos_ref.shape[0]
        last = block[:, D + QUARTER :]
        pos_ref[:, place] = jnp.concatenate([last[:rows], last[rows:]], axis=1)


def bit_orders(groups):
    first = list(range(groups.bit_length() - 1))
    return first, first[1:] + first[:1]


def block_map(groups, way):
    order = bit_orders(groups)[way]
    bits = len(order)
    return [sum(1 << order[n] for n in range(bits) if j >> (bits - 1 - n) & 1) for j in range(groups)]


def swap_core(value):
    return lax.ppermute(value, "section", [(s, s ^ 1) for s in range(4)])


def swap_y(value):
    return lax.ppermute(value, "section", [(s, s ^ 2) for s in range(4)])


def swap_stage(value, groups, stage, way=0):
    bit = 1 << bit_orders(groups)[way][stage]
    return lax.ppermute(value, "dp", [(g, g ^ bit) for g in range(groups)])


def cut(value, start, length, axis):
    return lax.dynamic_slice_in_dim(value, start, length, axis)


def narrow_mlp_sums(blocks, second_blocks, piece, core, far, normed, first, second, cotangent, w_up, b_up, w_down, pre_grad, hidden):
    rows = first.shape[0]
    quarter = hidden.shape[2]
    order = lambda v, chosen_blocks: jnp.concatenate([cut(v, b * piece, piece, 1) for b in chosen_blocks], axis=1)
    other_cot = [cut(cotangent, ((1 - far) * 2 + c) * rows, rows, 0) for c in (core, 1 - core)]
    other = jnp.concatenate([first, second])
    pre = dot(other, cut(w_up, (2 * core + far) * quarter, quarter, 1), (1, 0)) + cut(
        b_up, (2 * core + far) * quarter, quarter, 0
    )
    gate, slope = gelu_both(pre)
    back = dot(jnp.concatenate(other_cot), cut(w_down, (2 * core + far) * quarter, quarter, 0), (1, 1))
    pre_grads = jnp.concatenate([lax.dynamic_index_in_dim(pre_grad, far, 0, False), (back * slope).astype(bf16)])
    hiddens = jnp.concatenate([lax.dynamic_index_in_dim(hidden, far, 0, False), gate.astype(bf16)])
    up = dot(order(jnp.concatenate([normed, other]), blocks), pre_grads, (0, 0), bf16)
    cots = jnp.concatenate([cut(cotangent, far * 2 * rows, 2 * rows, 0)] + other_cot)
    down = dot(order(cots, second_blocks), hiddens, (0, 0), bf16)
    return up[D // 2 :], up[: D // 2], down[D // 2 :], down[: D // 2]


def narrow_head_sums(blocks, piece, core, far, normed, keep, send, attended, attended_far, mid_grad):
    order = lambda v: jnp.concatenate([cut(v, b * piece, piece, 1) for b in blocks], axis=1)
    left = order(normed)
    features = order(jnp.where(core == 0, *(jnp.concatenate(v, axis=1) for v in ((attended, attended_far), (attended_far, attended)))))
    one = [dot(left, v[:, : 2 * QUARTER], (0, 0), bf16) for v in (send, keep)]
    parts = []
    for v, y in ((keep, far), (send, 1 - far)):
        parts.append(dot(left, v[:, 2 * QUARTER :], (0, 0), bf16))
        parts.append(dot(features, cut(mid_grad, core * HALF + y * QUARTER, QUARTER, 1), (0, 0), bf16))
    two = jnp.concatenate(parts, axis=1)
    return one + [two[D // 2 :], two[: D // 2]]


def narrow_side_sums(blocks, piece, core, head, head_far, start_sides, small):
    order = lambda v, width: jnp.concatenate([cut(v, b * width, width, 0) for b in blocks])
    heads = order(jnp.where(core == 0, *(jnp.concatenate(v) for v in ((head, head_far), (head_far, head)))), piece)
    count, seq = blocks.shape[0], head.shape[1]
    parts = []
    for side in range(2):
        start = start_sides[:, side * QUARTER : (side + 1) * QUARTER]
        parts.append(dot(heads, start, (1, 0), bf16))
        pos = order(start, seq // count).reshape(count, seq // count, 2, LANES)
        parts.append(jnp.transpose(pos, (0, 2, 1, 3)).reshape(-1, LANES))
    kept, sent = jnp.concatenate(parts[:2], axis=1), jnp.concatenate(parts[2:], axis=1)
    return jnp.concatenate([by_squares(sent), small]), kept


def added(kept, arrived):
    return (kept.astype(f32) + arrived.astype(f32)).astype(bf16)


def local(
    pixels, cell_mask, lead_time, query, w_query, w_key, w_value, b_value, w_out, b_out, w_embed,
    var_embed, pos_embed, w_lead, b_lead, gain_one, shift_one, w_qkv, w_proj, b_proj, gain_two,
    shift_two, w_up, b_up, w_down, b_down, cotangent,
):
    groups = lax.axis_size("dp")
    stages = groups.bit_length() - 1
    me = lax.axis_index("dp")
    section = lax.axis_index("section")
    core, far = section % 2, section // 2
    seq = pixels.shape[0] // lead_time.shape[0]
    rows = seq // 2
    units = w_up.shape[1]
    quarter = units // 4
    piece = D // groups
    narrow = piece % LANES != 0
    blocks, second_blocks = (me ^ jnp.array(block_map(groups, way), jnp.int32) for way in range(2))
    scalars = jnp.concatenate([jnp.stack([core, far, me]), blocks, second_blocks]).astype(jnp.int32)
    row = lambda v: v.reshape(1, -1)
    pix, mask = jnp.transpose(pixels), jnp.transpose(cell_mask)
    lead = scalar(lead_time)
    half = groups // 2
    sizes = dict(piece=piece, groups=groups)
    held = lambda *shape: pltpu.VMEM(shape, bf16)
    wide = lambda *shape: pltpu.VMEM(shape, f32)
    kept_far = True

    start_part, per_head, coef, tv, table, probe = call(
        start_kernel,
        scalars,
        [
            remote(pix), remote(mask), row(query), remote(w_query), remote(w_key), remote(w_value), row(b_value),
            remote(w_out), remote(w_embed), remote(var_embed),
        ],
        [
            ((seq, D), bf16), ((HALF, seq), bf16, kept_far), ((PADDED, OWN_HEADS), f32), ((HALF, PADDED), bf16, kept_far),
            ((PADDED, D), bf16, kept_far), ((16, D), f32),
        ],
        scratch=[
            held(D, HALF), held(D, HALF), held(D, HALF), held(HALF, D), held(HALF, seq), held(HALF, PADDED), held(PADDED, D),
            held(CELLS, seq), pltpu.VMEM((CELLS, seq), jnp.int32), held(CELLS, D), held(VARS, D),
        ],
        us=6,
    )
    start_near, proj_part, start, normed_one, qkv, lse, attended = call(
        attend_kernel,
        scalars,
        [
            start_part, swap_core(start_part), pos_embed, lead, row(w_lead), row(b_lead), row(b_out), row(gain_one),
            row(shift_one), remote(w_qkv), remote(w_proj),
        ],
        [
            ((seq, D), bf16), ((seq, D), bf16), ((seq, D), bf16, kept_far), ((seq, D), bf16, kept_far),
            ((seq, 3 * HALF), bf16, kept_far), ((OWN_HEADS // 2, seq, LANES), f32, kept_far),
            ((seq, HALF), bf16, kept_far),
        ],
        scratch=[
            held(3, D, HALF), held(HALF, D), held(seq, D), held(seq, 3 * HALF), wide(OWN_HEADS // 2, seq, LANES),
            held(seq, HALF),
        ],
        us=12,
    )
    proj_came = swap_core(proj_part)
    normed_near, half_two, mid, normed_two = call(
        middle_kernel,
        scalars,
        [
            start_near, lead, row(w_lead), row(b_lead), row(b_proj), proj_part, proj_came, row(gain_two), row(shift_two),
        ],
        [((seq, D), bf16), ((rows, D), bf16), ((seq, D), bf16, kept_far), ((seq, D), bf16, kept_far)],
        scratch=[held(seq, D)],
        us=2.5,
    )
    other_two = swap_y(half_two)
    up_sums, normed_part, hidden, pre_grad = call(
        mlp_kernel,
        scalars,
        [normed_near, remote(cotangent), remote(w_up), row(b_up), remote(w_down)],
        [
            ((1, 2 * quarter), f32), ((seq, D), bf16), ((2, seq, quarter), bf16, kept_far),
            ((2, seq, quarter), bf16, kept_far),
        ],
        scratch=[
            held(2, seq, quarter), held(2, seq, quarter), held(2, D, quarter), held(2, quarter, D), held(seq, D),
        ],
        mb=32,
        us=11,
    )
    normed_came = swap_core(normed_part)
    other_held, _ = lax.optimization_barrier((other_two, normed_part))
    other_two_far = swap_core(other_held)
    if narrow:
        up_send, up_keep, down_send, down_keep = narrow_mlp_sums(
            blocks, second_blocks, piece, core, far, normed_two, other_two, other_two_far, cotangent, w_up, b_up, w_down, pre_grad, hidden
        )
    else:
        up_send, up_keep, down_send, down_keep = call(
            functools.partial(mlp_grads_kernel, **sizes),
            scalars,
            [remote(x) for x in (normed_two, other_two, other_two_far, cotangent, w_up)]
            + [row(b_up), remote(w_down), remote(pre_grad), remote(hidden)],
            [((D // 2, quarter), bf16, kept_far)] * 4,
            scratch=[
                held(2 * seq, D), held(2 * seq, D), held(D, quarter), held(quarter, D), held(2 * seq, quarter),
                held(2 * seq, quarter), held(2, D, quarter),
            ],
            us=15,
            mb=40,
            after=[normed_came],
        )
    by_block = lambda value: value.reshape(half, piece, value.shape[1])
    up_keep, down_keep = by_block(up_keep), by_block(down_keep)
    up_came = swap_stage(by_block(up_send), groups, 0)
    down_came = swap_stage(by_block(down_send), groups, 0, 1)

    def halved(arrays, after):
        outs = [((v.shape[0] // 2,) + v.shape[1:], bf16) for v in arrays[::2] for _ in range(2)]
        return call(halves_kernel, scalars, arrays, outs, us=1, mb=16, after=after)


    norm_one, norm_two, mid_sums, qkv_keep, qkv_send, mid_grad = call(
        attend_back_kernel,
        scalars,
        [
            normed_part, normed_came, remote(mid), remote(cotangent), row(gain_two), remote(qkv), remote(attended),
            remote(lse), remote(w_proj), remote(w_qkv),
        ],
        [
            ((rows, D), bf16), ((rows, D), bf16), ((8, D), f32), ((seq, 3 * QUARTER), bf16, kept_far),
            ((seq, 3 * QUARTER), bf16, kept_far),
            ((seq, D), bf16, kept_far),
        ],
        scratch=[
            held(seq, D), held(seq, D), held(seq, 3 * HALF), held(seq, HALF), wide(OWN_HEADS // 2, seq, LANES),
            held(3, D, HALF), held(HALF, D), held(seq, HALF), held(seq, 3 * HALF), held(seq, 3 * QUARTER),
            held(seq, 3 * QUARTER), held(seq, D),
        ],
        mb=32,
        us=14,
        after=[up_send],
    )
    one_norm_came, two_norm_came = swap_core(norm_one), swap_core(norm_two)
    attended_far, per_head_far = swap_core(attended), swap_core(per_head)
    if narrow:
        one_send, one_keep, two_send, two_keep = narrow_head_sums(
            blocks, piece, core, far, normed_one, qkv_keep, qkv_send, attended, attended_far, mid_grad
        )
    else:
        one_send, one_keep, two_send, two_keep = call(
            functools.partial(head_grads_kernel, **sizes),
            scalars,
            [remote(x) for x in (normed_one, qkv_keep, qkv_send, attended, attended_far, mid_grad)],
            [((D, HALF), bf16)] * 2 + [((D // 2, D), bf16)] * 2,
            scratch=[held(seq, D), held(2, seq, 3 * QUARTER), held(2, seq, HALF), held(seq, HALF)],
            us=4,
            after=[norm_one],
        )
    one_came = swap_y(one_send.reshape(groups, piece, HALF))
    two_came = swap_stage(by_block(two_send), groups, 0)

    pix_kept, pix_sent, start_sides, small = call(
        start_back_kernel,
        scalars,
        [
            norm_one, norm_two, one_norm_came, two_norm_came, remote(start), lead, row(w_lead), row(b_lead), row(gain_one), remote(mid_grad),
            remote(w_out), remote(pix), remote(mask), coef, remote(tv), mid_sums, up_sums,
        ],
        [
            ((CELLS, rows), f32), ((CELLS, rows), bf16), ((seq, HALF), bf16, kept_far), ((SMALL_ROWS, D), bf16),
        ],
        scratch=[
            wide(CELLS, seq), held(HALF, D), held(seq, D), held(seq, D), held(HALF, PADDED), held(seq, D),
            held(seq, HALF), held(CELLS, seq), pltpu.VMEM((CELLS, seq), jnp.int32),
        ],
        us=7,
        after=[one_send],
    )
    small_came = swap_y(small)
    pixels_grad = jnp.transpose(pix_kept + swap_core(pix_sent).astype(f32))

    if narrow:
        side_sent, side_keep = narrow_side_sums(blocks, piece, core, per_head, per_head_far, start_sides, small)
    else:
        side_sent, side_keep = call(
            functools.partial(side_grads_kernel, **sizes),
            scalars,
            [remote(x) for x in (per_head, per_head_far, start_sides)] + [small],
            [((QUARTER + LANES + SMALL_ROWS, D), bf16), ((D, QUARTER + LANES), bf16)],
            scratch=[held(2, HALF, seq), held(seq, HALF), wide(seq, HALF)],
            us=4,
        )
    side_came = swap_y(side_sent)
    up_keep, up_send, down_keep, down_send = halved([up_keep, up_came, down_keep, down_came], [side_keep])
    up_came, down_came = swap_stage(up_send, groups, 1), swap_stage(down_send, groups, 1, 1)
    out_sent, out_kept = call(
        out_kernel,
        scalars,
        [remote(hidden), remote(w_down), remote(mid), row(b_down)],
        [((rows, D), bf16), ((rows, D), f32)],
        scratch=[wide(seq, D), held(2, seq, quarter), held(2, quarter, D), held(rows, D)],
        us=4,
        after=[up_keep],
    )
    out_came = swap_core(out_sent)

    block_out = (out_kept + out_came.astype(f32)).astype(bf16)

    def summed(kept, arrived, after=()):
        return call(sum_kernel, scalars, [kept, arrived], [(kept.shape, bf16)], us=1, mb=16, after=after)[0]

    head_rows = ((half, piece, HALF), bf16)
    one_keep, one_send, two_keep, two_send = call(
        heads_kernel,
        scalars,
        [one_keep.reshape(groups, piece, HALF), one_came, by_block(two_keep), two_came],
        [head_rows] * 4,
        us=1,
        mb=16,
        after=[out_sent],
    )
    one_came, two_came = swap_stage(one_send, groups, 0), swap_y(two_send)
    stages = groups.bit_length() - 1
    last = one_keep
    for stage in range(2, stages):
        up_keep, up_send, down_keep, down_send = halved([up_keep, up_came, down_keep, down_came], [last])
        up_came, down_came = swap_stage(up_send, groups, stage), swap_stage(down_send, groups, stage, 1)
        last = up_keep
    side_rows = ((D // 2, QUARTER + LANES), bf16)
    side_keep, side_send, small = call(
        sides_kernel,
        scalars,
        [side_keep, small, side_came],
        [side_rows] * 2 + [((SMALL_ROWS, D), bf16)],
        us=1,
        mb=16,
        after=[last],
    )
    side_came, small_came = swap_stage(by_block(side_send), groups, 0), swap_stage(small, groups, 0)
    mlp_piece = call(
        last_kernel,
        scalars,
        [up_keep, up_came, down_keep, down_came],
        [((piece, 2 * quarter), bf16)],
        us=1,
        after=[side_keep],
    )[0]
    mlp_y, mlp_core = swap_y(mlp_piece), swap_core(mlp_piece)
    small = summed(small, small_came, [mlp_piece])
    small_came = swap_stage(small, groups, 1)
    rest = ((half // 2, piece, D + QUARTER + LANES), bf16)
    attend_keep, attend_send = call(
        merge_kernel,
        scalars,
        [one_keep, one_came, two_keep, two_came, by_block(side_keep), side_came],
        [rest] * 2,
        us=1,
        mb=16,
        after=[small],
    )
    attend_came = swap_stage(attend_send, groups, 1)
    for stage in range(2, stages):
        small = summed(small, small_came, [attend_keep])
        small_came = swap_stage(small, groups, stage)
        attend_keep, attend_send = halved([attend_keep, attend_came], [small])
        attend_came = swap_stage(attend_send, groups, stage)
    small = summed(small, small_came, [attend_keep])
    other_small = swap_core(small)

    far_probe = swap_core(probe)
    probes = jnp.concatenate([jnp.where(core == c, probe, far_probe)[:OWN_HEADS] for c in range(2)])
    my_probe = cut(probes, me * piece, piece, 1)
    my_table = cut(table, me * piece, piece, 1)
    my_query = row(cut(query, me * piece, piece, 0))
    embed_grad, var_grad, w_value_grad, w_key_grad, w_query_grad, query_rows, bias_rows = call(
        functools.partial(small_kernel, piece=piece),
        scalars,
        [
            small, other_small, remote(table), probe, far_probe, remote(w_value), remote(w_key), row(query),
            remote(w_query), my_table, my_probe, my_query,
        ],
        [
            ((CELLS, piece), f32), ((VARS, piece), f32), ((piece, D), f32), ((piece, D), f32), ((piece, D), f32),
            ((8, piece), f32), ((8, D), f32),
        ],
        scratch=[held(PADDED, D), held(piece, D), held(D, D), held(piece, D)],
        us=6,
        after=[small],
    )
    query_grad = query_rows[0]
    my_value_bias = cut(bias_rows, me * piece, piece, 1)[0]
    shared = jnp.where(core == 0, small, other_small)[136:145].astype(f32)
    shared = cut(shared, me * piece, piece, 1)
    gain_two_grad, shift_two_grad, b_proj_grad, b_down_grad, gain_one_grad = (shared[n] for n in range(5))
    shift_one_grad, b_lead_grad, w_lead_grad, b_out_grad = (shared[n] for n in range(5, 9))
    up_rows = [jnp.where(core == c, small, other_small)[145:147] for c in range(2)]
    up_bias_grad = jnp.concatenate(up_rows).reshape(-1).astype(f32)
    my_up_bias = cut(up_bias_grad, me * (units // groups), units // groups, 0)

    w_up_grad, w_down_grad = call(
        mlp_final_kernel,
        scalars,
        [mlp_piece, mlp_y, mlp_core, swap_core(mlp_y)],
        [((piece, units), f32), ((units, piece), f32)],
        us=3,
        after=[embed_grad],
    )
    attend_piece = call(
        last_kernel, scalars, [attend_keep, attend_came], [((piece, D + QUARTER + LANES), bf16)], us=1, after=[w_up_grad]
    )[0]
    attend_y = swap_y(attend_piece)
    attend_core = swap_core(attend_piece)
    w_qkv_grad, w_proj_grad, w_out_grad, pos_grad = call(
        attend_final_kernel,
        scalars,
        [attend_piece, attend_y, attend_core, swap_core(attend_y)],
        [((piece, 3 * D), f32), ((piece, D), f32), ((piece, D), f32), ((seq // groups, D), f32)],
    )
    return (
        block_out, pixels_grad, query_grad, w_query_grad, w_key_grad, w_value_grad, my_value_bias, w_out_grad, b_out_grad,
        embed_grad, var_grad, pos_grad, w_lead_grad, b_lead_grad, gain_one_grad, shift_one_grad, w_qkv_grad, w_proj_grad,
        b_proj_grad, gain_two_grad, shift_two_grad, w_up_grad, my_up_bias, w_down_grad, b_down_grad,
    )


def solution(mesh):
    whole = P()
    args = (P("dp", None), P("dp", None), P("dp")) + (whole,) * 23 + (P("dp", None),)
    outs = (
        (P(axes, None),) * 2
        + (P("dp"),)
        + (P("dp", None),) * 3
        + (P("dp"), P("dp", None), P("dp"), P(None, "dp"), P(None, "dp"), P("dp", None))
        + (P("dp"),) * 4
        + (P("dp", None),) * 2
        + (P("dp"),) * 3
        + (P("dp", None), P("dp"), P(None, "dp"), P("dp"))
    )
    return jax.shard_map(local, mesh=mesh, in_specs=args, out_specs=outs, check_vma=False)
```

```python
import functools

import jax
import jax.numpy as jnp
from jax import lax
from jax.experimental import pallas as pl
from jax.experimental.pallas import tpu as pltpu
from jax.sharding import PartitionSpec as P

D = 1024
HEADS = 16
HD = 64
VARS = 48
PIX = 4
CELLS = VARS * PIX
ROWS = CELLS + VARS
PADDED = 256
OWN_HEADS = HEADS // 2
HALF = D // 2
QUARTER = D // 4
LANES = 128
SMALL_ROWS = 160

highest = lax.Precision.HIGHEST
epsilon = 1e-05
bf16 = jnp.bfloat16
f32 = jnp.float32
axes = ("dp", "section")


def dot(a, b, contract, kind=f32, precision=None):
    return lax.dot_general(
        a, b, ((contract[:1], contract[1:]), ((), ())), precision=precision, preferred_element_type=kind
    )


def call(body, scalars, ins, outs, scratch=(), us=2, mb=16, after=()):
    del scalars
    arrays, in_specs = [], []
    for item in list(ins) + [x if isinstance(x, tuple) else (x, pl.ANY) for x in after]:
        array, space = item if isinstance(item, tuple) else (item, pltpu.VMEM)
        in_specs.append(pl.BlockSpec(memory_space=space))
        arrays.append(array)
    count = len(ins)

    def placed(*refs):
        body(Place(), *refs[:count], *refs[count + len(after) :])

    return pl.pallas_call(
        placed,
        in_specs=in_specs,
        out_specs=[pl.BlockSpec(memory_space=pltpu.HBM if len(item) > 2 else pltpu.VMEM) for item in outs],
        out_shape=[
            pltpu.HBM(*item[:2]) if len(item) > 2 else jax.ShapeDtypeStruct(*item) for item in outs
        ],
        scratch_shapes=list(scratch) + [pltpu.SemaphoreType.DMA((24,))],
        compiler_params=pltpu.CompilerParams(vmem_limit_bytes=mb << 20),
        cost_estimate=pl.CostEstimate(flops=int(us * 1e7), bytes_accessed=1 << 12, transcendentals=0),
    )(*arrays)


class Place:
    def __getitem__(self, n):
        if n < 2:
            section = lax.axis_index("section")
            return section & 1 if n == 0 else section >> 1
        me = lax.axis_index("dp")
        if n == 2:
            return me
        groups = lax.axis_size("dp")
        return me ^ block_map(groups, (n - 3) // groups)[(n - 3) % groups]


def remote(array):
    return pltpu.with_memory_space_constraint(array, pltpu.HBM), pltpu.HBM


def scalar(array):
    return array, pltpu.SMEM


class Moves:
    def __init__(self, sems):
        self.sems, self.count = sems, 0

    def start(self, source, place):
        copy = pltpu.make_async_copy(source, place, self.sems.at[self.count])
        self.count += 1
        copy.start()
        return copy


def wait(*copies):
    for copy in copies:
        copy.wait()


def part_of(start, size):
    return pl.ds(pl.multiple_of(start * size, size), size)


def cell_order():
    row = lax.broadcasted_iota(jnp.int32, (CELLS, CELLS), 0)
    column = lax.broadcasted_iota(jnp.int32, (CELLS, CELLS), 1)
    cell = sum((row >= n * VARS).astype(jnp.int32) for n in range(1, PIX))
    return ((row - cell * VARS) * PIX + cell == column).astype(f32).astype(bf16)


def in_three(value):
    high = value.astype(bf16).astype(f32)
    middle = (value - high).astype(bf16).astype(f32)
    return jnp.concatenate([high, middle, value - high - middle], axis=0).astype(bf16)


def summed_rows(value, rows):
    return value[:rows] + value[rows : 2 * rows] + value[2 * rows :]


def head_weights(cells, pen, coef, h):
    scores = pen + coef[CELLS:ROWS, h : h + 1]
    for j in range(PIX):
        rows = slice(j * VARS, (j + 1) * VARS)
        scores = scores + cells[rows] * coef[rows, h : h + 1]
    raised = jnp.exp(scores - jnp.max(scores, axis=0, keepdims=True))
    return raised / jnp.sum(raised, axis=0, keepdims=True)


def head_features(cells, weight):
    parts = [weight * cells[j * VARS : (j + 1) * VARS] for j in range(PIX)]
    parts = parts + [weight, jnp.ones((PADDED - ROWS, weight.shape[1]), f32)]
    return jnp.concatenate(parts, axis=0).astype(bf16)


def load_cells(pix_ref, mask_ref, perm):
    mask = mask_ref[...].astype(f32).astype(bf16)
    masked = pix_ref[...] * mask
    cells = dot(perm, masked, (1, 0))
    seen = dot(perm, mask, (1, 0))
    present = seen[:VARS]
    for j in range(1, PIX):
        present = jnp.maximum(present, seen[j * VARS : (j + 1) * VARS])
    return cells, seen, (present - 1.0) * 10000.0


def start_kernel(
    s, pix_hbm, mask_hbm, query_ref, w_query_hbm, w_key_hbm, w_value_hbm, b_value_hbm, w_out_hbm, embed_hbm, var_hbm,
    part_ref, per_head_hbm, coef_ref, tv_hbm, table_hbm, probe_ref,
    w_query_ref, w_key_ref, w_value_ref, w_out_ref, per_head_ref, tv_ref, table_ref, pix_ref, mask_ref, embed_ref, var_ref,
    b_value_ref, sems,
):
    half = part_of(s[0], HALF)
    seq = part_ref.shape[0]
    moves = Moves(sems)
    sample = part_of(s[1], seq)
    tables = [moves.start(embed_hbm, embed_ref), moves.start(var_hbm, var_ref)]
    pixels = [
        moves.start(pix_hbm.at[:, sample], pix_ref), moves.start(mask_hbm.at[:, sample], mask_ref),
        moves.start(b_value_hbm, b_value_ref),
    ]
    copies = [
        moves.start(w_query_hbm.at[:, half], w_query_ref),
        moves.start(w_key_hbm.at[:, half], w_key_ref),
        moves.start(w_value_hbm.at[:, half], w_value_ref),
        moves.start(w_out_hbm.at[half, :], w_out_ref),
    ]
    perm = cell_order()
    wait(*tables)
    table = jnp.concatenate(
        [
            dot(perm, embed_ref[...], (1, 0)),
            var_ref[...].astype(f32),
            jnp.zeros((PADDED - ROWS, D), f32),
        ]
    ).astype(bf16)
    table_ref[...] = table
    saved = [moves.start(table_ref, table_hbm)]
    wait(*pixels)
    cells, _, pen = load_cells(pix_ref, mask_ref, perm)
    wait(*copies[:3])
    asked = dot(query_ref[...], w_query_ref[...], (1, 0))
    row = lax.broadcasted_iota(jnp.int32, (OWN_HEADS, HALF), 0)
    lane = lax.broadcasted_iota(jnp.int32, (OWN_HEADS, HALF), 1)
    by_head = jnp.where((lane >= row * HD) & (lane < (row + 1) * HD), asked, 0.0)
    probe = summed_rows(dot(in_three(by_head), w_key_ref[...], (1, 1)), OWN_HEADS)
    asked_row = jnp.concatenate([jnp.broadcast_to(asked, (8, HALF)), jnp.zeros((8, HALF), f32)], axis=1)
    probe_ref[...] = jnp.concatenate([probe, asked_row], axis=0)
    coef3 = dot(table, in_three(probe), (1, 1)) * 0.125
    coef = coef3[:, :OWN_HEADS] + coef3[:, OWN_HEADS : 2 * OWN_HEADS] + coef3[:, 2 * OWN_HEADS :]
    coef_ref[...] = coef
    tv = jnp.transpose(dot(table, w_value_ref[...], (1, 0))).astype(bf16)
    lane = lax.broadcasted_iota(jnp.int32, tv.shape, 1)
    tv = jnp.where(lane < ROWS, tv, jnp.zeros_like(tv))
    tv_ref[...] = tv
    saved.append(moves.start(tv_ref, tv_hbm))
    bias = b_value_ref[:, half]
    for h in range(OWN_HEADS):
        rows = slice(h * HD, (h + 1) * HD)
        features = head_features(cells, head_weights(cells, pen, coef, h))
        column = jnp.transpose(jnp.broadcast_to(bias[:, rows], (8, HD)))[:, :1]
        per_head_ref[rows, :] = (dot(tv[rows], features, (1, 0)) + column).astype(bf16)
    saved.append(moves.start(per_head_ref, per_head_hbm))
    wait(copies[3])
    part_ref[...] = dot(per_head_ref[...], w_out_ref[...], (0, 0)).astype(bf16)
    wait(*saved)


def norm_parts(value):
    average = jnp.mean(value, axis=-1, keepdims=True)
    centered = value - average
    scale = lax.rsqrt(jnp.mean(centered * centered, axis=-1, keepdims=True) + epsilon)
    return centered * scale, scale


def norm_back(normal, scale, gain, grad):
    inner = grad * gain
    return scale * (
        inner
        - jnp.mean(inner, axis=-1, keepdims=True)
        - normal * jnp.mean(inner * normal, axis=-1, keepdims=True)
    )


def gelu_both(x):
    k = 0.7978845608028654
    square = x * x
    t = jnp.tanh(x * (k + k * 0.044715 * square))
    gate = 0.5 + 0.5 * t
    slope = gate + (0.5 * x) * (1.0 - t * t) * (k + 3 * k * 0.044715 * square)
    return x * gate, slope


def total(first_ref, second_ref):
    return first_ref[...].astype(f32) + second_ref[...].astype(f32)


def column_sums(value):
    return jnp.sum(value, axis=0, keepdims=True)


def only_half(block, half):
    lane = lax.broadcasted_iota(jnp.int32, block.shape, 1)
    return jnp.where((lane >= HD) if half else (lane < HD), block, jnp.zeros_like(block))


def joined(low, high):
    lane = lax.broadcasted_iota(jnp.int32, low.shape, 1)
    return jnp.where(lane < HD, low, high)


def pair_columns(pair, part=0):
    return pl.ds(pl.multiple_of(part * HALF + pair * LANES, LANES), LANES)


def fetch_heads(moves, s, w_qkv_hbm, w_ref):
    return [moves.start(w_qkv_hbm.at[:, part_of(2 * n + s[0], HALF)], w_ref.at[n]) for n in range(3)]


def attend_kernel(
    s, own_ref, came_ref, pos_ref, lead_ref, w_lead_ref, b_lead_ref, b_out_ref, gain_ref, shift_ref, w_qkv_hbm,
    w_proj_hbm,
    start_ref, part_ref, start_hbm, normed_hbm, qkv_hbm, lse_hbm, out_hbm,
    w_ref, w_proj_ref, normed_ref, qkv_ref, lse_ref, out_ref, sems,
):
    moves = Moves(sems)
    copies = fetch_heads(moves, s, w_qkv_hbm, w_ref)
    proj_copy = moves.start(w_proj_hbm.at[part_of(s[0], HALF), :], w_proj_ref)
    start = (total(own_ref, came_ref) + b_out_ref[...] + pos_ref[...].astype(f32)).astype(bf16)
    start_ref[...] = start
    saved = [moves.start(start_ref, start_hbm)]
    stream = start.astype(f32) + lead_ref[s[1]] * w_lead_ref[...] + b_lead_ref[...]
    normal, _ = norm_parts(stream)
    normed = (normal * gain_ref[...] + shift_ref[...]).astype(bf16)
    normed_ref[...] = normed
    saved.append(moves.start(normed_ref, normed_hbm))
    wait(*copies)
    for n in range(3):
        qkv_ref[:, n * HALF : (n + 1) * HALF] = dot(normed, w_ref[n], (1, 0)).astype(bf16)
    saved.append(moves.start(qkv_ref, qkv_hbm))

    def one_pair(pair, carried):
        q, k, v = (qkv_ref[:, pair_columns(pair, part)] for part in range(3))
        lane = lax.broadcasted_iota(jnp.int32, v.shape, 1)
        outs, weights, norms = [], [], []
        for half in range(2):
            mine = (lane >= HD) if half else (lane < HD)
            logits = dot(only_half(q * jnp.asarray(0.125, bf16), half), k, (1, 1))
            top = jnp.max(logits, axis=1, keepdims=True)
            raised = jnp.exp(logits - top).astype(bf16)
            both = dot(raised, jnp.where(mine, v, jnp.ones_like(v)), (1, 0))
            outs.append(both)
            weights.append(pltpu.roll(both, HD, 1))
            norms.append(jnp.broadcast_to(top, both.shape))
        weight = joined(*weights)
        out_ref[:, pair_columns(pair)] = (joined(*outs) / weight).astype(bf16)
        lse_ref[pair] = joined(*norms) + jnp.log(weight)
        return carried

    lax.fori_loop(0, OWN_HEADS // 2, one_pair, 0)
    saved.append(moves.start(lse_ref, lse_hbm))
    saved.append(moves.start(out_ref, out_hbm))
    wait(proj_copy)
    part_ref[...] = dot(out_ref[...], w_proj_ref[...], (1, 0)).astype(bf16)
    wait(*saved)


def middle_kernel(
    s, start_ref, lead_ref, w_lead_ref, b_lead_ref, b_proj_ref, own_ref, came_ref, gain_ref, shift_ref,
    normed_ref, half_ref, mid_hbm, normed_hbm, mid_ref, sems,
):
    moves = Moves(sems)
    stream = start_ref[...].astype(f32) + lead_ref[s[1]] * w_lead_ref[...] + b_lead_ref[...]
    mid = (stream + b_proj_ref[...] + total(own_ref, came_ref)).astype(bf16)
    mid_ref[...] = mid
    saved = [moves.start(mid_ref, mid_hbm)]
    normal, _ = norm_parts(mid.astype(f32))
    normed_ref[...] = (normal * gain_ref[...] + shift_ref[...]).astype(bf16)
    saved.append(moves.start(normed_ref, normed_hbm))
    half_ref[...] = normed_ref[part_of(s[0], half_ref.shape[0]), :]
    wait(*saved)


def mlp_kernel(
    s, normed_ref, cot_hbm, w_up_hbm, b_up_ref, w_down_hbm, sums_ref, part_ref, hidden_hbm, pre_grad_hbm,
    hidden_ref, pre_grad_ref, w_up_ref, w_down_ref, cot_ref, sems,
):
    width = w_up_ref.shape[2]
    moves = Moves(sems)
    ups, downs, saved = [], [], []
    for n in range(2):
        place = part_of(2 * s[0] + n, width)
        ups.append(moves.start(w_up_hbm.at[:, place], w_up_ref.at[n]))
        if n == 0:
            cot_copy = moves.start(cot_hbm.at[part_of(s[1], cot_ref.shape[0]), :], cot_ref)
        downs.append(moves.start(w_down_hbm.at[place, :], w_down_ref.at[n]))
    wait(cot_copy)
    back = None
    for n in range(2):
        columns = slice(n * width, (n + 1) * width)
        wait(ups[n], downs[n])
        pre = dot(normed_ref[...], w_up_ref[n], (1, 0)) + b_up_ref[:, part_of(2 * s[0] + n, width)]
        hidden_grad = dot(cot_ref[...], w_down_ref[n], (1, 1))
        hidden, slope = gelu_both(pre)
        hidden_ref[n] = hidden.astype(bf16)
        pre_grad = hidden_grad * slope
        sums_ref[:, columns] = column_sums(pre_grad)
        low = pre_grad.astype(bf16)
        pre_grad_ref[n] = low
        term = dot(low, w_up_ref[n], (1, 1))
        back = term if back is None else back + term
        saved.append(moves.start(hidden_ref.at[n], hidden_hbm.at[n]))
        saved.append(moves.start(pre_grad_ref.at[n], pre_grad_hbm.at[n]))
    part_ref[...] = back.astype(bf16)
    wait(*saved)


def out_kernel(
    s, hidden_hbm, w_down_hbm, mid_hbm, b_down_ref, sent_ref, kept_ref, total_ref, hidden_ref, w_down_ref, mid_ref, sems
):
    width = w_down_ref.shape[1]
    rows = sent_ref.shape[0]
    moves = Moves(sems)
    copies = []
    for n in range(2):
        copies.append(moves.start(hidden_hbm.at[n], hidden_ref.at[n]))
        copies.append(moves.start(w_down_hbm.at[part_of(2 * s[0] + n, width), :], w_down_ref.at[n]))
    mid_copy = moves.start(mid_hbm.at[part_of(s[0], rows), :], mid_ref)
    wait(*copies[:2])
    result = dot(hidden_ref[0], w_down_ref[0], (1, 0))
    wait(*copies[2:])
    total_ref[...] = result + dot(hidden_ref[1], w_down_ref[1], (1, 0))
    wait(mid_copy)
    sent_ref[...] = total_ref[part_of(1 - s[0], rows), :].astype(bf16)
    kept_ref[...] = total_ref[part_of(s[0], rows), :] + mid_ref[...].astype(f32) + b_down_ref[...]


def attend_back_kernel(
    s, own_ref, came_ref, mid_hbm, cot_hbm, gain_ref, qkv_hbm, out_hbm, lse_hbm, w_proj_hbm, w_qkv_hbm,
    part_ref, sums_ref, keep_hbm, send_hbm, mid_grad_hbm,
    mid_ref, cot_ref, qkv_ref, out_ref, lse_ref, w_ref, w_proj_ref, grad_ref, back_ref, keep_ref, send_ref, mid_grad_ref,
    sems,
):
    seq = own_ref.shape[0]
    moves = Moves(sems)
    first = [moves.start(mid_hbm, mid_ref), moves.start(cot_hbm.at[part_of(s[1], seq), :], cot_ref)]
    proj_copy = moves.start(w_proj_hbm.at[part_of(s[0], HALF), :], w_proj_ref)
    copies = [
        moves.start(qkv_hbm, qkv_ref), moves.start(out_hbm, out_ref), moves.start(lse_hbm, lse_ref)
    ]
    heads = fetch_heads(moves, s, w_qkv_hbm, w_ref)
    grad = total(own_ref, came_ref)
    wait(*first)
    cot = cot_ref[...].astype(f32)
    normal, scale = norm_parts(mid_ref[...].astype(f32))
    mid_grad = cot + norm_back(normal, scale, gain_ref[...], grad)
    sums_ref[...] = jnp.concatenate(
        [column_sums(grad * normal), column_sums(grad), column_sums(mid_grad), column_sums(cot), jnp.zeros((4, D), f32)]
    )
    low = mid_grad.astype(bf16)
    mid_grad_ref[...] = low
    saved = [moves.start(mid_grad_ref, mid_grad_hbm)]
    wait(proj_copy, *copies)
    grad_ref[...] = dot(low, w_proj_ref[...], (1, 1)).astype(bf16)

    def one_pair(pair, carried):
        q, k, v = (qkv_ref[:, pair_columns(pair, part)] for part in range(3))
        out_grad = grad_ref[:, pair_columns(pair)]
        weighted = out_grad.astype(f32) * out_ref[:, pair_columns(pair)].astype(f32)
        norms = lse_ref[pair]
        results = []
        for half in range(2):
            logits = dot(only_half(q * jnp.asarray(0.125, bf16), half), k, (1, 1))
            probs = jnp.exp(logits - norms[:, half * HD : half * HD + 1])
            probs_grad = dot(only_half(out_grad, half), v, (1, 1))
            shift = jnp.sum(only_half(weighted, half), axis=1, keepdims=True)
            logits_grad = (probs * (probs_grad - shift)).astype(bf16)
            results.append(
                (
                    dot(logits_grad, k, (1, 0)) * 0.125,
                    dot(logits_grad, q, (0, 0)) * 0.125,
                    dot(probs.astype(bf16), out_grad, (0, 0)),
                )
            )
        for part, (low_head, high_head) in enumerate(zip(*results)):
            back_ref[:, pair_columns(pair, part)] = joined(low_head, high_head).astype(bf16)
        return carried

    lax.fori_loop(0, OWN_HEADS // 2, one_pair, 0)
    for part in range(3):
        columns = slice(part * QUARTER, (part + 1) * QUARTER)
        mine = pl.multiple_of(part * HALF + s[1] * QUARTER, LANES)
        theirs = pl.multiple_of(part * HALF + (1 - s[1]) * QUARTER, LANES)
        keep_ref[:, columns] = back_ref[:, pl.ds(mine, QUARTER)]
        send_ref[:, columns] = back_ref[:, pl.ds(theirs, QUARTER)]
    saved += [moves.start(keep_ref, keep_hbm), moves.start(send_ref, send_hbm)]
    wait(*heads)
    back = None
    for n in range(3):
        term = dot(back_ref[:, n * HALF : (n + 1) * HALF], w_ref[n], (1, 1))
        back = term if back is None else back + term
    part_ref[...] = back.astype(bf16)
    wait(*saved)


def start_back_kernel(
    s, own_ref, came_ref, start_hbm, lead_ref, w_lead_ref, b_lead_ref, gain_ref, mid_grad_hbm, w_out_hbm, pix_hbm,
    mask_hbm, coef_ref, tv_hbm, sums_ref, up_sums_ref,
    pix_keep_ref, pix_send_ref, side_hbm, small_ref,
    held_ref, w_out_ref, start_ref, mid_grad_ref, tv_ref, start_grad_ref, side_ref, pix_ref, mask_ref, sems,
):
    moves = Moves(sems)
    first = [moves.start(start_hbm, start_ref), moves.start(mid_grad_hbm, mid_grad_ref)]
    seq = own_ref.shape[0]
    sample = part_of(s[1], seq)
    copies = [
        moves.start(w_out_hbm.at[part_of(s[0], HALF), :], w_out_ref), moves.start(tv_hbm, tv_ref),
        moves.start(pix_hbm.at[:, sample], pix_ref), moves.start(mask_hbm.at[:, sample], mask_ref),
    ]
    grad = total(own_ref, came_ref)
    lead = lead_ref[s[1]]
    wait(*first)
    stream = start_ref[...].astype(f32) + lead * w_lead_ref[...] + b_lead_ref[...]
    normal, scale = norm_parts(stream)
    stream_grad = mid_grad_ref[...].astype(f32) + norm_back(normal, scale, gain_ref[...], grad)
    start_grad = stream_grad.astype(bf16)
    start_grad_ref[...] = start_grad
    for side in range(2):
        side_ref[:, side * QUARTER : (side + 1) * QUARTER] = start_grad_ref[:, quarter_columns(s, side)]
    saved = [moves.start(side_ref, side_hbm)]
    lead_sum = column_sums(stream_grad)
    vectors = [
        sums_ref[0:4, :],
        column_sums(grad * normal),
        column_sums(grad),
        lead_sum,
        lead * lead_sum,
        column_sums(start_grad.astype(f32)),
        up_sums_ref[:, :D],
        up_sums_ref[:, D:],
        jnp.zeros((SMALL_ROWS - 136 - 11, D), f32),
    ]
    wait(*copies)
    per_head_grad = dot(w_out_ref[...], start_grad, (1, 1)).astype(bf16)

    cells, seen, pen = load_cells(pix_ref, mask_ref, cell_order())
    coef = coef_ref[...]
    tv = tv_ref[...]
    lane = lax.broadcasted_iota(jnp.int32, (PADDED, LANES), 1)
    coef_grad = jnp.zeros((PADDED, LANES), f32)
    cell_grad = [jnp.zeros((VARS, cells.shape[1]), f32) for _ in range(PIX)]
    for h in range(OWN_HEADS):
        rows = slice(h * HD, (h + 1) * HD)
        weight = head_weights(cells, pen, coef, h)
        features = head_features(cells, weight)
        head_grad = per_head_grad[rows]
        small_rows = slice((h % 2) * HD, (h % 2 + 1) * HD)
        small_ref[small_rows, (h // 2) * PADDED : (h // 2 + 1) * PADDED] = dot(head_grad, features, (1, 1)).astype(bf16)
        feature_grad = dot(tv[rows], head_grad, (0, 0))
        weight_grad = feature_grad[CELLS:ROWS]
        for j in range(PIX):
            part = slice(j * VARS, (j + 1) * VARS)
            weight_grad = weight_grad + feature_grad[part] * cells[part]
        score_grad = weight * (weight_grad - jnp.sum(weight * weight_grad, axis=0, keepdims=True))
        sums = []
        for j in range(PIX):
            part = slice(j * VARS, (j + 1) * VARS)
            cell_grad[j] = cell_grad[j] + feature_grad[part] * weight + score_grad * coef[part, h : h + 1]
            sums.append(jnp.sum(score_grad * cells[part], axis=1, keepdims=True))
        sums.append(jnp.sum(score_grad, axis=1, keepdims=True))
        sums.append(jnp.zeros((PADDED - ROWS, 1), f32))
        coef_grad = jnp.where(lane == h, jnp.concatenate(sums, axis=0), coef_grad)
    coef_rows = jnp.transpose(coef_grad)[:OWN_HEADS]
    coef_rows = jnp.concatenate([coef_rows, jnp.zeros((OWN_HEADS, D - PADDED), f32)], axis=1)
    small_ref[LANES:, :] = jnp.concatenate([coef_rows] + vectors, axis=0).astype(bf16)
    cell_grads = (jnp.concatenate(cell_grad, axis=0) * seen).astype(bf16)
    held_ref[...] = dot(cell_order(), cell_grads, (0, 0))
    columns = pix_keep_ref.shape[1]
    pix_keep_ref[...] = held_ref[:, part_of(s[0], columns)]
    pix_send_ref[...] = held_ref[:, part_of(1 - s[0], columns)].astype(bf16)
    wait(*saved)


def quarter_columns(s, side):
    far = s[1] if side == 0 else 1 - s[1]
    return pl.ds(pl.multiple_of(s[0] * HALF + far * QUARTER, QUARTER), QUARTER)


def mlp_grads_kernel(
    s, normed_hbm, first_hbm, second_hbm, cot_hbm, w_up_hbm, b_up_ref, w_down_hbm, pre_grad_hbm, hidden_hbm,
    up_send_hbm, up_keep_hbm, down_send_hbm, down_keep_hbm,
    normed_ref, cot_ref, w_up_ref, w_down_ref, pre_grad_ref, hidden_ref, sum_ref, sems, *, piece, groups,
):
    width = w_up_ref.shape[1]
    rows = first_hbm.shape[0]
    seq = 2 * rows
    place = part_of(2 * s[0] + s[1], width)
    moves = Moves(sems)
    own, one, two = pl.ds(0, seq), pl.ds(seq, rows), pl.ds(seq + rows, rows)
    first = [
        moves.start(w_up_hbm.at[:, place], w_up_ref),
        moves.start(first_hbm, normed_ref.at[one, :]),
        moves.start(second_hbm, normed_ref.at[two, :]),
        moves.start(cot_hbm.at[part_of((1 - s[1]) * 2 + s[0], rows), :], cot_ref.at[one, :]),
        moves.start(cot_hbm.at[part_of((1 - s[1]) * 2 + (1 - s[0]), rows), :], cot_ref.at[two, :]),
        moves.start(w_down_hbm.at[place, :], w_down_ref),
    ]
    then = [
        moves.start(cot_hbm.at[part_of(s[1], seq), :], cot_ref.at[own, :]),
        moves.start(normed_hbm, normed_ref.at[own, :]),
        moves.start(hidden_hbm.at[s[1]], hidden_ref.at[own, :]),
        moves.start(pre_grad_hbm.at[s[1]], pre_grad_ref.at[own, :]),
    ]
    wait(*first)
    pre = dot(normed_ref[seq:, :], w_up_ref[...], (1, 0)) + b_up_ref[:, place]
    hidden_grad = dot(cot_ref[seq:, :], w_down_ref[...], (1, 1))
    hidden, slope = gelu_both(pre)
    hidden_ref[seq:, :] = hidden.astype(bf16)
    pre_grad_ref[seq:, :] = (hidden_grad * slope).astype(bf16)
    wait(*then)
    half = groups // 2 * piece
    outs = ((up_send_hbm, up_keep_hbm), (down_send_hbm, down_keep_hbm))
    saved = []
    for n, (left_ref, right_ref) in enumerate(((normed_ref, pre_grad_ref), (cot_ref, hidden_ref))):
        left = chosen(left_ref, [s[3 + n * groups + b] for b in range(groups)], piece)
        sum_ref[n] = dot(left, right_ref[...], (0, 0)).astype(bf16)
        send_hbm, keep_hbm = outs[n]
        saved.append(moves.start(sum_ref.at[n, half:, :], send_hbm))
        saved.append(moves.start(sum_ref.at[n, :half, :], keep_hbm))
    wait(*saved)


def chosen(ref, blocks, piece):
    return jnp.concatenate([ref[:, part_of(b, piece)] for b in blocks], axis=1)


def head_grads_kernel(
    s, normed_hbm, keep_hbm, send_hbm, attended_hbm, attended_far_hbm, mid_grad_hbm, one_send_hbm, one_keep_hbm,
    two_send_hbm, two_keep_hbm, normed_ref, right_ref, attended_ref, mid_ref, one_ref, two_ref, sems, *, piece, groups,
):
    moves = Moves(sems)
    copies = [
        moves.start(normed_hbm, normed_ref), moves.start(send_hbm, right_ref.at[1]), moves.start(keep_hbm, right_ref.at[0])
    ]
    then = [
        moves.start(attended_hbm, attended_ref.at[s[0]]),
        moves.start(attended_far_hbm, attended_ref.at[1 - s[0]]),
        moves.start(mid_grad_hbm.at[:, quarter_columns(s, 0)], mid_ref.at[:, :QUARTER]),
        moves.start(mid_grad_hbm.at[:, quarter_columns(s, 1)], mid_ref.at[:, QUARTER:]),
    ]
    blocks = [s[3 + n] for n in range(groups)]
    wait(*copies)
    left = chosen(normed_ref, [s[3 + groups + n] for n in range(groups)], piece)
    both_qk = 2 * QUARTER
    saved = []
    for side, target in ((1, one_send_hbm), (0, one_keep_hbm)):
        one_ref[side] = dot(left, right_ref[side, :, :both_qk], (0, 0)).astype(bf16)
        saved.append(moves.start(one_ref.at[side], target))
    left = chosen(normed_ref, blocks, piece)
    wait(*then)
    features = jnp.concatenate([attended_ref[b >> 2, :, part_of(b & 3, piece)] for b in blocks], axis=1)
    half = two_keep_hbm.shape[0]
    for side in range(2):
        quarter = slice(side * QUARTER, (side + 1) * QUARTER)
        columns = side * both_qk
        two_ref[:, columns : columns + QUARTER] = dot(left, right_ref[side, :, both_qk:], (0, 0)).astype(bf16)
        two_ref[:, columns + QUARTER : columns + both_qk] = dot(features, mid_ref[:, quarter], (0, 0)).astype(bf16)
    saved.append(moves.start(two_ref.at[half:, :], two_send_hbm))
    saved.append(moves.start(two_ref.at[:half, :], two_keep_hbm))
    wait(*saved)


def side_grads_kernel(
    s, head_hbm, head_far_hbm, start_hbm, small_ref, sent_ref, kept_ref, head_ref, start_ref, pos_ref, sems, *, piece, groups
):
    moves = Moves(sems)
    seq = start_ref.shape[0]
    wait(
        moves.start(head_hbm, head_ref.at[s[0]]),
        moves.start(head_far_hbm, head_ref.at[1 - s[0]]),
        moves.start(start_hbm, start_ref),
    )
    pos_ref[...] = start_ref[...].astype(f32)
    count = groups // 2
    for first in (count, 0):
        blocks = [s[3 + n] for n in range(first, first + count)]
        per_head = jnp.concatenate([head_ref[b >> 2, part_of(b & 3, piece), :] for b in blocks], axis=0)
        out = dot(per_head, start_ref[...], (1, 0)).astype(bf16)
        columns = []
        for side in range(2):
            quarter = slice(side * QUARTER, (side + 1) * QUARTER)
            pos = []
            for b in blocks:
                block = pos_ref[part_of(b, seq // groups), quarter]
                pos += [block[:, :LANES], block[:, LANES:]]
            columns += [out[:, quarter], jnp.concatenate(pos, axis=0).astype(bf16)]
        columns = jnp.concatenate(columns, axis=1)
        if first == 0:
            kept_ref[...] = columns
        else:
            sent_ref[...] = packed(columns, small_ref[...])


def by_squares(value):
    rows, columns = value.shape
    return jnp.concatenate(
        [
            jnp.concatenate([value[r : r + LANES, c : c + LANES] for r in range(0, rows, LANES)], axis=1)
            for c in range(0, columns, LANES)
        ],
        axis=0,
    )


def packed(side, small):
    width = side.shape[0]
    return jnp.concatenate([by_squares(side)] + [small[:, n : n + width] for n in range(0, D, width)], axis=0)


def unpacked(value, columns):
    small = value[columns:]
    parts = D // value.shape[1]
    return by_squares(value[:columns]), jnp.concatenate(
        [small[n * SMALL_ROWS : (n + 1) * SMALL_ROWS] for n in range(parts)], axis=1
    )


def both(one, two):
    return (one.astype(f32) + two.astype(f32)).astype(bf16)


def fetched_halves_kernel(s, one_hbm, one_came, two_hbm, two_came, *refs):
    *outs, one_ref, two_ref, sems = refs
    moves = Moves(sems)
    copies = [moves.start(one_hbm, one_ref), moves.start(two_hbm, two_ref)]
    for n, (kept, came) in enumerate(((one_ref, one_came), (two_ref, two_came))):
        copies[n].wait()
        keep, send = outs[2 * n : 2 * n + 2]
        half = keep.shape[0]
        send[...] = both(kept[half:], came[half:])
        keep[...] = both(kept[:half], came[:half])


def halves_kernel(s, *refs):
    count = len(refs) // 4
    for n in range(count):
        kept, came = refs[2 * n : 2 * n + 2]
        keep, send = refs[2 * count + 2 * n : 2 * count + 2 * n + 2]
        half = keep.shape[0]
        send[...] = both(kept[half:], came[half:])
        keep[...] = both(kept[:half], came[:half])


def heads_kernel(s, one_ref, one_came_ref, two_ref, two_came_ref, one_keep, one_send, two_keep, two_send, sems):
    half = one_keep.shape[0]
    one_send[...] = both(one_ref[half:], one_came_ref[half:])
    one_keep[...] = both(one_ref[:half], one_came_ref[:half])
    width = two_keep.shape[2]
    two_send[...] = both(two_ref[:, :, width:], two_came_ref[:, :, width:])
    two_keep[...] = both(two_ref[:, :, :width], two_came_ref[:, :, :width])


def side_step_kernel(s, side_ref, small_ref, came_ref, keep_ref, sum_ref, *rest):
    side, small = unpacked(came_ref[...], side_ref.shape[1])
    side = both(side_ref[...], side)
    small = both(small_ref[...], small)
    sum_ref[...] = small
    rows, columns = keep_ref.shape
    keep_ref[...] = side[:rows, :columns]
    if columns < side.shape[1]:
        rest[0][...] = packed(side[:, columns:], small)
    elif rows < side.shape[0]:
        rest[0][...] = packed(side[rows:], small)


def last_kernel(s, *refs):
    sum_ref = refs[-2]
    start = 0
    pairs = (len(refs) - 2) // 2
    if len(refs) % 2:
        sum_ref[:, sum_ref.shape[1] - refs[-3].shape[1] :] = refs[-3][...]
    for n in range(pairs):
        kept, came = refs[2 * n : 2 * n + 2]
        width = kept.shape[2]
        sum_ref[:, start : start + width] = both(kept[0], came[0])
        start += width


def sum_kernel(s, kept_ref, came_ref, sum_ref, sems):
    sum_ref[...] = both(kept_ref[...], came_ref[...])


def small_kernel(
    s, own_ref, came_ref, table_hbm, probe_ref, far_probe_ref, w_value_hbm, w_key_hbm, query_ref, w_query_hbm, cut_table_ref,
    cut_probe_ref, cut_query_ref,
    embed_ref, var_ref, value_grad_ref, key_grad_ref, query_grad_ref, vector_ref, bias_ref,
    table_ref, my_value_ref, w_key_ref, my_w_query_ref, sems, *, piece,
):
    moves = Moves(sems)
    mine = pl.ds(pl.multiple_of(s[2] * piece, piece), piece)
    copies = [
        moves.start(table_hbm, table_ref),
        moves.start(w_value_hbm.at[mine, :], my_value_ref),
        moves.start(w_key_hbm, w_key_ref),
        moves.start(w_query_hbm.at[mine, :], my_w_query_ref),
    ]
    own, came = own_ref[...], came_ref[...]
    swap = s[0] == 1
    low = jnp.where(swap, came, own)
    high = jnp.where(swap, own, came)
    probes = (probe_ref[...], far_probe_ref[...])
    probe_low = jnp.where(swap, probes[1], probes[0])
    probe_high = jnp.where(swap, probes[0], probes[1])
    my_table = cut_table_ref[...]
    my_probe = cut_probe_ref[...]
    marked = (lax.broadcasted_iota(jnp.int32, (8, PADDED), 1) == ROWS).astype(f32).astype(bf16)
    wait(*copies)
    my_value = my_value_ref[...]
    table_grad = None
    for c, part in enumerate((low, high)):
        for n in range(HALF // LANES):
            g = part[:LANES, n * PADDED : (n + 1) * PADDED]
            columns = slice(c * HALF + n * LANES, c * HALF + (n + 1) * LANES)
            value_grad_ref[:, columns] = dot(my_table, g, (0, 1))
            bias_ref[:, columns] = dot(marked, g, (1, 1))
            term = dot(g, my_value[:, columns], (0, 1))
            table_grad = term if table_grad is None else table_grad + term
    coef = jnp.concatenate([low[128:136, :PADDED].astype(f32), high[128:136, :PADDED].astype(f32)], axis=0) * 0.125
    coef_low = coef.astype(bf16)
    probe3 = in_three(my_probe)
    for n in range(3):
        table_grad = table_grad + dot(coef_low, probe3[n * HEADS : (n + 1) * HEADS], (0, 0))
    by_cell = in_three(table_grad[:CELLS])
    perm = cell_order()
    embed_ref[...] = sum(dot(perm, by_cell[n * CELLS : (n + 1) * CELLS], (0, 0)) for n in range(3))
    var_ref[...] = table_grad[CELLS:ROWS]
    probe_grad = dot(coef_low, table_ref[...], (1, 0))
    my_probe_grad = dot(coef_low, my_table, (1, 0))
    row = lax.broadcasted_iota(jnp.int32, (HEADS, D), 0)
    lane = lax.broadcasted_iota(jnp.int32, (HEADS, D), 1)
    own_head = (lane >= row * HD) & (lane < (row + 1) * HD)
    asked = jnp.concatenate([probe_low[8:9, :HALF], probe_high[8:9, :HALF]], axis=1)
    key_grad_ref[...] = dot(my_probe_grad, jnp.where(own_head, asked, 0.0), (0, 0), f32, highest)
    asked_grad = summed_rows(dot(in_three(probe_grad), w_key_ref[...], (1, 0)), HEADS)
    asked_grad = column_sums(jnp.where(own_head, asked_grad, 0.0))
    my_query = jnp.broadcast_to(cut_query_ref[...].astype(f32), (8, piece))
    first_row = lax.broadcasted_iota(jnp.int32, (8, D), 0) == 0
    query_grad_ref[...] = dot(my_query, jnp.where(first_row, asked_grad, 0.0), (0, 0), f32, highest)
    vector_ref[...] = summed_rows(dot(in_three(jnp.broadcast_to(asked_grad, (8, D))), my_w_query_ref[...], (1, 1)), 8)


def four_places(s, refs, width):
    for n, ref in enumerate(refs):
        core = s[0] if n < 2 else 1 - s[0]
        far = s[1] if n % 2 == 0 else 1 - s[1]
        yield ref[...].astype(f32), pl.multiple_of((core * 2 + far) * width, width)


def mlp_final_kernel(s, one_ref, two_ref, three_ref, four_ref, up_ref, down_ref, sems):
    width = one_ref.shape[1] // 2
    for block, start in four_places(s, (one_ref, two_ref, three_ref, four_ref), width):
        up_ref[:, pl.ds(start, width)] = block[:, :width]
        down_ref[pl.ds(start, width), :] = jnp.transpose(block[:, width:])


def attend_final_kernel(s, one_ref, two_ref, three_ref, four_ref, qkv_ref, proj_ref, out_ref, pos_ref, sems):
    for block, start in four_places(s, (one_ref, two_ref, three_ref, four_ref), QUARTER):
        for n in range(3):
            place = pl.ds(pl.multiple_of(n * D + start, QUARTER), QUARTER)
            qkv_ref[:, place] = block[:, n * QUARTER : (n + 1) * QUARTER]
        place = pl.ds(start, QUARTER)
        proj_ref[:, place] = block[:, 3 * QUARTER : D]
        out_ref[:, place] = block[:, D : D + QUARTER]
        rows = pos_ref.shape[0]
        last = block[:, D + QUARTER :]
        pos_ref[:, place] = jnp.concatenate([last[:rows], last[rows:]], axis=1)


def bit_orders(groups):
    first = list(range(groups.bit_length() - 1))
    return first, first[1:] + first[:1]


def block_map(groups, way):
    order = bit_orders(groups)[way]
    bits = len(order)
    return [sum(1 << order[n] for n in range(bits) if j >> (bits - 1 - n) & 1) for j in range(groups)]


def swap_core(value):
    return lax.ppermute(value, "section", [(s, s ^ 1) for s in range(4)])


def swap_y(value):
    return lax.ppermute(value, "section", [(s, s ^ 2) for s in range(4)])


def swap_stage(value, groups, stage, way=0):
    bit = 1 << bit_orders(groups)[way][stage]
    return lax.ppermute(value, "dp", [(g, g ^ bit) for g in range(groups)])


def cut(value, start, length, axis):
    return lax.dynamic_slice_in_dim(value, start, length, axis)


def packed_narrow(side, small):
    return jnp.concatenate([side.reshape(-1), small.reshape(-1)]).reshape(-1, side.shape[0])


def unpacked_narrow(value, columns):
    flat = value.reshape(-1)
    size = columns * value.shape[1]
    return flat[:size].reshape(value.shape[1], columns), flat[size:].reshape(SMALL_ROWS, D)


def narrow_mlp_sums(blocks, second_blocks, piece, core, far, normed, first, second, cotangent, w_up, b_up, w_down, pre_grad, hidden):
    rows = first.shape[0]
    quarter = hidden.shape[2]
    order = lambda v, chosen_blocks: jnp.concatenate([cut(v, b * piece, piece, 1) for b in chosen_blocks], axis=1)
    other_cot = [cut(cotangent, ((1 - far) * 2 + c) * rows, rows, 0) for c in (core, 1 - core)]
    other = jnp.concatenate([first, second])
    pre = dot(other, cut(w_up, (2 * core + far) * quarter, quarter, 1), (1, 0)) + cut(
        b_up, (2 * core + far) * quarter, quarter, 0
    )
    gate, slope = gelu_both(pre)
    back = dot(jnp.concatenate(other_cot), cut(w_down, (2 * core + far) * quarter, quarter, 0), (1, 1))
    pre_grads = jnp.concatenate([lax.dynamic_index_in_dim(pre_grad, far, 0, False), (back * slope).astype(bf16)])
    hiddens = jnp.concatenate([lax.dynamic_index_in_dim(hidden, far, 0, False), gate.astype(bf16)])
    up = dot(order(jnp.concatenate([normed, other]), blocks), pre_grads, (0, 0), bf16)
    cots = jnp.concatenate([cut(cotangent, far * 2 * rows, 2 * rows, 0)] + other_cot)
    down = dot(order(cots, second_blocks), hiddens, (0, 0), bf16)
    return up[D // 2 :], up[: D // 2], down[D // 2 :], down[: D // 2]


def narrow_head_sums(blocks, second_blocks, piece, core, far, normed, keep, send, attended, attended_far, mid_grad):
    order = lambda v, way: jnp.concatenate([cut(v, b * piece, piece, 1) for b in way], axis=1)
    left = order(normed, second_blocks)
    features = [jnp.concatenate(v, axis=1) for v in ((attended, attended_far), (attended_far, attended))]
    features = order(jnp.where(core == 0, *features), blocks)
    one = [dot(left, v[:, : 2 * QUARTER], (0, 0), bf16) for v in (send, keep)]
    left = order(normed, blocks)
    parts = []
    for v, y in ((keep, far), (send, 1 - far)):
        parts.append(dot(left, v[:, 2 * QUARTER :], (0, 0), bf16))
        parts.append(dot(features, cut(mid_grad, core * HALF + y * QUARTER, QUARTER, 1), (0, 0), bf16))
    two = jnp.concatenate(parts, axis=1)
    return one + [two[D // 2 :], two[: D // 2]]


def narrow_side_sums(blocks, piece, core, head, head_far, start_sides, small):
    order = lambda v, width: jnp.concatenate([cut(v, b * width, width, 0) for b in blocks])
    heads = order(jnp.where(core == 0, *(jnp.concatenate(v) for v in ((head, head_far), (head_far, head)))), piece)
    count, seq = blocks.shape[0], head.shape[1]
    parts = []
    for side in range(2):
        start = start_sides[:, side * QUARTER : (side + 1) * QUARTER]
        parts.append(dot(heads, start, (1, 0), bf16))
        pos = order(start, seq // count).reshape(count, seq // count, 2, LANES)
        parts.append(jnp.transpose(pos, (0, 2, 1, 3)).reshape(-1, LANES))
    result = jnp.concatenate(parts, axis=1)
    return packed(result[D // 2 :], small), result[: D // 2]


def added(kept, arrived):
    return (kept.astype(f32) + arrived.astype(f32)).astype(bf16)


def local(
    pixels, cell_mask, lead_time, query, w_query, w_key, w_value, b_value, w_out, b_out, w_embed,
    var_embed, pos_embed, w_lead, b_lead, gain_one, shift_one, w_qkv, w_proj, b_proj, gain_two,
    shift_two, w_up, b_up, w_down, b_down, cotangent,
):
    groups = lax.axis_size("dp")
    stages = groups.bit_length() - 1
    me = lax.axis_index("dp")
    section = lax.axis_index("section")
    core, far = section % 2, section // 2
    seq = pixels.shape[0] // lead_time.shape[0]
    rows = seq // 2
    units = w_up.shape[1]
    quarter = units // 4
    piece = D // groups
    narrow = piece % LANES != 0
    blocks, second_blocks = (me ^ jnp.array(block_map(groups, way), jnp.int32) for way in range(2))
    scalars = jnp.concatenate([jnp.stack([core, far, me]), blocks, second_blocks]).astype(jnp.int32)
    row = lambda v: v.reshape(1, -1)
    pix, mask = jnp.transpose(pixels), jnp.transpose(cell_mask)
    lead = scalar(lead_time)
    half = groups // 2
    sizes = dict(piece=piece, groups=groups)
    held = lambda *shape: pltpu.VMEM(shape, bf16)
    wide = lambda *shape: pltpu.VMEM(shape, f32)
    kept_far = True

    start_part, per_head, coef, tv, table, probe = call(
        start_kernel,
        scalars,
        [
            remote(pix), remote(mask), row(query), remote(w_query), remote(w_key), remote(w_value), remote(row(b_value)),
            remote(w_out), remote(w_embed), remote(var_embed),
        ],
        [
            ((seq, D), bf16), ((HALF, seq), bf16, kept_far), ((PADDED, OWN_HEADS), f32), ((HALF, PADDED), bf16, kept_far),
            ((PADDED, D), bf16, kept_far), ((16, D), f32),
        ],
        scratch=[
            held(D, HALF), held(D, HALF), held(D, HALF), held(HALF, D), held(HALF, seq), held(HALF, PADDED), held(PADDED, D),
            held(CELLS, seq), pltpu.VMEM((CELLS, seq), jnp.int32), held(CELLS, D), held(VARS, D), wide(1, D),
        ],
        us=6,
    )
    far_probe = swap_core(probe)
    start_near, proj_part, start, normed_one, qkv, lse, attended = call(
        attend_kernel,
        scalars,
        [
            start_part, swap_core(start_part), pos_embed, lead, row(w_lead), row(b_lead), row(b_out), row(gain_one),
            row(shift_one), remote(w_qkv), remote(w_proj),
        ],
        [
            ((seq, D), bf16), ((seq, D), bf16), ((seq, D), bf16, kept_far), ((seq, D), bf16, kept_far),
            ((seq, 3 * HALF), bf16, kept_far), ((OWN_HEADS // 2, seq, LANES), f32, kept_far),
            ((seq, HALF), bf16, kept_far),
        ],
        scratch=[
            held(3, D, HALF), held(HALF, D), held(seq, D), held(seq, 3 * HALF), wide(OWN_HEADS // 2, seq, LANES),
            held(seq, HALF),
        ],
        us=12,
        after=[far_probe],
    )
    proj_came = swap_core(proj_part)
    normed_near, half_two, mid, normed_two = call(
        middle_kernel,
        scalars,
        [
            start_near, lead, row(w_lead), row(b_lead), row(b_proj), proj_part, proj_came, row(gain_two), row(shift_two),
        ],
        [((seq, D), bf16), ((rows, D), bf16), ((seq, D), bf16, kept_far), ((seq, D), bf16, kept_far)],
        scratch=[held(seq, D)],
        us=2.5,
    )
    other_two = swap_y(half_two)
    up_sums, normed_part, hidden, pre_grad = call(
        mlp_kernel,
        scalars,
        [normed_near, remote(cotangent), remote(w_up), row(b_up), remote(w_down)],
        [
            ((1, 2 * quarter), f32), ((seq, D), bf16), ((2, seq, quarter), bf16, kept_far),
            ((2, seq, quarter), bf16, kept_far),
        ],
        scratch=[
            held(2, seq, quarter), held(2, seq, quarter), held(2, D, quarter), held(2, quarter, D), held(seq, D),
        ],
        mb=22,
        us=11,
    )
    normed_came = swap_core(normed_part)
    by_block = lambda value: value.reshape(half, piece, value.shape[1])
    def halved(arrays, after):
        outs = [((v.shape[0] // 2,) + v.shape[1:], bf16) for v in arrays[::2] for _ in range(2)]
        return call(halves_kernel, scalars, arrays, outs, us=600, mb=16, after=after)


    attended_far, per_head_far = swap_core(attended), swap_core(per_head)
    other_held, _ = lax.optimization_barrier((other_two, normed_part))
    other_two_far = swap_core(other_held)
    if narrow:
        up_send, up_keep, down_send, down_keep = narrow_mlp_sums(
            blocks, second_blocks, piece, core, far, normed_two, other_two, other_two_far, cotangent, w_up, b_up, w_down, pre_grad, hidden
        )
    else:
        up_send, up_keep, down_send, down_keep = call(
            functools.partial(mlp_grads_kernel, **sizes),
            scalars,
            [remote(normed_two), other_two, other_two_far, remote(cotangent), remote(w_up)]
            + [row(b_up), remote(w_down), remote(pre_grad), remote(hidden)],
            [((D // 2, quarter), bf16, kept_far)] * 4,
            scratch=[
                held(2 * seq, D), held(2 * seq, D), held(D, quarter), held(quarter, D), held(2 * seq, quarter),
                held(2 * seq, quarter), held(2, D, quarter),
            ],
            us=15,
            mb=24,
            after=[normed_came, attended_far, per_head_far],
        )
    up_keep, down_keep = by_block(up_keep), by_block(down_keep)
    up_came = swap_stage(by_block(up_send), groups, 0)
    down_came = swap_stage(by_block(down_send), groups, 0, 1)

    class Sum:
        def __init__(self, keep, way, stage, sent=None, came=None):
            self.keep, self.way, self.stage = keep, way, stage
            self.came = swap_stage(sent, groups, stage, way) if came is None else came

    def onward(sums, after):
        results = halved([v for x in sums for v in (x.keep, x.came)], after)
        for n, x in enumerate(sums):
            x.keep, x.stage = results[2 * n], x.stage + 1
            x.came = swap_stage(results[2 * n + 1], groups, x.stage, x.way)
        return results[0]

    def last(sums, after):
        columns = sum(x.keep.shape[2] for x in sums)
        arrays = [v for x in sums for v in (x.keep, x.came)]
        return call(last_kernel, scalars, arrays, [((piece, columns), bf16)], us=600, after=after)[0]

    norm_part, mid_sums, qkv_keep, qkv_send, mid_grad = call(
        attend_back_kernel,
        scalars,
        [
            normed_part, normed_came, remote(mid), remote(cotangent), row(gain_two), remote(qkv), remote(attended),
            remote(lse), remote(w_proj), remote(w_qkv),
        ],
        [
            ((seq, D), bf16), ((8, D), f32), ((seq, 3 * QUARTER), bf16, kept_far), ((seq, 3 * QUARTER), bf16, kept_far),
            ((seq, D), bf16, kept_far),
        ],
        scratch=[
            held(seq, D), held(seq, D), held(seq, 3 * HALF), held(seq, HALF), wide(OWN_HEADS // 2, seq, LANES),
            held(3, D, HALF), held(HALF, D), held(seq, HALF), held(seq, 3 * HALF), held(seq, 3 * QUARTER),
            held(seq, 3 * QUARTER), held(seq, D),
        ],
        mb=22,
        us=14,
        after=[remote(up_send)],
    )
    norm_came = swap_core(norm_part)
    if narrow:
        one_send, one_keep, two_send, two_keep = narrow_head_sums(
            blocks, second_blocks, piece, core, far, normed_one, qkv_keep, qkv_send, attended, attended_far, mid_grad
        )
    else:
        one_send, one_keep, two_send, two_keep = call(
            functools.partial(head_grads_kernel, **sizes),
            scalars,
            [remote(x) for x in (normed_one, qkv_keep, qkv_send, attended, attended_far, mid_grad)],
            [((D, HALF), bf16, kept_far)] * 2 + [((D // 2, D), bf16, kept_far)] * 2,
            scratch=[
                held(seq, D), held(2, seq, 3 * QUARTER), held(2, seq, HALF), held(seq, HALF), held(2, D, HALF), held(D, D),
            ],
            us=4,
            after=[norm_part],
        )
    one_came = swap_y(one_send.reshape(groups, piece, HALF))
    two_came = swap_stage(by_block(two_send), groups, 0)

    outs = [((half // 2, piece, quarter), bf16)] * 4
    up_keep, up_send, down_keep, down_send = call(
        fetched_halves_kernel,
        scalars,
        [remote(up_keep), up_came, remote(down_keep), down_came],
        outs,
        scratch=[held(half, piece, quarter)] * 2,
        us=600,
        after=[remote(one_send)],
    )
    up, down = Sum(up_keep, 0, 1, up_send), Sum(down_keep, 1, 1, down_send)

    pix_kept, pix_sent, start_sides, small = call(
        start_back_kernel,
        scalars,
        [
            norm_part, norm_came, remote(start), lead, row(w_lead), row(b_lead), row(gain_one), remote(mid_grad),
            remote(w_out), remote(pix), remote(mask), coef, remote(tv), mid_sums, up_sums,
        ],
        [
            ((CELLS, rows), f32), ((CELLS, rows), bf16), ((seq, HALF), bf16, kept_far), ((SMALL_ROWS, D), bf16),
        ],
        scratch=[
            wide(CELLS, seq), held(HALF, D), held(seq, D), held(seq, D), held(HALF, PADDED), held(seq, D),
            held(seq, HALF), held(CELLS, seq), pltpu.VMEM((CELLS, seq), jnp.int32),
        ],
        us=7,
        after=[up.keep],
    )

    if narrow:
        side_sent, side_keep = narrow_side_sums(blocks, piece, core, per_head, per_head_far, start_sides, small)
    else:
        side_sent, side_keep = call(
            functools.partial(side_grads_kernel, **sizes),
            scalars,
            [remote(x) for x in (per_head, per_head_far, start_sides)] + [small],
            [((2 * (QUARTER + LANES + SMALL_ROWS), HALF), bf16), ((HALF, 2 * (QUARTER + LANES)), bf16)],
            scratch=[held(2, HALF, seq), held(seq, HALF), wide(seq, HALF)],
            us=4,
            after=[small],
        )
    side_came = swap_stage(side_sent, groups, 0)
    out_sent, out_kept = call(
        out_kernel,
        scalars,
        [remote(hidden), remote(w_down), remote(mid), row(b_down)],
        [((rows, D), bf16), ((rows, D), f32)],
        scratch=[wide(seq, D), held(2, seq, quarter), held(2, quarter, D), held(rows, D)],
        us=4,
        after=[side_keep],
    )


    def summed(kept, arrived, after=()):
        return call(sum_kernel, scalars, [kept, arrived], [(kept.shape, bf16)], us=600, mb=16, after=after)[0]

    head_rows = ((half, piece, HALF), bf16)
    one_keep, one_send, two_keep, two_send = call(
        heads_kernel,
        scalars,
        [one_keep.reshape(groups, piece, HALF), one_came, by_block(two_keep), two_came],
        [head_rows] * 4,
        us=600,
        mb=16,
        after=[out_sent],
    )
    two_came = swap_y(two_send)
    stages = groups.bit_length() - 1

    one = Sum(one_keep, 1, 0, one_send)
    two = Sum(two_keep, 0, 0, came=two_came)
    after = one_keep
    for _ in range(stages - 2):
        after = onward([up, down], [after])

    def side_step(side, small, came, after):
        rows, columns = side.shape
        if columns > QUARTER + LANES:
            columns //= 2
            outs = [((rows, columns), bf16), (small.shape, bf16), ((columns + SMALL_ROWS * D // rows, rows), bf16)]
        elif rows == piece:
            outs = [(side.shape, bf16), (small.shape, bf16)]
        else:
            outs = [((rows // 2, columns), bf16), (small.shape, bf16)]
            outs.append(((columns + SMALL_ROWS * D * 2 // rows, rows // 2), bf16))
        if narrow and rows <= LANES:
            arrived = (unpacked if rows == LANES else unpacked_narrow)(came, columns)
            side, small = added(side, arrived[0]), added(small, arrived[1])
            if rows == piece:
                return side, small
            return side[: rows // 2], small, packed_narrow(side[rows // 2 :], small)
        return call(side_step_kernel, scalars, [side, small, came], outs, us=600, mb=16, after=after)

    side_keep, small, side_send = side_step(side_keep, small, side_came, [after])
    side_came = swap_y(side_send)
    after = onward([one, two], [side_keep])
    mlp_piece = last([up, down], [after])
    mlp_y, mlp_core = swap_y(mlp_piece), swap_core(mlp_piece)
    after = mlp_piece
    for stage in range(1, stages):
        side_keep, small, side_send = side_step(side_keep, small, side_came, [after])
        side_came = swap_stage(side_send, groups, stage)
        after = onward([one, two], [side_keep]) if stage < stages - 1 else side_keep
    side_keep, small = side_step(side_keep, small, side_came, [after])
    other_small = swap_core(small)
    attend_piece = jnp.concatenate([last([one, two], [small]), side_keep], axis=1) if narrow else call(
        last_kernel,
        scalars,
        [one.keep, one.came, two.keep, two.came, side_keep],
        [((piece, D + QUARTER + LANES), bf16)],
        us=600,
        after=[small],
    )[0]
    attend_y, attend_core = swap_y(attend_piece), swap_core(attend_piece)
    out_late, pix_late, _ = lax.optimization_barrier((out_sent, pix_sent, attend_piece))
    block_out = (out_kept + swap_core(out_late).astype(f32)).astype(bf16)
    pixels_grad = jnp.transpose(pix_kept + swap_core(pix_late).astype(f32))

    probes = jnp.concatenate([jnp.where(core == c, probe, far_probe)[:OWN_HEADS] for c in range(2)])
    probes, table_late, query_late, _ = lax.optimization_barrier((probes, table, query, mlp_piece))
    my_probe = cut(probes, me * piece, piece, 1)
    my_table = cut(table_late, me * piece, piece, 1)
    my_query = row(cut(query_late, me * piece, piece, 0))
    embed_grad, var_grad, w_value_grad, w_key_grad, w_query_grad, query_rows, bias_rows = call(
        functools.partial(small_kernel, piece=piece),
        scalars,
        [
            small, other_small, remote(table), probe, far_probe, remote(w_value), remote(w_key), row(query),
            remote(w_query), my_table, my_probe, my_query,
        ],
        [
            ((CELLS, piece), f32), ((VARS, piece), f32), ((piece, D), f32), ((piece, D), f32), ((piece, D), f32),
            ((8, piece), f32), ((8, D), f32),
        ],
        scratch=[held(PADDED, D), held(piece, D), held(D, D), held(piece, D)],
        us=600,
        after=[attend_piece],
    )
    query_grad = query_rows[0]
    my_value_bias = cut(bias_rows, me * piece, piece, 1)[0]
    shared = jnp.where(core == 0, small, other_small)[136:145].astype(f32)
    shared = cut(shared, me * piece, piece, 1)
    gain_two_grad, shift_two_grad, b_proj_grad, b_down_grad, gain_one_grad = (shared[n] for n in range(5))
    shift_one_grad, b_lead_grad, w_lead_grad, b_out_grad = (shared[n] for n in range(5, 9))
    up_rows = [jnp.where(core == c, small, other_small)[145:147] for c in range(2)]
    up_bias_grad = jnp.concatenate(up_rows).reshape(-1).astype(f32)
    my_up_bias = cut(up_bias_grad, me * (units // groups), units // groups, 0)

    w_up_grad, w_down_grad = call(
        mlp_final_kernel,
        scalars,
        [mlp_piece, mlp_y, mlp_core, swap_core(mlp_y)],
        [((piece, units), f32), ((units, piece), f32)],
        us=300,
        after=[embed_grad],
    )
    w_qkv_grad, w_proj_grad, w_out_grad, pos_grad = call(
        attend_final_kernel,
        scalars,
        [attend_piece, attend_y, attend_core, swap_core(attend_y)],
        [((piece, 3 * D), f32), ((piece, D), f32), ((piece, D), f32), ((seq // groups, D), f32)],
        after=[w_up_grad],
    )
    return (
        block_out, pixels_grad, query_grad, w_query_grad, w_key_grad, w_value_grad, my_value_bias, w_out_grad, b_out_grad,
        embed_grad, var_grad, pos_grad, w_lead_grad, b_lead_grad, gain_one_grad, shift_one_grad, w_qkv_grad, w_proj_grad,
        b_proj_grad, gain_two_grad, shift_two_grad, w_up_grad, my_up_bias, w_down_grad, b_down_grad,
    )


def solution(mesh):
    whole = P()
    args = (P("dp", None), P("dp", None), P("dp")) + (whole,) * 23 + (P("dp", None),)
    outs = (
        (P(axes, None),) * 2
        + (P("dp"),)
        + (P("dp", None),) * 3
        + (P("dp"), P("dp", None), P("dp"), P(None, "dp"), P(None, "dp"), P("dp", None))
        + (P("dp"),) * 4
        + (P("dp", None),) * 2
        + (P("dp"),) * 3
        + (P("dp", None), P("dp"), P(None, "dp"), P("dp"))
    )
    return jax.shard_map(local, mesh=mesh, in_specs=args, out_specs=outs, check_vma=False)
```

```python
import functools

import jax
import jax.numpy as jnp
from jax import lax
from jax.experimental import pallas as pl
from jax.experimental.pallas import tpu as pltpu
from jax.sharding import PartitionSpec as P

D = 1024
HEADS = 16
HD = 64
VARS = 48
PIX = 4
CELLS = VARS * PIX
ROWS = CELLS + VARS
PADDED = 256
OWN_HEADS = HEADS // 2
HALF = D // 2
QUARTER = D // 4
LANES = 128
SMALL_ROWS = 160

highest = lax.Precision.HIGHEST
epsilon = 1e-05
bf16 = jnp.bfloat16
f32 = jnp.float32
axes = ("dp", "section")


def dot(a, b, contract, kind=f32, precision=None):
    return lax.dot_general(
        a, b, ((contract[:1], contract[1:]), ((), ())), precision=precision, preferred_element_type=kind
    )


def call(body, scalars, ins, outs, scratch=(), us=2, mb=16, after=()):
    del scalars
    arrays, in_specs = [], []
    for item in list(ins) + [x if isinstance(x, tuple) else (x, pl.ANY) for x in after]:
        array, space = item if isinstance(item, tuple) else (item, pltpu.VMEM)
        in_specs.append(pl.BlockSpec(memory_space=space))
        arrays.append(array)
    count = len(ins)

    def placed(*refs):
        body(Place(), *refs[:count], *refs[count + len(after) :])

    return pl.pallas_call(
        placed,
        in_specs=in_specs,
        out_specs=[pl.BlockSpec(memory_space=pltpu.HBM if len(item) > 2 else pltpu.VMEM) for item in outs],
        out_shape=[
            pltpu.HBM(*item[:2]) if len(item) > 2 else jax.ShapeDtypeStruct(*item) for item in outs
        ],
        scratch_shapes=list(scratch) + [pltpu.SemaphoreType.DMA((24,))],
        compiler_params=pltpu.CompilerParams(vmem_limit_bytes=mb << 20),
        cost_estimate=pl.CostEstimate(flops=int(us * 1e7), bytes_accessed=1 << 12, transcendentals=0),
    )(*arrays)


class Place:
    def __getitem__(self, n):
        if n < 2:
            section = lax.axis_index("section")
            return section & 1 if n == 0 else section >> 1
        me = lax.axis_index("dp")
        if n == 2:
            return me
        groups = lax.axis_size("dp")
        return me ^ block_map(groups, (n - 3) // groups)[(n - 3) % groups]


def remote(array):
    return pltpu.with_memory_space_constraint(array, pltpu.HBM), pltpu.HBM


def scalar(array):
    return array, pltpu.SMEM


class Moves:
    def __init__(self, sems):
        self.sems, self.count = sems, 0

    def start(self, source, place):
        copy = pltpu.make_async_copy(source, place, self.sems.at[self.count])
        self.count += 1
        copy.start()
        return copy


def wait(*copies):
    for copy in copies:
        copy.wait()


def part_of(start, size):
    return pl.ds(pl.multiple_of(start * size, size), size)


def cell_order():
    row = lax.broadcasted_iota(jnp.int32, (CELLS, CELLS), 0)
    column = lax.broadcasted_iota(jnp.int32, (CELLS, CELLS), 1)
    cell = sum((row >= n * VARS).astype(jnp.int32) for n in range(1, PIX))
    return ((row - cell * VARS) * PIX + cell == column).astype(f32).astype(bf16)


def in_three(value):
    high = value.astype(bf16).astype(f32)
    middle = (value - high).astype(bf16).astype(f32)
    return jnp.concatenate([high, middle, value - high - middle], axis=0).astype(bf16)


def summed_rows(value, rows):
    return value[:rows] + value[rows : 2 * rows] + value[2 * rows :]


def head_weights(cells, pen, coef, h):
    scores = pen + coef[CELLS:ROWS, h : h + 1]
    for j in range(PIX):
        rows = slice(j * VARS, (j + 1) * VARS)
        scores = scores + cells[rows] * coef[rows, h : h + 1]
    raised = jnp.exp(scores - jnp.max(scores, axis=0, keepdims=True))
    return raised / jnp.sum(raised, axis=0, keepdims=True)


def head_features(cells, weight):
    parts = [weight * cells[j * VARS : (j + 1) * VARS] for j in range(PIX)]
    parts = parts + [weight, jnp.ones((PADDED - ROWS, weight.shape[1]), f32)]
    return jnp.concatenate(parts, axis=0).astype(bf16)


def load_cells(pix_ref, mask_ref, perm):
    mask = mask_ref[...].astype(f32).astype(bf16)
    masked = pix_ref[...] * mask
    cells = dot(perm, masked, (1, 0))
    seen = dot(perm, mask, (1, 0))
    present = seen[:VARS]
    for j in range(1, PIX):
        present = jnp.maximum(present, seen[j * VARS : (j + 1) * VARS])
    return cells, seen, (present - 1.0) * 10000.0


def start_kernel(
    s, pix_hbm, mask_hbm, query_ref, w_query_hbm, w_key_hbm, w_value_hbm, b_value_hbm, w_out_hbm, embed_hbm, var_hbm,
    part_ref, per_head_hbm, coef_ref, tv_hbm, table_hbm, probe_ref,
    w_query_ref, w_key_ref, w_value_ref, w_out_ref, per_head_ref, tv_ref, table_ref, pix_ref, mask_ref, embed_ref, var_ref,
    b_value_ref, sems,
):
    half = part_of(s[0], HALF)
    seq = part_ref.shape[0]
    moves = Moves(sems)
    sample = part_of(s[1], seq)
    tables = [moves.start(embed_hbm, embed_ref), moves.start(var_hbm, var_ref)]
    pixels = [
        moves.start(pix_hbm.at[:, sample], pix_ref), moves.start(mask_hbm.at[:, sample], mask_ref),
        moves.start(b_value_hbm, b_value_ref),
    ]
    copies = [
        moves.start(w_query_hbm.at[:, half], w_query_ref),
        moves.start(w_key_hbm.at[:, half], w_key_ref),
        moves.start(w_value_hbm.at[:, half], w_value_ref),
        moves.start(w_out_hbm.at[half, :], w_out_ref),
    ]
    perm = cell_order()
    wait(*tables)
    table = jnp.concatenate(
        [
            dot(perm, embed_ref[...], (1, 0)),
            var_ref[...].astype(f32),
            jnp.zeros((PADDED - ROWS, D), f32),
        ]
    ).astype(bf16)
    table_ref[...] = table
    saved = [moves.start(table_ref, table_hbm)]
    wait(*pixels)
    cells, _, pen = load_cells(pix_ref, mask_ref, perm)
    wait(*copies[:3])
    asked = dot(query_ref[...], w_query_ref[...], (1, 0))
    row = lax.broadcasted_iota(jnp.int32, (OWN_HEADS, HALF), 0)
    lane = lax.broadcasted_iota(jnp.int32, (OWN_HEADS, HALF), 1)
    by_head = jnp.where((lane >= row * HD) & (lane < (row + 1) * HD), asked, 0.0)
    probe = summed_rows(dot(in_three(by_head), w_key_ref[...], (1, 1)), OWN_HEADS)
    asked_row = jnp.concatenate([jnp.broadcast_to(asked, (8, HALF)), jnp.zeros((8, HALF), f32)], axis=1)
    probe_ref[...] = jnp.concatenate([probe, asked_row], axis=0)
    coef3 = dot(table, in_three(probe), (1, 1)) * 0.125
    coef = coef3[:, :OWN_HEADS] + coef3[:, OWN_HEADS : 2 * OWN_HEADS] + coef3[:, 2 * OWN_HEADS :]
    coef_ref[...] = coef
    tv = jnp.transpose(dot(table, w_value_ref[...], (1, 0))).astype(bf16)
    lane = lax.broadcasted_iota(jnp.int32, tv.shape, 1)
    tv = jnp.where(lane < ROWS, tv, jnp.zeros_like(tv))
    tv_ref[...] = tv
    saved.append(moves.start(tv_ref, tv_hbm))
    bias = b_value_ref[:, half]
    for h in range(OWN_HEADS):
        rows = slice(h * HD, (h + 1) * HD)
        features = head_features(cells, head_weights(cells, pen, coef, h))
        column = jnp.transpose(jnp.broadcast_to(bias[:, rows], (8, HD)))[:, :1]
        per_head_ref[rows, :] = (dot(tv[rows], features, (1, 0)) + column).astype(bf16)
    saved.append(moves.start(per_head_ref, per_head_hbm))
    wait(copies[3])
    part_ref[...] = dot(per_head_ref[...], w_out_ref[...], (0, 0)).astype(bf16)
    wait(*saved)


def norm_parts(value):
    average = jnp.mean(value, axis=-1, keepdims=True)
    centered = value - average
    scale = lax.rsqrt(jnp.mean(centered * centered, axis=-1, keepdims=True) + epsilon)
    return centered * scale, scale


def norm_back(normal, scale, gain, grad):
    inner = grad * gain
    return scale * (
        inner
        - jnp.mean(inner, axis=-1, keepdims=True)
        - normal * jnp.mean(inner * normal, axis=-1, keepdims=True)
    )


def gelu_both(x):
    k = 0.7978845608028654
    square = x * x
    t = jnp.tanh(x * (k + k * 0.044715 * square))
    gate = 0.5 + 0.5 * t
    slope = gate + (0.5 * x) * (1.0 - t * t) * (k + 3 * k * 0.044715 * square)
    return x * gate, slope


def total(first_ref, second_ref):
    return first_ref[...].astype(f32) + second_ref[...].astype(f32)


def column_sums(value):
    return jnp.sum(value, axis=0, keepdims=True)


def only_half(block, half):
    lane = lax.broadcasted_iota(jnp.int32, block.shape, 1)
    return jnp.where((lane >= HD) if half else (lane < HD), block, jnp.zeros_like(block))


def joined(low, high):
    lane = lax.broadcasted_iota(jnp.int32, low.shape, 1)
    return jnp.where(lane < HD, low, high)


def pair_columns(pair, part=0):
    return pl.ds(pl.multiple_of(part * HALF + pair * LANES, LANES), LANES)


def fetch_heads(moves, s, w_qkv_hbm, w_ref):
    return [moves.start(w_qkv_hbm.at[:, part_of(2 * n + s[0], HALF)], w_ref.at[n]) for n in range(3)]


def attend_kernel(
    s, own_ref, came_ref, pos_ref, lead_ref, w_lead_ref, b_lead_ref, b_out_ref, gain_ref, shift_ref, w_qkv_hbm,
    w_proj_hbm,
    start_ref, part_ref, start_hbm, normed_hbm, qkv_hbm, lse_hbm, out_hbm,
    w_ref, w_proj_ref, normed_ref, qkv_ref, lse_ref, out_ref, sems,
):
    moves = Moves(sems)
    copies = fetch_heads(moves, s, w_qkv_hbm, w_ref)
    proj_copy = moves.start(w_proj_hbm.at[part_of(s[0], HALF), :], w_proj_ref)
    start = (total(own_ref, came_ref) + b_out_ref[...] + pos_ref[...].astype(f32)).astype(bf16)
    start_ref[...] = start
    saved = [moves.start(start_ref, start_hbm)]
    stream = start.astype(f32) + lead_ref[s[1]] * w_lead_ref[...] + b_lead_ref[...]
    normal, _ = norm_parts(stream)
    normed = (normal * gain_ref[...] + shift_ref[...]).astype(bf16)
    normed_ref[...] = normed
    saved.append(moves.start(normed_ref, normed_hbm))
    wait(*copies)
    for n in range(3):
        qkv_ref[:, n * HALF : (n + 1) * HALF] = dot(normed, w_ref[n], (1, 0)).astype(bf16)
    saved.append(moves.start(qkv_ref, qkv_hbm))

    def one_pair(pair, carried):
        q, k, v = (qkv_ref[:, pair_columns(pair, part)] for part in range(3))
        lane = lax.broadcasted_iota(jnp.int32, v.shape, 1)
        outs, weights, norms = [], [], []
        for half in range(2):
            mine = (lane >= HD) if half else (lane < HD)
            logits = dot(only_half(q * jnp.asarray(0.125, bf16), half), k, (1, 1))
            top = jnp.max(logits, axis=1, keepdims=True)
            raised = jnp.exp(logits - top).astype(bf16)
            both = dot(raised, jnp.where(mine, v, jnp.ones_like(v)), (1, 0))
            outs.append(both)
            weights.append(pltpu.roll(both, HD, 1))
            norms.append(jnp.broadcast_to(top, both.shape))
        weight = joined(*weights)
        out_ref[:, pair_columns(pair)] = (joined(*outs) / weight).astype(bf16)
        lse_ref[pair] = joined(*norms) + jnp.log(weight)
        return carried

    lax.fori_loop(0, OWN_HEADS // 2, one_pair, 0, unroll=2)
    saved.append(moves.start(lse_ref, lse_hbm))
    saved.append(moves.start(out_ref, out_hbm))
    wait(proj_copy)
    part_ref[...] = dot(out_ref[...], w_proj_ref[...], (1, 0)).astype(bf16)
    wait(*saved)


def middle_kernel(
    s, start_ref, lead_ref, w_lead_ref, b_lead_ref, b_proj_ref, own_ref, came_ref, gain_ref, shift_ref,
    normed_ref, half_ref, mid_hbm, normed_hbm, mid_ref, sems,
):
    moves = Moves(sems)
    stream = start_ref[...].astype(f32) + lead_ref[s[1]] * w_lead_ref[...] + b_lead_ref[...]
    mid = (stream + b_proj_ref[...] + total(own_ref, came_ref)).astype(bf16)
    mid_ref[...] = mid
    saved = [moves.start(mid_ref, mid_hbm)]
    normal, _ = norm_parts(mid.astype(f32))
    normed_ref[...] = (normal * gain_ref[...] + shift_ref[...]).astype(bf16)
    saved.append(moves.start(normed_ref, normed_hbm))
    half_ref[...] = normed_ref[part_of(s[0], half_ref.shape[0]), :]
    wait(*saved)


def mlp_kernel(
    s, normed_ref, cot_hbm, w_up_hbm, b_up_ref, w_down_hbm, sums_ref, part_ref, hidden_hbm, pre_grad_hbm,
    hidden_ref, pre_grad_ref, w_up_ref, w_down_ref, cot_ref, sems,
):
    width = w_up_ref.shape[2]
    moves = Moves(sems)
    ups, downs, saved = [], [], []
    for n in range(2):
        place = part_of(2 * s[0] + n, width)
        ups.append(moves.start(w_up_hbm.at[:, place], w_up_ref.at[n]))
        if n == 0:
            cot_copy = moves.start(cot_hbm.at[part_of(s[1], cot_ref.shape[0]), :], cot_ref)
        downs.append(moves.start(w_down_hbm.at[place, :], w_down_ref.at[n]))
    wait(cot_copy)
    back = None
    for n in range(2):
        columns = slice(n * width, (n + 1) * width)
        wait(ups[n], downs[n])
        pre = dot(normed_ref[...], w_up_ref[n], (1, 0)) + b_up_ref[:, part_of(2 * s[0] + n, width)]
        hidden_grad = dot(cot_ref[...], w_down_ref[n], (1, 1))
        hidden, slope = gelu_both(pre)
        hidden_ref[n] = hidden.astype(bf16)
        pre_grad = hidden_grad * slope
        sums_ref[:, columns] = column_sums(pre_grad)
        low = pre_grad.astype(bf16)
        pre_grad_ref[n] = low
        term = dot(low, w_up_ref[n], (1, 1))
        back = term if back is None else back + term
        saved.append(moves.start(hidden_ref.at[n], hidden_hbm.at[n]))
        saved.append(moves.start(pre_grad_ref.at[n], pre_grad_hbm.at[n]))
    part_ref[...] = back.astype(bf16)
    wait(*saved)


def out_kernel(
    s, hidden_hbm, w_down_hbm, mid_hbm, b_down_ref, sent_ref, kept_ref, total_ref, hidden_ref, w_down_ref, mid_ref, sems
):
    width = w_down_ref.shape[1]
    rows = sent_ref.shape[0]
    moves = Moves(sems)
    copies = []
    for n in range(2):
        copies.append(moves.start(hidden_hbm.at[n], hidden_ref.at[n]))
        copies.append(moves.start(w_down_hbm.at[part_of(2 * s[0] + n, width), :], w_down_ref.at[n]))
    mid_copy = moves.start(mid_hbm.at[part_of(s[0], rows), :], mid_ref)
    wait(*copies[:2])
    result = dot(hidden_ref[0], w_down_ref[0], (1, 0))
    wait(*copies[2:])
    total_ref[...] = result + dot(hidden_ref[1], w_down_ref[1], (1, 0))
    wait(mid_copy)
    sent_ref[...] = total_ref[part_of(1 - s[0], rows), :].astype(bf16)
    kept_ref[...] = total_ref[part_of(s[0], rows), :] + mid_ref[...].astype(f32) + b_down_ref[...]


def attend_back_kernel(
    s, own_ref, came_ref, mid_hbm, cot_hbm, gain_ref, qkv_hbm, out_hbm, lse_hbm, w_proj_hbm, w_qkv_hbm,
    part_ref, sums_ref, keep_hbm, send_hbm, mid_grad_hbm,
    mid_ref, cot_ref, qkv_ref, out_ref, lse_ref, w_ref, w_proj_ref, grad_ref, back_ref, keep_ref, send_ref, mid_grad_ref,
    sems,
):
    seq = own_ref.shape[0]
    moves = Moves(sems)
    first = [moves.start(mid_hbm, mid_ref), moves.start(cot_hbm.at[part_of(s[1], seq), :], cot_ref)]
    proj_copy = moves.start(w_proj_hbm.at[part_of(s[0], HALF), :], w_proj_ref)
    copies = [
        moves.start(qkv_hbm, qkv_ref), moves.start(out_hbm, out_ref), moves.start(lse_hbm, lse_ref)
    ]
    heads = fetch_heads(moves, s, w_qkv_hbm, w_ref)
    grad = total(own_ref, came_ref)
    wait(*first)
    cot = cot_ref[...].astype(f32)
    normal, scale = norm_parts(mid_ref[...].astype(f32))
    mid_grad = cot + norm_back(normal, scale, gain_ref[...], grad)
    sums_ref[...] = jnp.concatenate(
        [column_sums(grad * normal), column_sums(grad), column_sums(mid_grad), column_sums(cot), jnp.zeros((4, D), f32)]
    )
    low = mid_grad.astype(bf16)
    mid_grad_ref[...] = low
    saved = [moves.start(mid_grad_ref, mid_grad_hbm)]
    wait(proj_copy, *copies)
    grad_ref[...] = dot(low, w_proj_ref[...], (1, 1)).astype(bf16)

    def one_pair(pair, carried):
        q, k, v = (qkv_ref[:, pair_columns(pair, part)] for part in range(3))
        out_grad = grad_ref[:, pair_columns(pair)]
        weighted = out_grad.astype(f32) * out_ref[:, pair_columns(pair)].astype(f32)
        norms = lse_ref[pair]
        results = []
        for half in range(2):
            logits = dot(only_half(q * jnp.asarray(0.125, bf16), half), k, (1, 1))
            probs = jnp.exp(logits - norms[:, half * HD : half * HD + 1])
            probs_grad = dot(only_half(out_grad, half), v, (1, 1))
            shift = jnp.sum(only_half(weighted, half), axis=1, keepdims=True)
            logits_grad = (probs * (probs_grad - shift)).astype(bf16)
            results.append(
                (
                    dot(logits_grad, k, (1, 0)) * 0.125,
                    dot(logits_grad, q, (0, 0)) * 0.125,
                    dot(probs.astype(bf16), out_grad, (0, 0)),
                )
            )
        for part, (low_head, high_head) in enumerate(zip(*results)):
            back_ref[:, pair_columns(pair, part)] = joined(low_head, high_head).astype(bf16)
        return carried

    lax.fori_loop(0, OWN_HEADS // 2, one_pair, 0)
    for part in range(3):
        columns = slice(part * QUARTER, (part + 1) * QUARTER)
        mine = pl.multiple_of(part * HALF + s[1] * QUARTER, LANES)
        theirs = pl.multiple_of(part * HALF + (1 - s[1]) * QUARTER, LANES)
        keep_ref[:, columns] = back_ref[:, pl.ds(mine, QUARTER)]
        send_ref[:, columns] = back_ref[:, pl.ds(theirs, QUARTER)]
    saved += [moves.start(keep_ref, keep_hbm), moves.start(send_ref, send_hbm)]
    wait(*heads)
    back = None
    for n in range(3):
        term = dot(back_ref[:, n * HALF : (n + 1) * HALF], w_ref[n], (1, 1))
        back = term if back is None else back + term
    part_ref[...] = back.astype(bf16)
    wait(*saved)


def start_back_kernel(
    s, own_ref, came_ref, start_hbm, lead_ref, w_lead_ref, b_lead_ref, gain_ref, mid_grad_hbm, w_out_hbm, pix_hbm,
    mask_hbm, coef_ref, tv_hbm, sums_ref, up_sums_ref,
    pix_keep_ref, pix_send_ref, side_hbm, small_ref,
    held_ref, w_out_ref, start_ref, mid_grad_ref, tv_ref, start_grad_ref, side_ref, pix_ref, mask_ref, sems,
):
    moves = Moves(sems)
    first = [moves.start(start_hbm, start_ref), moves.start(mid_grad_hbm, mid_grad_ref)]
    seq = own_ref.shape[0]
    sample = part_of(s[1], seq)
    copies = [
        moves.start(w_out_hbm.at[part_of(s[0], HALF), :], w_out_ref), moves.start(tv_hbm, tv_ref),
        moves.start(pix_hbm.at[:, sample], pix_ref), moves.start(mask_hbm.at[:, sample], mask_ref),
    ]
    grad = total(own_ref, came_ref)
    lead = lead_ref[s[1]]
    wait(*first)
    stream = start_ref[...].astype(f32) + lead * w_lead_ref[...] + b_lead_ref[...]
    normal, scale = norm_parts(stream)
    stream_grad = mid_grad_ref[...].astype(f32) + norm_back(normal, scale, gain_ref[...], grad)
    start_grad = stream_grad.astype(bf16)
    start_grad_ref[...] = start_grad
    for side in range(2):
        side_ref[:, side * QUARTER : (side + 1) * QUARTER] = start_grad_ref[:, quarter_columns(s, side)]
    saved = [moves.start(side_ref, side_hbm)]
    lead_sum = column_sums(stream_grad)
    vectors = [
        sums_ref[0:4, :],
        column_sums(grad * normal),
        column_sums(grad),
        lead_sum,
        lead * lead_sum,
        column_sums(start_grad.astype(f32)),
        up_sums_ref[:, :D],
        up_sums_ref[:, D:],
        jnp.zeros((SMALL_ROWS - 136 - 11, D), f32),
    ]
    wait(*copies)
    per_head_grad = dot(w_out_ref[...], start_grad, (1, 1)).astype(bf16)

    cells, seen, pen = load_cells(pix_ref, mask_ref, cell_order())
    coef = coef_ref[...]
    tv = tv_ref[...]
    lane = lax.broadcasted_iota(jnp.int32, (PADDED, LANES), 1)
    coef_grad = jnp.zeros((PADDED, LANES), f32)
    cell_grad = [jnp.zeros((VARS, cells.shape[1]), f32) for _ in range(PIX)]
    for h in range(OWN_HEADS):
        rows = slice(h * HD, (h + 1) * HD)
        weight = head_weights(cells, pen, coef, h)
        features = head_features(cells, weight)
        head_grad = per_head_grad[rows]
        small_rows = slice((h % 2) * HD, (h % 2 + 1) * HD)
        small_ref[small_rows, (h // 2) * PADDED : (h // 2 + 1) * PADDED] = dot(head_grad, features, (1, 1)).astype(bf16)
        feature_grad = dot(tv[rows], head_grad, (0, 0))
        weight_grad = feature_grad[CELLS:ROWS]
        for j in range(PIX):
            part = slice(j * VARS, (j + 1) * VARS)
            weight_grad = weight_grad + feature_grad[part] * cells[part]
        score_grad = weight * (weight_grad - jnp.sum(weight * weight_grad, axis=0, keepdims=True))
        sums = []
        for j in range(PIX):
            part = slice(j * VARS, (j + 1) * VARS)
            cell_grad[j] = cell_grad[j] + feature_grad[part] * weight + score_grad * coef[part, h : h + 1]
            sums.append(jnp.sum(score_grad * cells[part], axis=1, keepdims=True))
        sums.append(jnp.sum(score_grad, axis=1, keepdims=True))
        sums.append(jnp.zeros((PADDED - ROWS, 1), f32))
        coef_grad = jnp.where(lane == h, jnp.concatenate(sums, axis=0), coef_grad)
    coef_rows = jnp.transpose(coef_grad)[:OWN_HEADS]
    coef_rows = jnp.concatenate([coef_rows, jnp.zeros((OWN_HEADS, D - PADDED), f32)], axis=1)
    small_ref[LANES:, :] = jnp.concatenate([coef_rows] + vectors, axis=0).astype(bf16)
    cell_grads = (jnp.concatenate(cell_grad, axis=0) * seen).astype(bf16)
    held_ref[...] = dot(cell_order(), cell_grads, (0, 0))
    columns = pix_keep_ref.shape[1]
    pix_keep_ref[...] = held_ref[:, part_of(s[0], columns)]
    pix_send_ref[...] = held_ref[:, part_of(1 - s[0], columns)].astype(bf16)
    wait(*saved)


def quarter_columns(s, side):
    far = s[1] if side == 0 else 1 - s[1]
    return pl.ds(pl.multiple_of(s[0] * HALF + far * QUARTER, QUARTER), QUARTER)


def mlp_grads_kernel(
    s, normed_hbm, first_hbm, second_hbm, cot_hbm, w_up_hbm, b_up_ref, w_down_hbm, pre_grad_hbm, hidden_hbm,
    up_send_hbm, up_keep_hbm, down_send_hbm, down_keep_hbm,
    normed_ref, cot_ref, w_up_ref, w_down_ref, pre_grad_ref, hidden_ref, sum_ref, sems, *, piece, groups,
):
    width = w_up_ref.shape[1]
    rows = first_hbm.shape[0]
    seq = 2 * rows
    place = part_of(2 * s[0] + s[1], width)
    moves = Moves(sems)
    own, one, two = pl.ds(0, seq), pl.ds(seq, rows), pl.ds(seq + rows, rows)
    first = [
        moves.start(w_up_hbm.at[:, place], w_up_ref),
        moves.start(first_hbm, normed_ref.at[one, :]),
        moves.start(second_hbm, normed_ref.at[two, :]),
        moves.start(cot_hbm.at[part_of((1 - s[1]) * 2 + s[0], rows), :], cot_ref.at[one, :]),
        moves.start(cot_hbm.at[part_of((1 - s[1]) * 2 + (1 - s[0]), rows), :], cot_ref.at[two, :]),
        moves.start(w_down_hbm.at[place, :], w_down_ref),
    ]
    then = [
        moves.start(cot_hbm.at[part_of(s[1], seq), :], cot_ref.at[own, :]),
        moves.start(normed_hbm, normed_ref.at[own, :]),
        moves.start(hidden_hbm.at[s[1]], hidden_ref.at[own, :]),
        moves.start(pre_grad_hbm.at[s[1]], pre_grad_ref.at[own, :]),
    ]
    wait(*first)
    pre = dot(normed_ref[seq:, :], w_up_ref[...], (1, 0)) + b_up_ref[:, place]
    hidden_grad = dot(cot_ref[seq:, :], w_down_ref[...], (1, 1))
    hidden, slope = gelu_both(pre)
    hidden_ref[seq:, :] = hidden.astype(bf16)
    pre_grad_ref[seq:, :] = (hidden_grad * slope).astype(bf16)
    wait(*then)
    half = groups // 2 * piece
    outs = ((up_send_hbm, up_keep_hbm), (down_send_hbm, down_keep_hbm))
    saved = []
    for n, (left_ref, right_ref) in enumerate(((normed_ref, pre_grad_ref), (cot_ref, hidden_ref))):
        left = chosen(left_ref, [s[3 + n * groups + b] for b in range(groups)], piece)
        sum_ref[n] = dot(left, right_ref[...], (0, 0)).astype(bf16)
        send_hbm, keep_hbm = outs[n]
        saved.append(moves.start(sum_ref.at[n, half:, :], send_hbm))
        saved.append(moves.start(sum_ref.at[n, :half, :], keep_hbm))
    wait(*saved)


def chosen(ref, blocks, piece):
    return jnp.concatenate([ref[:, part_of(b, piece)] for b in blocks], axis=1)


def head_grads_kernel(
    s, normed_hbm, keep_hbm, send_hbm, attended_hbm, attended_far_hbm, mid_grad_hbm, one_send_hbm, one_keep_hbm,
    two_send_hbm, two_keep_hbm, normed_ref, right_ref, attended_ref, mid_ref, one_ref, two_ref, sems, *, piece, groups,
):
    moves = Moves(sems)
    copies = [
        moves.start(normed_hbm, normed_ref), moves.start(send_hbm, right_ref.at[1]), moves.start(keep_hbm, right_ref.at[0])
    ]
    then = [
        moves.start(attended_hbm, attended_ref.at[s[0]]),
        moves.start(attended_far_hbm, attended_ref.at[1 - s[0]]),
        moves.start(mid_grad_hbm.at[:, quarter_columns(s, 0)], mid_ref.at[:, :QUARTER]),
        moves.start(mid_grad_hbm.at[:, quarter_columns(s, 1)], mid_ref.at[:, QUARTER:]),
    ]
    blocks = [s[3 + n] for n in range(groups)]
    wait(*copies)
    left = chosen(normed_ref, [s[3 + groups + n] for n in range(groups)], piece)
    both_qk = 2 * QUARTER
    saved = []
    for side, target in ((1, one_send_hbm), (0, one_keep_hbm)):
        one_ref[side] = dot(left, right_ref[side, :, :both_qk], (0, 0)).astype(bf16)
        saved.append(moves.start(one_ref.at[side], target))
    left = chosen(normed_ref, blocks, piece)
    wait(*then)
    features = jnp.concatenate([attended_ref[b >> 2, :, part_of(b & 3, piece)] for b in blocks], axis=1)
    half = two_keep_hbm.shape[0]
    for side in range(2):
        quarter = slice(side * QUARTER, (side + 1) * QUARTER)
        columns = side * both_qk
        two_ref[:, columns : columns + QUARTER] = dot(left, right_ref[side, :, both_qk:], (0, 0)).astype(bf16)
        two_ref[:, columns + QUARTER : columns + both_qk] = dot(features, mid_ref[:, quarter], (0, 0)).astype(bf16)
    saved.append(moves.start(two_ref.at[half:, :], two_send_hbm))
    saved.append(moves.start(two_ref.at[:half, :], two_keep_hbm))
    wait(*saved)


def side_grads_kernel(
    s, head_hbm, head_far_hbm, start_hbm, small_ref, sent_ref, kept_ref, head_ref, start_ref, pos_ref, sems, *, piece, groups
):
    moves = Moves(sems)
    seq = start_ref.shape[0]
    wait(
        moves.start(head_hbm, head_ref.at[s[0]]),
        moves.start(head_far_hbm, head_ref.at[1 - s[0]]),
        moves.start(start_hbm, start_ref),
    )
    pos_ref[...] = start_ref[...].astype(f32)
    count = groups // 2
    for first in (count, 0):
        blocks = [s[3 + n] for n in range(first, first + count)]
        per_head = jnp.concatenate([head_ref[b >> 2, part_of(b & 3, piece), :] for b in blocks], axis=0)
        out = dot(per_head, start_ref[...], (1, 0)).astype(bf16)
        columns = []
        for side in range(2):
            quarter = slice(side * QUARTER, (side + 1) * QUARTER)
            pos = []
            for b in blocks:
                block = pos_ref[part_of(b, seq // groups), quarter]
                pos += [block[:, :LANES], block[:, LANES:]]
            columns += [out[:, quarter], jnp.concatenate(pos, axis=0).astype(bf16)]
        columns = jnp.concatenate(columns, axis=1)
        if first == 0:
            kept_ref[...] = columns
        else:
            sent_ref[...] = packed(columns, small_ref[...])


def by_squares(value):
    rows, columns = value.shape
    return jnp.concatenate(
        [
            jnp.concatenate([value[r : r + LANES, c : c + LANES] for r in range(0, rows, LANES)], axis=1)
            for c in range(0, columns, LANES)
        ],
        axis=0,
    )


def packed(side, small):
    width = side.shape[0]
    return jnp.concatenate([by_squares(side)] + [small[:, n : n + width] for n in range(0, D, width)], axis=0)


def unpacked(value, columns):
    small = value[columns:]
    parts = D // value.shape[1]
    return by_squares(value[:columns]), jnp.concatenate(
        [small[n * SMALL_ROWS : (n + 1) * SMALL_ROWS] for n in range(parts)], axis=1
    )


def both(one, two):
    return (one.astype(f32) + two.astype(f32)).astype(bf16)


def fetched_halves_kernel(s, one_hbm, one_came, two_hbm, two_came, *refs):
    *outs, one_ref, two_ref, sems = refs
    moves = Moves(sems)
    copies = [moves.start(one_hbm, one_ref), moves.start(two_hbm, two_ref)]
    for n, (kept, came) in enumerate(((one_ref, one_came), (two_ref, two_came))):
        copies[n].wait()
        keep, send = outs[2 * n : 2 * n + 2]
        half = keep.shape[0]
        send[...] = both(kept[half:], came[half:])
        keep[...] = both(kept[:half], came[:half])


def halves_kernel(s, *refs):
    count = len(refs) // 4
    for n in range(count):
        kept, came = refs[2 * n : 2 * n + 2]
        keep, send = refs[2 * count + 2 * n : 2 * count + 2 * n + 2]
        half = keep.shape[0]
        send[...] = both(kept[half:], came[half:])
        keep[...] = both(kept[:half], came[:half])


def heads_kernel(s, one_ref, one_came_ref, two_ref, two_came_ref, one_keep, one_send, two_keep, two_send, sems):
    half = one_keep.shape[0]
    one_send[...] = both(one_ref[half:], one_came_ref[half:])
    one_keep[...] = both(one_ref[:half], one_came_ref[:half])
    width = two_keep.shape[2]
    two_send[...] = both(two_ref[:, :, width:], two_came_ref[:, :, width:])
    two_keep[...] = both(two_ref[:, :, :width], two_came_ref[:, :, :width])


def side_step_kernel(s, side_ref, small_ref, came_ref, keep_ref, sum_ref, *rest):
    side, small = unpacked(came_ref[...], side_ref.shape[1])
    side = both(side_ref[...], side)
    small = both(small_ref[...], small)
    sum_ref[...] = small
    rows, columns = keep_ref.shape
    keep_ref[...] = side[:rows, :columns]
    if columns < side.shape[1]:
        rest[0][...] = packed(side[:, columns:], small)
    elif rows < side.shape[0]:
        rest[0][...] = packed(side[rows:], small)


def join_kernel(s, one_ref, two_ref, both_ref, sems):
    width = one_ref.shape[1]
    both_ref[:, :width] = one_ref[...]
    both_ref[:, width:] = two_ref[...]


def last_kernel(s, *refs):
    sum_ref = refs[-2]
    start = 0
    for n in range((len(refs) - 2) // 2):
        kept, came = refs[2 * n : 2 * n + 2]
        width = kept.shape[2]
        sum_ref[:, start : start + width] = both(kept[0], came[0])
        start += width


def sum_kernel(s, kept_ref, came_ref, sum_ref, sems):
    sum_ref[...] = both(kept_ref[...], came_ref[...])


def small_kernel(
    s, own_ref, came_ref, table_hbm, probe_ref, far_probe_ref, w_value_hbm, w_key_hbm, query_ref, w_query_hbm, cut_table_ref,
    cut_probe_ref, cut_query_ref,
    embed_ref, var_ref, value_grad_ref, key_grad_ref, query_grad_ref, vector_ref, bias_ref,
    table_ref, my_value_ref, w_key_ref, my_w_query_ref, sems, *, piece,
):
    moves = Moves(sems)
    mine = pl.ds(pl.multiple_of(s[2] * piece, piece), piece)
    copies = [
        moves.start(table_hbm, table_ref),
        moves.start(w_value_hbm.at[mine, :], my_value_ref),
        moves.start(w_key_hbm, w_key_ref),
        moves.start(w_query_hbm.at[mine, :], my_w_query_ref),
    ]
    own, came = own_ref[...], came_ref[...]
    swap = s[0] == 1
    low = jnp.where(swap, came, own)
    high = jnp.where(swap, own, came)
    probes = (probe_ref[...], far_probe_ref[...])
    probe_low = jnp.where(swap, probes[1], probes[0])
    probe_high = jnp.where(swap, probes[0], probes[1])
    my_table = cut_table_ref[...]
    my_probe = cut_probe_ref[...]
    marked = (lax.broadcasted_iota(jnp.int32, (8, PADDED), 1) == ROWS).astype(f32).astype(bf16)
    wait(*copies)
    my_value = my_value_ref[...]
    table_grad = None
    for c, part in enumerate((low, high)):
        for n in range(HALF // LANES):
            g = part[:LANES, n * PADDED : (n + 1) * PADDED]
            columns = slice(c * HALF + n * LANES, c * HALF + (n + 1) * LANES)
            value_grad_ref[:, columns] = dot(my_table, g, (0, 1))
            bias_ref[:, columns] = dot(marked, g, (1, 1))
            term = dot(g, my_value[:, columns], (0, 1))
            table_grad = term if table_grad is None else table_grad + term
    coef = jnp.concatenate([low[128:136, :PADDED].astype(f32), high[128:136, :PADDED].astype(f32)], axis=0) * 0.125
    coef_low = coef.astype(bf16)
    probe3 = in_three(my_probe)
    for n in range(3):
        table_grad = table_grad + dot(coef_low, probe3[n * HEADS : (n + 1) * HEADS], (0, 0))
    by_cell = in_three(table_grad[:CELLS])
    perm = cell_order()
    embed_ref[...] = sum(dot(perm, by_cell[n * CELLS : (n + 1) * CELLS], (0, 0)) for n in range(3))
    var_ref[...] = table_grad[CELLS:ROWS]
    probe_grad = dot(coef_low, table_ref[...], (1, 0))
    my_probe_grad = dot(coef_low, my_table, (1, 0))
    row = lax.broadcasted_iota(jnp.int32, (HEADS, D), 0)
    lane = lax.broadcasted_iota(jnp.int32, (HEADS, D), 1)
    own_head = (lane >= row * HD) & (lane < (row + 1) * HD)
    asked = jnp.concatenate([probe_low[8:9, :HALF], probe_high[8:9, :HALF]], axis=1)
    key_grad_ref[...] = dot(my_probe_grad, jnp.where(own_head, asked, 0.0), (0, 0), f32, highest)
    asked_grad = summed_rows(dot(in_three(probe_grad), w_key_ref[...], (1, 0)), HEADS)
    asked_grad = column_sums(jnp.where(own_head, asked_grad, 0.0))
    my_query = jnp.broadcast_to(cut_query_ref[...].astype(f32), (8, piece))
    first_row = lax.broadcasted_iota(jnp.int32, (8, D), 0) == 0
    query_grad_ref[...] = dot(my_query, jnp.where(first_row, asked_grad, 0.0), (0, 0), f32, highest)
    vector_ref[...] = summed_rows(dot(in_three(jnp.broadcast_to(asked_grad, (8, D))), my_w_query_ref[...], (1, 1)), 8)


def four_places(s, refs, width):
    for n, ref in enumerate(refs):
        core = s[0] if n < 2 else 1 - s[0]
        far = s[1] if n % 2 == 0 else 1 - s[1]
        yield ref[...].astype(f32), pl.multiple_of((core * 2 + far) * width, width)


def mlp_final_kernel(s, one_ref, two_ref, three_ref, four_ref, up_hbm, down_hbm, up_ref, down_ref, sems):
    width = one_ref.shape[1] // 2
    for block, start in four_places(s, (one_ref, two_ref, three_ref, four_ref), width):
        up_ref[:, pl.ds(start, width)] = block[:, :width]
        down_ref[pl.ds(start, width), :] = jnp.transpose(block[:, width:])
    moves = Moves(sems)
    wait(moves.start(up_ref, up_hbm), moves.start(down_ref, down_hbm))


def attend_final_kernel(s, one_ref, two_ref, three_ref, four_ref, qkv_ref, proj_ref, out_ref, pos_ref, sems):
    for block, start in four_places(s, (one_ref, two_ref, three_ref, four_ref), QUARTER):
        for n in range(3):
            place = pl.ds(pl.multiple_of(n * D + start, QUARTER), QUARTER)
            qkv_ref[:, place] = block[:, n * QUARTER : (n + 1) * QUARTER]
        place = pl.ds(start, QUARTER)
        proj_ref[:, place] = block[:, 3 * QUARTER : D]
        out_ref[:, place] = block[:, D : D + QUARTER]
        rows = pos_ref.shape[0]
        last = block[:, D + QUARTER :]
        pos_ref[:, place] = jnp.concatenate([last[:rows], last[rows:]], axis=1)


def bit_orders(groups):
    first = list(range(groups.bit_length() - 1))
    return first, first[1:] + first[:1]


def block_map(groups, way):
    order = bit_orders(groups)[way]
    bits = len(order)
    return [sum(1 << order[n] for n in range(bits) if j >> (bits - 1 - n) & 1) for j in range(groups)]


def swap_core(value):
    return lax.ppermute(value, "section", [(s, s ^ 1) for s in range(4)])


def swap_y(value):
    return lax.ppermute(value, "section", [(s, s ^ 2) for s in range(4)])


def swap_stage(value, groups, stage, way=0):
    bit = 1 << bit_orders(groups)[way][stage]
    return lax.ppermute(value, "dp", [(g, g ^ bit) for g in range(groups)])


def cut(value, start, length, axis):
    return lax.dynamic_slice_in_dim(value, start, length, axis)


def packed_narrow(side, small):
    return jnp.concatenate([side.reshape(-1), small.reshape(-1)]).reshape(-1, side.shape[0])


def unpacked_narrow(value, columns):
    flat = value.reshape(-1)
    size = columns * value.shape[1]
    return flat[:size].reshape(value.shape[1], columns), flat[size:].reshape(SMALL_ROWS, D)


def narrow_mlp_sums(blocks, second_blocks, piece, core, far, normed, first, second, cotangent, w_up, b_up, w_down, pre_grad, hidden):
    rows = first.shape[0]
    quarter = hidden.shape[2]
    order = lambda v, chosen_blocks: jnp.concatenate([cut(v, b * piece, piece, 1) for b in chosen_blocks], axis=1)
    other_cot = [cut(cotangent, ((1 - far) * 2 + c) * rows, rows, 0) for c in (core, 1 - core)]
    other = jnp.concatenate([first, second])
    pre = dot(other, cut(w_up, (2 * core + far) * quarter, quarter, 1), (1, 0)) + cut(
        b_up, (2 * core + far) * quarter, quarter, 0
    )
    gate, slope = gelu_both(pre)
    back = dot(jnp.concatenate(other_cot), cut(w_down, (2 * core + far) * quarter, quarter, 0), (1, 1))
    pre_grads = jnp.concatenate([lax.dynamic_index_in_dim(pre_grad, far, 0, False), (back * slope).astype(bf16)])
    hiddens = jnp.concatenate([lax.dynamic_index_in_dim(hidden, far, 0, False), gate.astype(bf16)])
    up = dot(order(jnp.concatenate([normed, other]), blocks), pre_grads, (0, 0), bf16)
    cots = jnp.concatenate([cut(cotangent, far * 2 * rows, 2 * rows, 0)] + other_cot)
    down = dot(order(cots, second_blocks), hiddens, (0, 0), bf16)
    return up[D // 2 :], up[: D // 2], down[D // 2 :], down[: D // 2]


def narrow_head_sums(blocks, second_blocks, piece, core, far, normed, keep, send, attended, attended_far, mid_grad):
    order = lambda v, way: jnp.concatenate([cut(v, b * piece, piece, 1) for b in way], axis=1)
    left = order(normed, second_blocks)
    features = [jnp.concatenate(v, axis=1) for v in ((attended, attended_far), (attended_far, attended))]
    features = order(jnp.where(core == 0, *features), blocks)
    one = [dot(left, v[:, : 2 * QUARTER], (0, 0), bf16) for v in (send, keep)]
    left = order(normed, blocks)
    parts = []
    for v, y in ((keep, far), (send, 1 - far)):
        parts.append(dot(left, v[:, 2 * QUARTER :], (0, 0), bf16))
        parts.append(dot(features, cut(mid_grad, core * HALF + y * QUARTER, QUARTER, 1), (0, 0), bf16))
    two = jnp.concatenate(parts, axis=1)
    return one + [two[D // 2 :], two[: D // 2]]


def narrow_side_sums(blocks, piece, core, head, head_far, start_sides, small):
    order = lambda v, width: jnp.concatenate([cut(v, b * width, width, 0) for b in blocks])
    heads = order(jnp.where(core == 0, *(jnp.concatenate(v) for v in ((head, head_far), (head_far, head)))), piece)
    count, seq = blocks.shape[0], head.shape[1]
    parts = []
    for side in range(2):
        start = start_sides[:, side * QUARTER : (side + 1) * QUARTER]
        parts.append(dot(heads, start, (1, 0), bf16))
        pos = order(start, seq // count).reshape(count, seq // count, 2, LANES)
        parts.append(jnp.transpose(pos, (0, 2, 1, 3)).reshape(-1, LANES))
    result = jnp.concatenate(parts, axis=1)
    return packed(result[D // 2 :], small), result[: D // 2]


def added(kept, arrived):
    return (kept.astype(f32) + arrived.astype(f32)).astype(bf16)


def local(
    pixels, cell_mask, lead_time, query, w_query, w_key, w_value, b_value, w_out, b_out, w_embed,
    var_embed, pos_embed, w_lead, b_lead, gain_one, shift_one, w_qkv, w_proj, b_proj, gain_two,
    shift_two, w_up, b_up, w_down, b_down, cotangent,
):
    groups = lax.axis_size("dp")
    stages = groups.bit_length() - 1
    me = lax.axis_index("dp")
    section = lax.axis_index("section")
    core, far = section % 2, section // 2
    seq = pixels.shape[0] // lead_time.shape[0]
    rows = seq // 2
    units = w_up.shape[1]
    quarter = units // 4
    piece = D // groups
    narrow = piece % LANES != 0
    blocks, second_blocks = (me ^ jnp.array(block_map(groups, way), jnp.int32) for way in range(2))
    scalars = jnp.concatenate([jnp.stack([core, far, me]), blocks, second_blocks]).astype(jnp.int32)
    row = lambda v: v.reshape(1, -1)
    pix, mask = jnp.transpose(pixels), jnp.transpose(cell_mask)
    lead = scalar(lead_time)
    half = groups // 2
    sizes = dict(piece=piece, groups=groups)
    held = lambda *shape: pltpu.VMEM(shape, bf16)
    wide = lambda *shape: pltpu.VMEM(shape, f32)
    kept_far = True

    start_part, per_head, coef, tv, table, probe = call(
        start_kernel,
        scalars,
        [
            remote(pix), remote(mask), row(query), remote(w_query), remote(w_key), remote(w_value), remote(row(b_value)),
            remote(w_out), remote(w_embed), remote(var_embed),
        ],
        [
            ((seq, D), bf16), ((HALF, seq), bf16, kept_far), ((PADDED, OWN_HEADS), f32), ((HALF, PADDED), bf16, kept_far),
            ((PADDED, D), bf16, kept_far), ((16, D), f32),
        ],
        scratch=[
            held(D, HALF), held(D, HALF), held(D, HALF), held(HALF, D), held(HALF, seq), held(HALF, PADDED), held(PADDED, D),
            held(CELLS, seq), pltpu.VMEM((CELLS, seq), jnp.int32), held(CELLS, D), held(VARS, D), wide(1, D),
        ],
        us=6,
    )
    far_probe = swap_core(probe)
    start_near, proj_part, start, normed_one, qkv, lse, attended = call(
        attend_kernel,
        scalars,
        [
            start_part, swap_core(start_part), pos_embed, lead, row(w_lead), row(b_lead), row(b_out), row(gain_one),
            row(shift_one), remote(w_qkv), remote(w_proj),
        ],
        [
            ((seq, D), bf16), ((seq, D), bf16), ((seq, D), bf16, kept_far), ((seq, D), bf16, kept_far),
            ((seq, 3 * HALF), bf16, kept_far), ((OWN_HEADS // 2, seq, LANES), f32, kept_far),
            ((seq, HALF), bf16, kept_far),
        ],
        scratch=[
            held(3, D, HALF), held(HALF, D), held(seq, D), held(seq, 3 * HALF), wide(OWN_HEADS // 2, seq, LANES),
            held(seq, HALF),
        ],
        us=12,
        after=[far_probe],
    )
    proj_came = swap_core(proj_part)
    normed_near, half_two, mid, normed_two = call(
        middle_kernel,
        scalars,
        [
            start_near, lead, row(w_lead), row(b_lead), row(b_proj), proj_part, proj_came, row(gain_two), row(shift_two),
        ],
        [((seq, D), bf16), ((rows, D), bf16), ((seq, D), bf16, kept_far), ((seq, D), bf16, kept_far)],
        scratch=[held(seq, D)],
        us=2.5,
    )
    other_two = swap_y(half_two)
    up_sums, normed_part, hidden, pre_grad = call(
        mlp_kernel,
        scalars,
        [normed_near, remote(cotangent), remote(w_up), row(b_up), remote(w_down)],
        [
            ((1, 2 * quarter), f32), ((seq, D), bf16), ((2, seq, quarter), bf16, kept_far),
            ((2, seq, quarter), bf16, kept_far),
        ],
        scratch=[
            held(2, seq, quarter), held(2, seq, quarter), held(2, D, quarter), held(2, quarter, D), held(seq, D),
        ],
        mb=22,
        us=11,
    )
    normed_came = swap_core(normed_part)
    by_block = lambda value: value.reshape(half, piece, value.shape[1])
    def halved(arrays, after):
        outs = [((v.shape[0] // 2,) + v.shape[1:], bf16) for v in arrays[::2] for _ in range(2)]
        return call(halves_kernel, scalars, arrays, outs, us=600, mb=16, after=after)


    attended_far, per_head_far = swap_core(attended), swap_core(per_head)
    other_held, _ = lax.optimization_barrier((other_two, normed_part))
    other_two_far = swap_core(other_held)
    if narrow:
        up_send, up_keep, down_send, down_keep = narrow_mlp_sums(
            blocks, second_blocks, piece, core, far, normed_two, other_two, other_two_far, cotangent, w_up, b_up, w_down, pre_grad, hidden
        )
    else:
        up_send, up_keep, down_send, down_keep = call(
            functools.partial(mlp_grads_kernel, **sizes),
            scalars,
            [remote(normed_two), other_two, other_two_far, remote(cotangent), remote(w_up)]
            + [row(b_up), remote(w_down), remote(pre_grad), remote(hidden)],
            [((D // 2, quarter), bf16, kept_far)] * 4,
            scratch=[
                held(2 * seq, D), held(2 * seq, D), held(D, quarter), held(quarter, D), held(2 * seq, quarter),
                held(2 * seq, quarter), held(2, D, quarter),
            ],
            us=15,
            mb=24,
            after=[normed_came, attended_far, per_head_far],
        )
    up_keep, down_keep = by_block(up_keep), by_block(down_keep)
    up_came = swap_stage(by_block(up_send), groups, 0)
    down_came = swap_stage(by_block(down_send), groups, 0, 1)

    class Sum:
        def __init__(self, keep, way, stage, sent=None, came=None):
            self.keep, self.way, self.stage = keep, way, stage
            self.came = swap_stage(sent, groups, stage, way) if came is None else came

    def onward(sums, after):
        results = halved([v for x in sums for v in (x.keep, x.came)], after)
        for n, x in enumerate(sums):
            x.keep, x.stage = results[2 * n], x.stage + 1
            x.came = swap_stage(results[2 * n + 1], groups, x.stage, x.way)
        return results[0]

    def last(sums, after):
        columns = sum(x.keep.shape[2] for x in sums)
        arrays = [v for x in sums for v in (x.keep, x.came)]
        return call(last_kernel, scalars, arrays, [((piece, columns), bf16)], us=600, after=after)[0]

    norm_part, mid_sums, qkv_keep, qkv_send, mid_grad = call(
        attend_back_kernel,
        scalars,
        [
            normed_part, normed_came, remote(mid), remote(cotangent), row(gain_two), remote(qkv), remote(attended),
            remote(lse), remote(w_proj), remote(w_qkv),
        ],
        [
            ((seq, D), bf16), ((8, D), f32), ((seq, 3 * QUARTER), bf16, kept_far), ((seq, 3 * QUARTER), bf16, kept_far),
            ((seq, D), bf16, kept_far),
        ],
        scratch=[
            held(seq, D), held(seq, D), held(seq, 3 * HALF), held(seq, HALF), wide(OWN_HEADS // 2, seq, LANES),
            held(3, D, HALF), held(HALF, D), held(seq, HALF), held(seq, 3 * HALF), held(seq, 3 * QUARTER),
            held(seq, 3 * QUARTER), held(seq, D),
        ],
        mb=22,
        us=14,
        after=[remote(up_send)],
    )
    norm_came = swap_core(norm_part)
    if narrow:
        one_send, one_keep, two_send, two_keep = narrow_head_sums(
            blocks, second_blocks, piece, core, far, normed_one, qkv_keep, qkv_send, attended, attended_far, mid_grad
        )
    else:
        one_send, one_keep, two_send, two_keep = call(
            functools.partial(head_grads_kernel, **sizes),
            scalars,
            [remote(x) for x in (normed_one, qkv_keep, qkv_send, attended, attended_far, mid_grad)],
            [((D, HALF), bf16, kept_far)] * 2 + [((D // 2, D), bf16, kept_far)] * 2,
            scratch=[
                held(seq, D), held(2, seq, 3 * QUARTER), held(2, seq, HALF), held(seq, HALF), held(2, D, HALF), held(D, D),
            ],
            us=4,
            after=[norm_part],
        )
    one_came = swap_y(one_send.reshape(groups, piece, HALF))
    two_came = swap_stage(by_block(two_send), groups, 0)

    outs = [((half // 2, piece, quarter), bf16)] * 4
    up_keep, up_send, down_keep, down_send = call(
        fetched_halves_kernel,
        scalars,
        [remote(up_keep), up_came, remote(down_keep), down_came],
        outs,
        scratch=[held(half, piece, quarter)] * 2,
        us=600,
        after=[remote(one_send)],
    )
    up, down = Sum(up_keep, 0, 1, up_send), Sum(down_keep, 1, 1, down_send)

    pix_kept, pix_sent, start_sides, small = call(
        start_back_kernel,
        scalars,
        [
            norm_part, norm_came, remote(start), lead, row(w_lead), row(b_lead), row(gain_one), remote(mid_grad),
            remote(w_out), remote(pix), remote(mask), coef, remote(tv), mid_sums, up_sums,
        ],
        [
            ((CELLS, rows), f32), ((CELLS, rows), bf16), ((seq, HALF), bf16, kept_far), ((SMALL_ROWS, D), bf16),
        ],
        scratch=[
            wide(CELLS, seq), held(HALF, D), held(seq, D), held(seq, D), held(HALF, PADDED), held(seq, D),
            held(seq, HALF), held(CELLS, seq), pltpu.VMEM((CELLS, seq), jnp.int32),
        ],
        us=7,
        after=[up.keep],
    )

    if narrow:
        side_sent, side_keep = narrow_side_sums(blocks, piece, core, per_head, per_head_far, start_sides, small)
    else:
        side_sent, side_keep = call(
            functools.partial(side_grads_kernel, **sizes),
            scalars,
            [remote(x) for x in (per_head, per_head_far, start_sides)] + [small],
            [((2 * (QUARTER + LANES + SMALL_ROWS), HALF), bf16), ((HALF, 2 * (QUARTER + LANES)), bf16)],
            scratch=[held(2, HALF, seq), held(seq, HALF), wide(seq, HALF)],
            us=4,
            after=[small],
        )
    side_came = swap_stage(side_sent, groups, 0)
    out_sent, out_kept = call(
        out_kernel,
        scalars,
        [remote(hidden), remote(w_down), remote(mid), row(b_down)],
        [((rows, D), bf16), ((rows, D), f32)],
        scratch=[wide(seq, D), held(2, seq, quarter), held(2, quarter, D), held(rows, D)],
        us=4,
        after=[side_keep],
    )


    def summed(kept, arrived, after=()):
        return call(sum_kernel, scalars, [kept, arrived], [(kept.shape, bf16)], us=600, mb=16, after=after)[0]

    head_rows = ((half, piece, HALF), bf16)
    one_keep, one_send, two_keep, two_send = call(
        heads_kernel,
        scalars,
        [one_keep.reshape(groups, piece, HALF), one_came, by_block(two_keep), two_came],
        [head_rows] * 4,
        us=600,
        mb=16,
        after=[out_sent],
    )
    two_came = swap_y(two_send)
    stages = groups.bit_length() - 1

    one = Sum(one_keep, 1, 0, one_send)
    two = Sum(two_keep, 0, 0, came=two_came)
    after = one_keep
    for _ in range(stages - 2):
        after = onward([up, down], [after])

    def side_step(side, small, came, after):
        rows, columns = side.shape
        if columns > QUARTER + LANES:
            columns //= 2
            outs = [((rows, columns), bf16), (small.shape, bf16), ((columns + SMALL_ROWS * D // rows, rows), bf16)]
        elif rows == piece:
            outs = [(side.shape, bf16), (small.shape, bf16)]
        else:
            outs = [((rows // 2, columns), bf16), (small.shape, bf16)]
            outs.append(((columns + SMALL_ROWS * D * 2 // rows, rows // 2), bf16))
        if narrow and rows <= LANES:
            arrived = (unpacked if rows == LANES else unpacked_narrow)(came, columns)
            side, small = added(side, arrived[0]), added(small, arrived[1])
            if rows == piece:
                return side, small
            return side[: rows // 2], small, packed_narrow(side[rows // 2 :], small)
        return call(side_step_kernel, scalars, [side, small, came], outs, us=600, mb=16, after=after)

    side_keep, small, side_send = side_step(side_keep, small, side_came, [after])
    side_came = swap_y(side_send)
    after = onward([one, two], [side_keep])
    mlp_piece = last([up, down], [after])
    after = mlp_piece
    for stage in range(1, stages):
        side_keep, small, side_send = side_step(side_keep, small, side_came, [after])
        side_came = swap_stage(side_send, groups, stage)
        after = onward([one, two], [side_keep]) if stage < stages - 1 else side_keep
    probes = jnp.concatenate([jnp.where(core == c, probe, far_probe)[:OWN_HEADS] for c in range(2)])
    probes, table_late, query_late, _ = lax.optimization_barrier((probes, table, query, mlp_piece))
    my_probe = cut(probes, me * piece, piece, 1)
    my_table = cut(table_late, me * piece, piece, 1)
    my_query = row(cut(query_late, me * piece, piece, 0))
    mlp_held, _ = lax.optimization_barrier((mlp_piece, one.keep))
    mlp_y, mlp_core = swap_y(mlp_held), swap_core(mlp_held)
    heads_piece = last([one, two], [after])
    w_up_grad, w_down_grad = call(
        mlp_final_kernel,
        scalars,
        [mlp_piece, mlp_y, mlp_core, swap_core(mlp_y)],
        [((piece, units), f32, kept_far), ((units, piece), f32, kept_far)],
        scratch=[wide(piece, units), wide(units, piece)],
        us=1,
        after=[heads_piece],
    )
    side_keep, small = side_step(side_keep, small, side_came, [remote(w_up_grad), my_probe, my_query, my_table])
    other_small = swap_core(small)
    attend_piece = call(
        join_kernel, scalars, [heads_piece, side_keep], [((piece, D + QUARTER + LANES), bf16)], us=1, after=[small]
    )[0]
    attend_y, attend_core = swap_y(attend_piece), swap_core(attend_piece)
    embed_grad, var_grad, w_value_grad, w_key_grad, w_query_grad, query_rows, bias_rows = call(
        functools.partial(small_kernel, piece=piece),
        scalars,
        [
            small, other_small, remote(table), probe, far_probe, remote(w_value), remote(w_key), row(query),
            remote(w_query), my_table, my_probe, my_query,
        ],
        [
            ((CELLS, piece), f32), ((VARS, piece), f32), ((piece, D), f32), ((piece, D), f32), ((piece, D), f32),
            ((8, piece), f32), ((8, D), f32),
        ],
        scratch=[held(PADDED, D), held(piece, D), held(D, D), held(piece, D)],
        us=600,
        after=[attend_piece],
    )
    out_late, pix_late, _ = lax.optimization_barrier((out_sent, pix_sent, embed_grad))
    block_out = (out_kept + swap_core(out_late).astype(f32)).astype(bf16)
    pixels_grad = jnp.transpose(pix_kept + swap_core(pix_late).astype(f32))

    query_grad = query_rows[0]
    my_value_bias = cut(bias_rows, me * piece, piece, 1)[0]
    shared = jnp.where(core == 0, small, other_small)[136:145].astype(f32)
    shared = cut(shared, me * piece, piece, 1)
    gain_two_grad, shift_two_grad, b_proj_grad, b_down_grad, gain_one_grad = (shared[n] for n in range(5))
    shift_one_grad, b_lead_grad, w_lead_grad, b_out_grad = (shared[n] for n in range(5, 9))
    up_rows = [jnp.where(core == c, small, other_small)[145:147] for c in range(2)]
    up_bias_grad = jnp.concatenate(up_rows).reshape(-1).astype(f32)
    my_up_bias = cut(up_bias_grad, me * (units // groups), units // groups, 0)

    w_qkv_grad, w_proj_grad, w_out_grad, pos_grad = call(
        attend_final_kernel,
        scalars,
        [attend_piece, attend_y, attend_core, swap_core(attend_y)],
        [((piece, 3 * D), f32), ((piece, D), f32), ((piece, D), f32), ((seq // groups, D), f32)],
        after=[embed_grad, block_out],
    )
    return (
        block_out, pixels_grad, query_grad, w_query_grad, w_key_grad, w_value_grad, my_value_bias, w_out_grad, b_out_grad,
        embed_grad, var_grad, pos_grad, w_lead_grad, b_lead_grad, gain_one_grad, shift_one_grad, w_qkv_grad, w_proj_grad,
        b_proj_grad, gain_two_grad, shift_two_grad, w_up_grad, my_up_bias, w_down_grad, b_down_grad,
    )


def solution(mesh):
    whole = P()
    args = (P("dp", None), P("dp", None), P("dp")) + (whole,) * 23 + (P("dp", None),)
    outs = (
        (P(axes, None),) * 2
        + (P("dp"),)
        + (P("dp", None),) * 3
        + (P("dp"), P("dp", None), P("dp"), P(None, "dp"), P(None, "dp"), P("dp", None))
        + (P("dp"),) * 4
        + (P("dp", None),) * 2
        + (P("dp"),) * 3
        + (P("dp", None), P("dp"), P(None, "dp"), P("dp"))
    )
    return jax.shard_map(local, mesh=mesh, in_specs=args, out_specs=outs, check_vma=False)
```

```python
import functools

import jax
import jax.numpy as jnp
from jax import lax
from jax.experimental import pallas as pl
from jax.experimental.pallas import tpu as pltpu
from jax.sharding import PartitionSpec as P

D = 1024
HEADS = 16
HD = 64
VARS = 48
PIX = 4
CELLS = VARS * PIX
ROWS = CELLS + VARS
PADDED = 256
OWN_HEADS = HEADS // 2
HALF = D // 2
QUARTER = D // 4
LANES = 128
SMALL_ROWS = 160

highest = lax.Precision.HIGHEST
epsilon = 1e-05
bf16 = jnp.bfloat16
f32 = jnp.float32
axes = ("dp", "section")


def dot(a, b, contract, kind=f32, precision=None):
    return lax.dot_general(
        a, b, ((contract[:1], contract[1:]), ((), ())), precision=precision, preferred_element_type=kind
    )


def call(body, scalars, ins, outs, scratch=(), us=2, mb=16, after=()):
    del scalars
    arrays, in_specs = [], []
    for item in list(ins) + [x if isinstance(x, tuple) else (x, pl.ANY) for x in after]:
        array, space = item if isinstance(item, tuple) else (item, pltpu.VMEM)
        in_specs.append(pl.BlockSpec(memory_space=space))
        arrays.append(array)
    count = len(ins)

    def placed(*refs):
        body(Place(), *refs[:count], *refs[count + len(after) :])

    return pl.pallas_call(
        placed,
        in_specs=in_specs,
        out_specs=[pl.BlockSpec(memory_space=pltpu.HBM if len(item) > 2 else pltpu.VMEM) for item in outs],
        out_shape=[
            pltpu.HBM(*item[:2]) if len(item) > 2 else jax.ShapeDtypeStruct(*item) for item in outs
        ],
        scratch_shapes=list(scratch) + [pltpu.SemaphoreType.DMA((24,))],
        compiler_params=pltpu.CompilerParams(vmem_limit_bytes=mb << 20),
        cost_estimate=pl.CostEstimate(flops=int(us * 1e7), bytes_accessed=1 << 12, transcendentals=0),
    )(*arrays)


class Place:
    def __getitem__(self, n):
        if n < 2:
            section = lax.axis_index("section")
            return section & 1 if n == 0 else section >> 1
        me = lax.axis_index("dp")
        if n == 2:
            return me
        groups = lax.axis_size("dp")
        return me ^ block_map(groups, (n - 3) // groups)[(n - 3) % groups]


def remote(array):
    return pltpu.with_memory_space_constraint(array, pltpu.HBM), pltpu.HBM


def scalar(array):
    return array, pltpu.SMEM


class Moves:
    def __init__(self, sems):
        self.sems, self.count = sems, 0

    def start(self, source, place):
        copy = pltpu.make_async_copy(source, place, self.sems.at[self.count])
        self.count += 1
        copy.start()
        return copy


def wait(*copies):
    for copy in copies:
        copy.wait()


def part_of(start, size):
    return pl.ds(pl.multiple_of(start * size, size), size)


def cell_order():
    row = lax.broadcasted_iota(jnp.int32, (CELLS, CELLS), 0)
    column = lax.broadcasted_iota(jnp.int32, (CELLS, CELLS), 1)
    cell = sum((row >= n * VARS).astype(jnp.int32) for n in range(1, PIX))
    return ((row - cell * VARS) * PIX + cell == column).astype(f32).astype(bf16)


def in_three(value):
    high = value.astype(bf16).astype(f32)
    middle = (value - high).astype(bf16).astype(f32)
    return jnp.concatenate([high, middle, value - high - middle], axis=0).astype(bf16)


def summed_rows(value, rows):
    return value[:rows] + value[rows : 2 * rows] + value[2 * rows :]


def head_weights(cells, pen, coef, h):
    scores = pen + coef[CELLS:ROWS, h : h + 1]
    for j in range(PIX):
        rows = slice(j * VARS, (j + 1) * VARS)
        scores = scores + cells[rows] * coef[rows, h : h + 1]
    raised = jnp.exp(scores - jnp.max(scores, axis=0, keepdims=True))
    return raised / jnp.sum(raised, axis=0, keepdims=True)


def head_features(cells, weight):
    parts = [weight * cells[j * VARS : (j + 1) * VARS] for j in range(PIX)]
    parts = parts + [weight, jnp.ones((PADDED - ROWS, weight.shape[1]), f32)]
    return jnp.concatenate(parts, axis=0).astype(bf16)


def load_cells(pix_ref, mask_ref, perm):
    mask = mask_ref[...].astype(f32).astype(bf16)
    masked = pix_ref[...] * mask
    cells = dot(perm, masked, (1, 0))
    seen = dot(perm, mask, (1, 0))
    present = seen[:VARS]
    for j in range(1, PIX):
        present = jnp.maximum(present, seen[j * VARS : (j + 1) * VARS])
    return cells, seen, (present - 1.0) * 10000.0


def start_kernel(
    s, pix_hbm, mask_hbm, query_hbm, w_query_hbm, w_key_hbm, w_value_hbm, b_value_hbm, w_out_hbm, embed_hbm, var_hbm,
    part_ref, per_head_hbm, coef_ref, tv_hbm, table_hbm, probe_ref,
    w_query_ref, w_key_ref, w_value_ref, w_out_ref, per_head_ref, tv_ref, table_ref, pix_ref, mask_ref, embed_ref, var_ref,
    b_value_ref, query_ref, sems,
):
    half = part_of(s[0], HALF)
    seq = part_ref.shape[0]
    moves = Moves(sems)
    sample = part_of(s[1], seq)
    tables = [moves.start(embed_hbm, embed_ref), moves.start(var_hbm, var_ref)]
    pixels = [
        moves.start(pix_hbm.at[:, sample], pix_ref), moves.start(mask_hbm.at[:, sample], mask_ref),
        moves.start(b_value_hbm, b_value_ref),
    ]
    query_copy = moves.start(query_hbm, query_ref)
    copies = [
        moves.start(w_query_hbm.at[:, half], w_query_ref),
        moves.start(w_key_hbm.at[:, half], w_key_ref),
        moves.start(w_value_hbm.at[:, half], w_value_ref),
        moves.start(w_out_hbm.at[half, :], w_out_ref),
    ]
    perm = cell_order()
    wait(*tables)
    table = jnp.concatenate(
        [
            dot(perm, embed_ref[...], (1, 0)),
            var_ref[...].astype(f32),
            jnp.zeros((PADDED - ROWS, D), f32),
        ]
    ).astype(bf16)
    table_ref[...] = table
    saved = [moves.start(table_ref, table_hbm)]
    wait(*pixels)
    cells, _, pen = load_cells(pix_ref, mask_ref, perm)
    wait(*copies[:3])
    wait(query_copy)
    rows_of_query = query_ref[...].astype(f32)
    whole_query = jnp.concatenate([rows_of_query[n : n + 1] for n in range(D // LANES)], axis=1).astype(bf16)
    asked = dot(whole_query, w_query_ref[...], (1, 0))
    row = lax.broadcasted_iota(jnp.int32, (OWN_HEADS, HALF), 0)
    lane = lax.broadcasted_iota(jnp.int32, (OWN_HEADS, HALF), 1)
    by_head = jnp.where((lane >= row * HD) & (lane < (row + 1) * HD), asked, 0.0)
    probe = summed_rows(dot(in_three(by_head), w_key_ref[...], (1, 1)), OWN_HEADS)
    asked_row = jnp.concatenate([jnp.broadcast_to(asked, (8, HALF)), jnp.zeros((8, HALF), f32)], axis=1)
    probe_ref[...] = jnp.concatenate([probe, asked_row], axis=0)
    coef3 = dot(table, in_three(probe), (1, 1)) * 0.125
    coef = coef3[:, :OWN_HEADS] + coef3[:, OWN_HEADS : 2 * OWN_HEADS] + coef3[:, 2 * OWN_HEADS :]
    coef_ref[...] = coef
    tv = jnp.transpose(dot(table, w_value_ref[...], (1, 0))).astype(bf16)
    lane = lax.broadcasted_iota(jnp.int32, tv.shape, 1)
    tv = jnp.where(lane < ROWS, tv, jnp.zeros_like(tv))
    tv_ref[...] = tv
    saved.append(moves.start(tv_ref, tv_hbm))
    bias = b_value_ref[:, half]
    for h in range(OWN_HEADS):
        rows = slice(h * HD, (h + 1) * HD)
        features = head_features(cells, head_weights(cells, pen, coef, h))
        column = jnp.transpose(jnp.broadcast_to(bias[:, rows], (8, HD)))[:, :1]
        per_head_ref[rows, :] = (dot(tv[rows], features, (1, 0)) + column).astype(bf16)
    saved.append(moves.start(per_head_ref, per_head_hbm))
    wait(copies[3])
    part_ref[...] = dot(per_head_ref[...], w_out_ref[...], (0, 0)).astype(bf16)
    wait(*saved)


def norm_parts(value):
    average = jnp.mean(value, axis=-1, keepdims=True)
    centered = value - average
    scale = lax.rsqrt(jnp.mean(centered * centered, axis=-1, keepdims=True) + epsilon)
    return centered * scale, scale


def norm_back(normal, scale, gain, grad):
    inner = grad * gain
    return scale * (
        inner
        - jnp.mean(inner, axis=-1, keepdims=True)
        - normal * jnp.mean(inner * normal, axis=-1, keepdims=True)
    )


def gelu_both(x):
    k = 0.7978845608028654
    square = x * x
    t = jnp.tanh(x * (k + k * 0.044715 * square))
    gate = 0.5 + 0.5 * t
    slope = gate + (0.5 * x) * (1.0 - t * t) * (k + 3 * k * 0.044715 * square)
    return x * gate, slope


def total(first_ref, second_ref):
    return first_ref[...].astype(f32) + second_ref[...].astype(f32)


def column_sums(value):
    return jnp.sum(value, axis=0, keepdims=True)


def only_half(block, half):
    lane = lax.broadcasted_iota(jnp.int32, block.shape, 1)
    return jnp.where((lane >= HD) if half else (lane < HD), block, jnp.zeros_like(block))


def joined(low, high):
    lane = lax.broadcasted_iota(jnp.int32, low.shape, 1)
    return jnp.where(lane < HD, low, high)


def pair_columns(pair, part=0):
    return pl.ds(pl.multiple_of(part * HALF + pair * LANES, LANES), LANES)


def fetch_heads(moves, s, w_qkv_hbm, w_ref):
    return [moves.start(w_qkv_hbm.at[:, part_of(2 * n + s[0], HALF)], w_ref.at[n]) for n in range(3)]


def attend_kernel(
    s, own_ref, came_ref, pos_ref, lead_ref, w_lead_ref, b_lead_ref, b_out_ref, gain_ref, shift_ref, w_qkv_hbm,
    w_proj_hbm,
    start_ref, part_ref, start_hbm, normed_hbm, qkv_hbm, lse_hbm, out_hbm,
    w_ref, w_proj_ref, normed_ref, qkv_ref, lse_ref, out_ref, sems,
):
    moves = Moves(sems)
    copies = fetch_heads(moves, s, w_qkv_hbm, w_ref)
    proj_copy = moves.start(w_proj_hbm.at[part_of(s[0], HALF), :], w_proj_ref)
    start = (total(own_ref, came_ref) + b_out_ref[...] + pos_ref[...].astype(f32)).astype(bf16)
    start_ref[...] = start
    saved = [moves.start(start_ref, start_hbm)]
    stream = start.astype(f32) + lead_ref[s[1]] * w_lead_ref[...] + b_lead_ref[...]
    normal, _ = norm_parts(stream)
    normed = (normal * gain_ref[...] + shift_ref[...]).astype(bf16)
    normed_ref[...] = normed
    saved.append(moves.start(normed_ref, normed_hbm))
    wait(*copies)
    for n in range(3):
        qkv_ref[:, n * HALF : (n + 1) * HALF] = dot(normed, w_ref[n], (1, 0)).astype(bf16)
    saved.append(moves.start(qkv_ref, qkv_hbm))

    def one_pair(pair, carried):
        q, k, v = (qkv_ref[:, pair_columns(pair, part)] for part in range(3))
        lane = lax.broadcasted_iota(jnp.int32, v.shape, 1)
        outs, weights, norms = [], [], []
        for half in range(2):
            mine = (lane >= HD) if half else (lane < HD)
            logits = dot(only_half(q * jnp.asarray(0.125, bf16), half), k, (1, 1))
            top = jnp.max(logits, axis=1, keepdims=True)
            raised = jnp.exp(logits - top).astype(bf16)
            both = dot(raised, jnp.where(mine, v, jnp.ones_like(v)), (1, 0))
            outs.append(both)
            weights.append(pltpu.roll(both, HD, 1))
            norms.append(jnp.broadcast_to(top, both.shape))
        weight = joined(*weights)
        out_ref[:, pair_columns(pair)] = (joined(*outs) / weight).astype(bf16)
        lse_ref[pair] = joined(*norms) + jnp.log(weight)
        return carried

    lax.fori_loop(0, OWN_HEADS // 2, one_pair, 0, unroll=2)
    saved.append(moves.start(lse_ref, lse_hbm))
    saved.append(moves.start(out_ref, out_hbm))
    wait(proj_copy)
    part_ref[...] = dot(out_ref[...], w_proj_ref[...], (1, 0)).astype(bf16)
    wait(*saved)


def middle_kernel(
    s, start_ref, lead_ref, w_lead_ref, b_lead_ref, b_proj_ref, own_ref, came_ref, gain_ref, shift_ref,
    normed_ref, half_ref, mid_hbm, normed_hbm, mid_ref, sems,
):
    moves = Moves(sems)
    stream = start_ref[...].astype(f32) + lead_ref[s[1]] * w_lead_ref[...] + b_lead_ref[...]
    mid = (stream + b_proj_ref[...] + total(own_ref, came_ref)).astype(bf16)
    mid_ref[...] = mid
    saved = [moves.start(mid_ref, mid_hbm)]
    normal, _ = norm_parts(mid.astype(f32))
    normed_ref[...] = (normal * gain_ref[...] + shift_ref[...]).astype(bf16)
    saved.append(moves.start(normed_ref, normed_hbm))
    half_ref[...] = normed_ref[part_of(s[0], half_ref.shape[0]), :]
    wait(*saved)


def mlp_kernel(
    s, normed_ref, cot_hbm, w_up_hbm, b_up_ref, w_down_hbm, sums_ref, part_ref, hidden_hbm, pre_grad_hbm,
    hidden_ref, pre_grad_ref, w_up_ref, w_down_ref, cot_ref, sems,
):
    width = w_up_ref.shape[2]
    moves = Moves(sems)
    ups, downs, saved = [], [], []
    for n in range(2):
        place = part_of(2 * s[0] + n, width)
        ups.append(moves.start(w_up_hbm.at[:, place], w_up_ref.at[n]))
        if n == 0:
            cot_copy = moves.start(cot_hbm.at[part_of(s[1], cot_ref.shape[0]), :], cot_ref)
        downs.append(moves.start(w_down_hbm.at[place, :], w_down_ref.at[n]))
    wait(cot_copy)
    back = None
    for n in range(2):
        columns = slice(n * width, (n + 1) * width)
        wait(ups[n], downs[n])
        pre = dot(normed_ref[...], w_up_ref[n], (1, 0)) + b_up_ref[:, part_of(2 * s[0] + n, width)]
        hidden_grad = dot(cot_ref[...], w_down_ref[n], (1, 1))
        hidden, slope = gelu_both(pre)
        hidden_ref[n] = hidden.astype(bf16)
        pre_grad = hidden_grad * slope
        sums_ref[:, columns] = column_sums(pre_grad)
        low = pre_grad.astype(bf16)
        pre_grad_ref[n] = low
        term = dot(low, w_up_ref[n], (1, 1))
        back = term if back is None else back + term
        saved.append(moves.start(hidden_ref.at[n], hidden_hbm.at[n]))
        saved.append(moves.start(pre_grad_ref.at[n], pre_grad_hbm.at[n]))
    part_ref[...] = back.astype(bf16)
    wait(*saved)


def out_kernel(
    s, hidden_hbm, w_down_hbm, mid_hbm, b_down_ref, sent_ref, kept_ref, total_ref, hidden_ref, w_down_ref, mid_ref, sems
):
    width = w_down_ref.shape[1]
    rows = sent_ref.shape[0]
    moves = Moves(sems)
    copies = []
    for n in range(2):
        copies.append(moves.start(hidden_hbm.at[n], hidden_ref.at[n]))
        copies.append(moves.start(w_down_hbm.at[part_of(2 * s[0] + n, width), :], w_down_ref.at[n]))
    mid_copy = moves.start(mid_hbm.at[part_of(s[0], rows), :], mid_ref)
    wait(*copies[:2])
    result = dot(hidden_ref[0], w_down_ref[0], (1, 0))
    wait(*copies[2:])
    total_ref[...] = result + dot(hidden_ref[1], w_down_ref[1], (1, 0))
    wait(mid_copy)
    sent_ref[...] = total_ref[part_of(1 - s[0], rows), :].astype(bf16)
    kept_ref[...] = total_ref[part_of(s[0], rows), :] + mid_ref[...].astype(f32) + b_down_ref[...]


def attend_back_kernel(
    s, own_ref, came_ref, mid_hbm, cot_hbm, gain_ref, qkv_hbm, out_hbm, lse_hbm, w_proj_hbm, w_qkv_hbm,
    part_ref, sums_ref, keep_hbm, send_hbm, mid_grad_hbm,
    mid_ref, cot_ref, qkv_ref, out_ref, lse_ref, w_ref, w_proj_ref, grad_ref, back_ref, keep_ref, send_ref, mid_grad_ref,
    sems,
):
    seq = own_ref.shape[0]
    moves = Moves(sems)
    first = [moves.start(mid_hbm, mid_ref), moves.start(cot_hbm.at[part_of(s[1], seq), :], cot_ref)]
    proj_copy = moves.start(w_proj_hbm.at[part_of(s[0], HALF), :], w_proj_ref)
    copies = [
        moves.start(qkv_hbm, qkv_ref), moves.start(out_hbm, out_ref), moves.start(lse_hbm, lse_ref)
    ]
    heads = fetch_heads(moves, s, w_qkv_hbm, w_ref)
    grad = total(own_ref, came_ref)
    wait(*first)
    cot = cot_ref[...].astype(f32)
    normal, scale = norm_parts(mid_ref[...].astype(f32))
    mid_grad = cot + norm_back(normal, scale, gain_ref[...], grad)
    sums_ref[...] = jnp.concatenate(
        [column_sums(grad * normal), column_sums(grad), column_sums(mid_grad), column_sums(cot), jnp.zeros((4, D), f32)]
    )
    low = mid_grad.astype(bf16)
    mid_grad_ref[...] = low
    saved = [moves.start(mid_grad_ref, mid_grad_hbm)]
    wait(proj_copy, *copies)
    grad_ref[...] = dot(low, w_proj_ref[...], (1, 1)).astype(bf16)

    def one_pair(pair, carried):
        q, k, v = (qkv_ref[:, pair_columns(pair, part)] for part in range(3))
        out_grad = grad_ref[:, pair_columns(pair)]
        weighted = out_grad.astype(f32) * out_ref[:, pair_columns(pair)].astype(f32)
        norms = lse_ref[pair]
        results = []
        for half in range(2):
            logits = dot(only_half(q * jnp.asarray(0.125, bf16), half), k, (1, 1))
            probs = jnp.exp(logits - norms[:, half * HD : half * HD + 1])
            probs_grad = dot(only_half(out_grad, half), v, (1, 1))
            shift = jnp.sum(only_half(weighted, half), axis=1, keepdims=True)
            logits_grad = (probs * (probs_grad - shift)).astype(bf16)
            results.append(
                (
                    dot(logits_grad, k, (1, 0)) * 0.125,
                    dot(logits_grad, q, (0, 0)) * 0.125,
                    dot(probs.astype(bf16), out_grad, (0, 0)),
                )
            )
        for part, (low_head, high_head) in enumerate(zip(*results)):
            back_ref[:, pair_columns(pair, part)] = joined(low_head, high_head).astype(bf16)
        return carried

    lax.fori_loop(0, OWN_HEADS // 2, one_pair, 0)
    for part in range(3):
        columns = slice(part * QUARTER, (part + 1) * QUARTER)
        mine = pl.multiple_of(part * HALF + s[1] * QUARTER, LANES)
        theirs = pl.multiple_of(part * HALF + (1 - s[1]) * QUARTER, LANES)
        keep_ref[:, columns] = back_ref[:, pl.ds(mine, QUARTER)]
        send_ref[:, columns] = back_ref[:, pl.ds(theirs, QUARTER)]
    saved += [moves.start(keep_ref, keep_hbm), moves.start(send_ref, send_hbm)]
    wait(*heads)
    back = None
    for n in range(3):
        term = dot(back_ref[:, n * HALF : (n + 1) * HALF], w_ref[n], (1, 1))
        back = term if back is None else back + term
    part_ref[...] = back.astype(bf16)
    wait(*saved)


def start_back_kernel(
    s, own_ref, came_ref, start_hbm, lead_ref, w_lead_ref, b_lead_ref, gain_ref, mid_grad_hbm, w_out_hbm, pix_hbm,
    mask_hbm, coef_ref, tv_hbm, sums_ref, up_sums_ref,
    pix_keep_ref, pix_send_ref, side_hbm, small_ref,
    held_ref, w_out_ref, start_ref, mid_grad_ref, tv_ref, start_grad_ref, side_ref, pix_ref, mask_ref, sems,
):
    moves = Moves(sems)
    first = [moves.start(start_hbm, start_ref), moves.start(mid_grad_hbm, mid_grad_ref)]
    seq = own_ref.shape[0]
    sample = part_of(s[1], seq)
    copies = [
        moves.start(w_out_hbm.at[part_of(s[0], HALF), :], w_out_ref), moves.start(tv_hbm, tv_ref),
        moves.start(pix_hbm.at[:, sample], pix_ref), moves.start(mask_hbm.at[:, sample], mask_ref),
    ]
    grad = total(own_ref, came_ref)
    lead = lead_ref[s[1]]
    wait(*first)
    stream = start_ref[...].astype(f32) + lead * w_lead_ref[...] + b_lead_ref[...]
    normal, scale = norm_parts(stream)
    stream_grad = mid_grad_ref[...].astype(f32) + norm_back(normal, scale, gain_ref[...], grad)
    start_grad = stream_grad.astype(bf16)
    start_grad_ref[...] = start_grad
    for side in range(2):
        side_ref[:, side * QUARTER : (side + 1) * QUARTER] = start_grad_ref[:, quarter_columns(s, side)]
    saved = [moves.start(side_ref, side_hbm)]
    lead_sum = column_sums(stream_grad)
    vectors = [
        sums_ref[0:4, :],
        column_sums(grad * normal),
        column_sums(grad),
        lead_sum,
        lead * lead_sum,
        column_sums(start_grad.astype(f32)),
        up_sums_ref[:, :D],
        up_sums_ref[:, D:],
        jnp.zeros((SMALL_ROWS - 136 - 11, D), f32),
    ]
    wait(*copies)
    per_head_grad = dot(w_out_ref[...], start_grad, (1, 1)).astype(bf16)

    cells, seen, pen = load_cells(pix_ref, mask_ref, cell_order())
    coef = coef_ref[...]
    tv = tv_ref[...]
    lane = lax.broadcasted_iota(jnp.int32, (PADDED, LANES), 1)
    coef_grad = jnp.zeros((PADDED, LANES), f32)
    cell_grad = [jnp.zeros((VARS, cells.shape[1]), f32) for _ in range(PIX)]
    for h in range(OWN_HEADS):
        rows = slice(h * HD, (h + 1) * HD)
        weight = head_weights(cells, pen, coef, h)
        features = head_features(cells, weight)
        head_grad = per_head_grad[rows]
        small_rows = slice((h % 2) * HD, (h % 2 + 1) * HD)
        small_ref[small_rows, (h // 2) * PADDED : (h // 2 + 1) * PADDED] = dot(head_grad, features, (1, 1)).astype(bf16)
        feature_grad = dot(tv[rows], head_grad, (0, 0))
        weight_grad = feature_grad[CELLS:ROWS]
        for j in range(PIX):
            part = slice(j * VARS, (j + 1) * VARS)
            weight_grad = weight_grad + feature_grad[part] * cells[part]
        score_grad = weight * (weight_grad - jnp.sum(weight * weight_grad, axis=0, keepdims=True))
        sums = []
        for j in range(PIX):
            part = slice(j * VARS, (j + 1) * VARS)
            cell_grad[j] = cell_grad[j] + feature_grad[part] * weight + score_grad * coef[part, h : h + 1]
            sums.append(jnp.sum(score_grad * cells[part], axis=1, keepdims=True))
        sums.append(jnp.sum(score_grad, axis=1, keepdims=True))
        sums.append(jnp.zeros((PADDED - ROWS, 1), f32))
        coef_grad = jnp.where(lane == h, jnp.concatenate(sums, axis=0), coef_grad)
    coef_rows = jnp.transpose(coef_grad)[:OWN_HEADS]
    coef_rows = jnp.concatenate([coef_rows, jnp.zeros((OWN_HEADS, D - PADDED), f32)], axis=1)
    small_ref[LANES:, :] = jnp.concatenate([coef_rows] + vectors, axis=0).astype(bf16)
    cell_grads = (jnp.concatenate(cell_grad, axis=0) * seen).astype(bf16)
    held_ref[...] = dot(cell_order(), cell_grads, (0, 0))
    columns = pix_keep_ref.shape[1]
    pix_keep_ref[...] = held_ref[:, part_of(s[0], columns)]
    pix_send_ref[...] = held_ref[:, part_of(1 - s[0], columns)].astype(bf16)
    wait(*saved)


def quarter_columns(s, side):
    far = s[1] if side == 0 else 1 - s[1]
    return pl.ds(pl.multiple_of(s[0] * HALF + far * QUARTER, QUARTER), QUARTER)


def mlp_grads_kernel(
    s, normed_hbm, first_hbm, second_hbm, cot_hbm, w_up_hbm, b_up_ref, w_down_hbm, pre_grad_hbm, hidden_hbm,
    up_send_hbm, up_keep_hbm, down_send_hbm, down_keep_hbm,
    normed_ref, cot_ref, w_up_ref, w_down_ref, pre_grad_ref, hidden_ref, sum_ref, sems, *, piece, groups,
):
    width = w_up_ref.shape[1]
    rows = first_hbm.shape[0]
    seq = 2 * rows
    place = part_of(2 * s[0] + s[1], width)
    moves = Moves(sems)
    own, one, two = pl.ds(0, seq), pl.ds(seq, rows), pl.ds(seq + rows, rows)
    first = [
        moves.start(w_up_hbm.at[:, place], w_up_ref),
        moves.start(first_hbm, normed_ref.at[one, :]),
        moves.start(second_hbm, normed_ref.at[two, :]),
        moves.start(cot_hbm.at[part_of((1 - s[1]) * 2 + s[0], rows), :], cot_ref.at[one, :]),
        moves.start(cot_hbm.at[part_of((1 - s[1]) * 2 + (1 - s[0]), rows), :], cot_ref.at[two, :]),
        moves.start(w_down_hbm.at[place, :], w_down_ref),
    ]
    then = [
        moves.start(cot_hbm.at[part_of(s[1], seq), :], cot_ref.at[own, :]),
        moves.start(normed_hbm, normed_ref.at[own, :]),
        moves.start(hidden_hbm.at[s[1]], hidden_ref.at[own, :]),
        moves.start(pre_grad_hbm.at[s[1]], pre_grad_ref.at[own, :]),
    ]
    wait(*first)
    pre = dot(normed_ref[seq:, :], w_up_ref[...], (1, 0)) + b_up_ref[:, place]
    hidden_grad = dot(cot_ref[seq:, :], w_down_ref[...], (1, 1))
    hidden, slope = gelu_both(pre)
    hidden_ref[seq:, :] = hidden.astype(bf16)
    pre_grad_ref[seq:, :] = (hidden_grad * slope).astype(bf16)
    wait(*then)
    half = groups // 2 * piece
    outs = ((up_send_hbm, up_keep_hbm), (down_send_hbm, down_keep_hbm))
    saved = []
    for n, (left_ref, right_ref) in enumerate(((normed_ref, pre_grad_ref), (cot_ref, hidden_ref))):
        left = chosen(left_ref, [s[3 + n * groups + b] for b in range(groups)], piece)
        sum_ref[n] = dot(left, right_ref[...], (0, 0)).astype(bf16)
        send_hbm, keep_hbm = outs[n]
        saved.append(moves.start(sum_ref.at[n, half:, :], send_hbm))
        saved.append(moves.start(sum_ref.at[n, :half, :], keep_hbm))
    wait(*saved)


def chosen(ref, blocks, piece):
    return jnp.concatenate([ref[:, part_of(b, piece)] for b in blocks], axis=1)


def head_grads_kernel(
    s, normed_hbm, keep_hbm, send_hbm, attended_hbm, attended_far_hbm, mid_grad_hbm, one_send_hbm, one_keep_hbm,
    two_send_hbm, two_keep_hbm, normed_ref, right_ref, attended_ref, mid_ref, one_ref, two_ref, sems, *, piece, groups,
):
    moves = Moves(sems)
    copies = [
        moves.start(normed_hbm, normed_ref), moves.start(send_hbm, right_ref.at[1]), moves.start(keep_hbm, right_ref.at[0])
    ]
    then = [
        moves.start(attended_hbm, attended_ref.at[s[0]]),
        moves.start(attended_far_hbm, attended_ref.at[1 - s[0]]),
        moves.start(mid_grad_hbm.at[:, quarter_columns(s, 0)], mid_ref.at[:, :QUARTER]),
        moves.start(mid_grad_hbm.at[:, quarter_columns(s, 1)], mid_ref.at[:, QUARTER:]),
    ]
    blocks = [s[3 + n] for n in range(groups)]
    wait(*copies)
    left = chosen(normed_ref, [s[3 + groups + n] for n in range(groups)], piece)
    both_qk = 2 * QUARTER
    saved = []
    for side, target in ((1, one_send_hbm), (0, one_keep_hbm)):
        one_ref[side] = dot(left, right_ref[side, :, :both_qk], (0, 0)).astype(bf16)
        saved.append(moves.start(one_ref.at[side], target))
    left = chosen(normed_ref, blocks, piece)
    wait(*then)
    features = jnp.concatenate([attended_ref[b >> 2, :, part_of(b & 3, piece)] for b in blocks], axis=1)
    half = two_keep_hbm.shape[0]
    for rows, target in ((slice(half, 2 * half), two_send_hbm), (slice(0, half), two_keep_hbm)):
        for side in range(2):
            quarter = slice(side * QUARTER, (side + 1) * QUARTER)
            columns = side * both_qk
            value = dot(left[:, rows], right_ref[side, :, both_qk:], (0, 0))
            two_ref[rows, columns : columns + QUARTER] = value.astype(bf16)
            proj = dot(features[:, rows], mid_ref[:, quarter], (0, 0))
            two_ref[rows, columns + QUARTER : columns + both_qk] = proj.astype(bf16)
        saved.append(moves.start(two_ref.at[rows, :], target))
    wait(*saved)


def side_grads_kernel(
    s, head_hbm, head_far_hbm, start_hbm, small_ref, sent_ref, kept_ref, head_ref, start_ref, pos_ref, sems, *, piece, groups
):
    moves = Moves(sems)
    seq = start_ref.shape[0]
    wait(
        moves.start(head_hbm, head_ref.at[s[0]]),
        moves.start(head_far_hbm, head_ref.at[1 - s[0]]),
        moves.start(start_hbm, start_ref),
    )
    pos_ref[...] = start_ref[...].astype(f32)
    count = groups // 2
    for first in (count, 0):
        blocks = [s[3 + n] for n in range(first, first + count)]
        per_head = jnp.concatenate([head_ref[b >> 2, part_of(b & 3, piece), :] for b in blocks], axis=0)
        out = dot(per_head, start_ref[...], (1, 0)).astype(bf16)
        columns = []
        for side in range(2):
            quarter = slice(side * QUARTER, (side + 1) * QUARTER)
            pos = []
            for b in blocks:
                block = pos_ref[part_of(b, seq // groups), quarter]
                pos += [block[:, :LANES], block[:, LANES:]]
            columns += [out[:, quarter], jnp.concatenate(pos, axis=0).astype(bf16)]
        columns = jnp.concatenate(columns, axis=1)
        if first == 0:
            kept_ref[...] = columns
        else:
            sent_ref[...] = packed(columns, small_ref[...])


def by_squares(value):
    rows, columns = value.shape
    return jnp.concatenate(
        [
            jnp.concatenate([value[r : r + LANES, c : c + LANES] for r in range(0, rows, LANES)], axis=1)
            for c in range(0, columns, LANES)
        ],
        axis=0,
    )


def packed(side, small):
    width = side.shape[0]
    return jnp.concatenate([by_squares(side)] + [small[:, n : n + width] for n in range(0, D, width)], axis=0)


def unpacked(value, columns):
    small = value[columns:]
    parts = D // value.shape[1]
    return by_squares(value[:columns]), jnp.concatenate(
        [small[n * SMALL_ROWS : (n + 1) * SMALL_ROWS] for n in range(parts)], axis=1
    )


def both(one, two):
    return (one.astype(f32) + two.astype(f32)).astype(bf16)


def fetched_halves_kernel(s, one_hbm, one_came, two_hbm, two_came, *refs):
    *outs, one_ref, two_ref, sems = refs
    moves = Moves(sems)
    copies = [moves.start(one_hbm, one_ref), moves.start(two_hbm, two_ref)]
    for n, (kept, came) in enumerate(((one_ref, one_came), (two_ref, two_came))):
        copies[n].wait()
        keep, send = outs[2 * n : 2 * n + 2]
        half = keep.shape[0]
        send[...] = both(kept[half:], came[half:])
        keep[...] = both(kept[:half], came[:half])


def halves_kernel(s, *refs):
    count = len(refs) // 4
    for n in range(count):
        kept, came = refs[2 * n : 2 * n + 2]
        keep, send = refs[2 * count + 2 * n : 2 * count + 2 * n + 2]
        half = keep.shape[0]
        send[...] = both(kept[half:], came[half:])
        keep[...] = both(kept[:half], came[:half])


def heads_kernel(s, one_ref, one_came_ref, two_ref, two_came_ref, one_keep, one_send, two_keep, two_send, sems):
    half = one_keep.shape[0]
    one_send[...] = both(one_ref[half:], one_came_ref[half:])
    one_keep[...] = both(one_ref[:half], one_came_ref[:half])
    width = two_keep.shape[2]
    two_send[...] = both(two_ref[:, :, width:], two_came_ref[:, :, width:])
    two_keep[...] = both(two_ref[:, :, :width], two_came_ref[:, :, :width])


def side_step_kernel(s, side_ref, small_ref, came_ref, keep_ref, sum_ref, *rest):
    side, small = unpacked(came_ref[...], side_ref.shape[1])
    side = both(side_ref[...], side)
    small = both(small_ref[...], small)
    sum_ref[...] = small
    rows, columns = keep_ref.shape
    keep_ref[...] = side[:rows, :columns]
    if columns < side.shape[1]:
        rest[0][...] = packed(side[:, columns:], small)
    elif rows < side.shape[0]:
        rest[0][...] = packed(side[rows:], small)


def join_kernel(s, one_ref, two_ref, both_ref, sems):
    width = one_ref.shape[1]
    both_ref[:, :width] = one_ref[...]
    both_ref[:, width:] = two_ref[...]


def last_kernel(s, *refs):
    sum_ref = refs[-2]
    start = 0
    for n in range((len(refs) - 2) // 2):
        kept, came = refs[2 * n : 2 * n + 2]
        width = kept.shape[2]
        sum_ref[:, start : start + width] = both(kept[0], came[0])
        start += width


def sum_kernel(s, kept_ref, came_ref, sum_ref, sems):
    sum_ref[...] = both(kept_ref[...], came_ref[...])


def small_kernel(
    s, own_ref, came_ref, table_hbm, probe_ref, far_probe_ref, w_value_hbm, w_key_hbm, query_ref, w_query_hbm, cut_table_ref,
    cut_probe_ref, cut_query_ref,
    embed_ref, var_ref, value_grad_ref, key_grad_ref, query_grad_ref, vector_ref, bias_ref,
    table_ref, my_value_ref, w_key_ref, my_w_query_ref, sems, *, piece,
):
    moves = Moves(sems)
    mine = pl.ds(pl.multiple_of(s[2] * piece, piece), piece)
    copies = [
        moves.start(table_hbm, table_ref),
        moves.start(w_value_hbm.at[mine, :], my_value_ref),
        moves.start(w_key_hbm, w_key_ref),
        moves.start(w_query_hbm.at[mine, :], my_w_query_ref),
    ]
    own, came = own_ref[...], came_ref[...]
    swap = s[0] == 1
    low = jnp.where(swap, came, own)
    high = jnp.where(swap, own, came)
    probes = (probe_ref[...], far_probe_ref[...])
    probe_low = jnp.where(swap, probes[1], probes[0])
    probe_high = jnp.where(swap, probes[0], probes[1])
    my_table = cut_table_ref[...]
    my_probe = cut_probe_ref[...]
    marked = (lax.broadcasted_iota(jnp.int32, (8, PADDED), 1) == ROWS).astype(f32).astype(bf16)
    wait(*copies)
    my_value = my_value_ref[...]
    table_grad = None
    for c, part in enumerate((low, high)):
        for n in range(HALF // LANES):
            g = part[:LANES, n * PADDED : (n + 1) * PADDED]
            columns = slice(c * HALF + n * LANES, c * HALF + (n + 1) * LANES)
            value_grad_ref[:, columns] = dot(my_table, g, (0, 1))
            bias_ref[:, columns] = dot(marked, g, (1, 1))
            term = dot(g, my_value[:, columns], (0, 1))
            table_grad = term if table_grad is None else table_grad + term
    coef = jnp.concatenate([low[128:136, :PADDED].astype(f32), high[128:136, :PADDED].astype(f32)], axis=0) * 0.125
    coef_low = coef.astype(bf16)
    probe3 = in_three(my_probe)
    for n in range(3):
        table_grad = table_grad + dot(coef_low, probe3[n * HEADS : (n + 1) * HEADS], (0, 0))
    by_cell = in_three(table_grad[:CELLS])
    perm = cell_order()
    embed_ref[...] = sum(dot(perm, by_cell[n * CELLS : (n + 1) * CELLS], (0, 0)) for n in range(3))
    var_ref[...] = table_grad[CELLS:ROWS]
    probe_grad = dot(coef_low, table_ref[...], (1, 0))
    my_probe_grad = dot(coef_low, my_table, (1, 0))
    row = lax.broadcasted_iota(jnp.int32, (HEADS, D), 0)
    lane = lax.broadcasted_iota(jnp.int32, (HEADS, D), 1)
    own_head = (lane >= row * HD) & (lane < (row + 1) * HD)
    asked = jnp.concatenate([probe_low[8:9, :HALF], probe_high[8:9, :HALF]], axis=1)
    key_grad_ref[...] = dot(my_probe_grad, jnp.where(own_head, asked, 0.0), (0, 0), f32, highest)
    asked_grad = summed_rows(dot(in_three(probe_grad), w_key_ref[...], (1, 0)), HEADS)
    asked_grad = column_sums(jnp.where(own_head, asked_grad, 0.0))
    my_query = jnp.broadcast_to(cut_query_ref[...].astype(f32), (8, piece))
    first_row = lax.broadcasted_iota(jnp.int32, (8, D), 0) == 0
    query_grad_ref[...] = dot(my_query, jnp.where(first_row, asked_grad, 0.0), (0, 0), f32, highest)
    vector_ref[...] = summed_rows(dot(in_three(jnp.broadcast_to(asked_grad, (8, D))), my_w_query_ref[...], (1, 1)), 8)


def four_places(s, refs, width):
    for n, ref in enumerate(refs):
        core = s[0] if n < 2 else 1 - s[0]
        far = s[1] if n % 2 == 0 else 1 - s[1]
        yield ref[...].astype(f32), pl.multiple_of((core * 2 + far) * width, width)


def mlp_final_kernel(s, one_ref, two_ref, three_ref, four_ref, up_hbm, down_hbm, up_ref, down_ref, sems):
    width = one_ref.shape[1] // 2
    for block, start in four_places(s, (one_ref, two_ref, three_ref, four_ref), width):
        up_ref[:, pl.ds(start, width)] = block[:, :width]
        down_ref[pl.ds(start, width), :] = jnp.transpose(block[:, width:])
    moves = Moves(sems)
    wait(moves.start(up_ref, up_hbm), moves.start(down_ref, down_hbm))


def attend_final_kernel(s, one_ref, two_ref, three_ref, four_ref, qkv_ref, proj_ref, out_ref, pos_ref, sems):
    for block, start in four_places(s, (one_ref, two_ref, three_ref, four_ref), QUARTER):
        for n in range(3):
            place = pl.ds(pl.multiple_of(n * D + start, QUARTER), QUARTER)
            qkv_ref[:, place] = block[:, n * QUARTER : (n + 1) * QUARTER]
        place = pl.ds(start, QUARTER)
        proj_ref[:, place] = block[:, 3 * QUARTER : D]
        out_ref[:, place] = block[:, D : D + QUARTER]
        rows = pos_ref.shape[0]
        last = block[:, D + QUARTER :]
        pos_ref[:, place] = jnp.concatenate([last[:rows], last[rows:]], axis=1)


def bit_orders(groups):
    first = list(range(groups.bit_length() - 1))
    return first, first[1:] + first[:1]


def block_map(groups, way):
    order = bit_orders(groups)[way]
    bits = len(order)
    return [sum(1 << order[n] for n in range(bits) if j >> (bits - 1 - n) & 1) for j in range(groups)]


def swap_core(value):
    return lax.ppermute(value, "section", [(s, s ^ 1) for s in range(4)])


def swap_y(value):
    return lax.ppermute(value, "section", [(s, s ^ 2) for s in range(4)])


def swap_stage(value, groups, stage, way=0):
    bit = 1 << bit_orders(groups)[way][stage]
    return lax.ppermute(value, "dp", [(g, g ^ bit) for g in range(groups)])


def cut(value, start, length, axis):
    return lax.dynamic_slice_in_dim(value, start, length, axis)


def packed_narrow(side, small):
    return jnp.concatenate([side.reshape(-1), small.reshape(-1)]).reshape(-1, side.shape[0])


def unpacked_narrow(value, columns):
    flat = value.reshape(-1)
    size = columns * value.shape[1]
    return flat[:size].reshape(value.shape[1], columns), flat[size:].reshape(SMALL_ROWS, D)


def narrow_mlp_sums(blocks, second_blocks, piece, core, far, normed, first, second, cotangent, w_up, b_up, w_down, pre_grad, hidden):
    rows = first.shape[0]
    quarter = hidden.shape[2]
    order = lambda v, chosen_blocks: jnp.concatenate([cut(v, b * piece, piece, 1) for b in chosen_blocks], axis=1)
    other_cot = [cut(cotangent, ((1 - far) * 2 + c) * rows, rows, 0) for c in (core, 1 - core)]
    other = jnp.concatenate([first, second])
    pre = dot(other, cut(w_up, (2 * core + far) * quarter, quarter, 1), (1, 0)) + cut(
        b_up, (2 * core + far) * quarter, quarter, 0
    )
    gate, slope = gelu_both(pre)
    back = dot(jnp.concatenate(other_cot), cut(w_down, (2 * core + far) * quarter, quarter, 0), (1, 1))
    pre_grads = jnp.concatenate([lax.dynamic_index_in_dim(pre_grad, far, 0, False), (back * slope).astype(bf16)])
    hiddens = jnp.concatenate([lax.dynamic_index_in_dim(hidden, far, 0, False), gate.astype(bf16)])
    up = dot(order(jnp.concatenate([normed, other]), blocks), pre_grads, (0, 0), bf16)
    cots = jnp.concatenate([cut(cotangent, far * 2 * rows, 2 * rows, 0)] + other_cot)
    down = dot(order(cots, second_blocks), hiddens, (0, 0), bf16)
    return up[D // 2 :], up[: D // 2], down[D // 2 :], down[: D // 2]


def narrow_head_sums(blocks, second_blocks, piece, core, far, normed, keep, send, attended, attended_far, mid_grad):
    order = lambda v, way: jnp.concatenate([cut(v, b * piece, piece, 1) for b in way], axis=1)
    left = order(normed, second_blocks)
    features = [jnp.concatenate(v, axis=1) for v in ((attended, attended_far), (attended_far, attended))]
    features = order(jnp.where(core == 0, *features), blocks)
    one = [dot(left, v[:, : 2 * QUARTER], (0, 0), bf16) for v in (send, keep)]
    left = order(normed, blocks)
    parts = []
    for v, y in ((keep, far), (send, 1 - far)):
        parts.append(dot(left, v[:, 2 * QUARTER :], (0, 0), bf16))
        parts.append(dot(features, cut(mid_grad, core * HALF + y * QUARTER, QUARTER, 1), (0, 0), bf16))
    two = jnp.concatenate(parts, axis=1)
    return one + [two[D // 2 :], two[: D // 2]]


def narrow_side_sums(blocks, piece, core, head, head_far, start_sides, small):
    order = lambda v, width: jnp.concatenate([cut(v, b * width, width, 0) for b in blocks])
    heads = order(jnp.where(core == 0, *(jnp.concatenate(v) for v in ((head, head_far), (head_far, head)))), piece)
    count, seq = blocks.shape[0], head.shape[1]
    parts = []
    for side in range(2):
        start = start_sides[:, side * QUARTER : (side + 1) * QUARTER]
        parts.append(dot(heads, start, (1, 0), bf16))
        pos = order(start, seq // count).reshape(count, seq // count, 2, LANES)
        parts.append(jnp.transpose(pos, (0, 2, 1, 3)).reshape(-1, LANES))
    result = jnp.concatenate(parts, axis=1)
    return packed(result[D // 2 :], small), result[: D // 2]


def added(kept, arrived):
    return (kept.astype(f32) + arrived.astype(f32)).astype(bf16)


def local(
    pixels, cell_mask, lead_time, query, w_query, w_key, w_value, b_value, w_out, b_out, w_embed,
    var_embed, pos_embed, w_lead, b_lead, gain_one, shift_one, w_qkv, w_proj, b_proj, gain_two,
    shift_two, w_up, b_up, w_down, b_down, cotangent,
):
    groups = lax.axis_size("dp")
    stages = groups.bit_length() - 1
    me = lax.axis_index("dp")
    section = lax.axis_index("section")
    core, far = section % 2, section // 2
    seq = pixels.shape[0] // lead_time.shape[0]
    rows = seq // 2
    units = w_up.shape[1]
    quarter = units // 4
    piece = D // groups
    narrow = piece % LANES != 0
    blocks, second_blocks = (me ^ jnp.array(block_map(groups, way), jnp.int32) for way in range(2))
    scalars = jnp.concatenate([jnp.stack([core, far, me]), blocks, second_blocks]).astype(jnp.int32)
    row = lambda v: v.reshape(1, -1)
    pix, mask = jnp.transpose(pixels), jnp.transpose(cell_mask)
    lead = scalar(lead_time)
    half = groups // 2
    sizes = dict(piece=piece, groups=groups)
    held = lambda *shape: pltpu.VMEM(shape, bf16)
    wide = lambda *shape: pltpu.VMEM(shape, f32)
    kept_far = True

    start_part, per_head, coef, tv, table, probe = call(
        start_kernel,
        scalars,
        [
            remote(pix), remote(mask), remote(query.reshape(-1, LANES)), remote(w_query), remote(w_key), remote(w_value), remote(row(b_value)),
            remote(w_out), remote(w_embed), remote(var_embed),
        ],
        [
            ((seq, D), bf16), ((HALF, seq), bf16, kept_far), ((PADDED, OWN_HEADS), f32), ((HALF, PADDED), bf16, kept_far),
            ((PADDED, D), bf16, kept_far), ((16, D), f32),
        ],
        scratch=[
            held(D, HALF), held(D, HALF), held(D, HALF), held(HALF, D), held(HALF, seq), held(HALF, PADDED), held(PADDED, D),
            held(CELLS, seq), pltpu.VMEM((CELLS, seq), jnp.int32), held(CELLS, D), held(VARS, D), wide(1, D),
            held(D // LANES, LANES),
        ],
        us=6,
    )
    far_probe = swap_core(probe)
    start_near, proj_part, start, normed_one, qkv, lse, attended = call(
        attend_kernel,
        scalars,
        [
            start_part, swap_core(start_part), pos_embed, lead, row(w_lead), row(b_lead), row(b_out), row(gain_one),
            row(shift_one), remote(w_qkv), remote(w_proj),
        ],
        [
            ((seq, D), bf16), ((seq, D), bf16), ((seq, D), bf16, kept_far), ((seq, D), bf16, kept_far),
            ((seq, 3 * HALF), bf16, kept_far), ((OWN_HEADS // 2, seq, LANES), f32, kept_far),
            ((seq, HALF), bf16, kept_far),
        ],
        scratch=[
            held(3, D, HALF), held(HALF, D), held(seq, D), held(seq, 3 * HALF), wide(OWN_HEADS // 2, seq, LANES),
            held(seq, HALF),
        ],
        us=12,
        after=[far_probe],
    )
    proj_came = swap_core(proj_part)
    normed_near, half_two, mid, normed_two = call(
        middle_kernel,
        scalars,
        [
            start_near, lead, row(w_lead), row(b_lead), row(b_proj), proj_part, proj_came, row(gain_two), row(shift_two),
        ],
        [((seq, D), bf16), ((rows, D), bf16), ((seq, D), bf16, kept_far), ((seq, D), bf16, kept_far)],
        scratch=[held(seq, D)],
        us=2.5,
    )
    other_two = swap_y(half_two)
    up_sums, normed_part, hidden, pre_grad = call(
        mlp_kernel,
        scalars,
        [normed_near, remote(cotangent), remote(w_up), row(b_up), remote(w_down)],
        [
            ((1, 2 * quarter), f32), ((seq, D), bf16), ((2, seq, quarter), bf16, kept_far),
            ((2, seq, quarter), bf16, kept_far),
        ],
        scratch=[
            held(2, seq, quarter), held(2, seq, quarter), held(2, D, quarter), held(2, quarter, D), held(seq, D),
        ],
        mb=22,
        us=11,
    )
    normed_came = swap_core(normed_part)
    by_block = lambda value: value.reshape(half, piece, value.shape[1])
    def halved(arrays, after):
        outs = [((v.shape[0] // 2,) + v.shape[1:], bf16) for v in arrays[::2] for _ in range(2)]
        return call(halves_kernel, scalars, arrays, outs, us=600, mb=16, after=after)


    attended_far, per_head_far = swap_core(attended), swap_core(per_head)
    other_held, _ = lax.optimization_barrier((other_two, normed_part))
    other_two_far = swap_core(other_held)
    if narrow:
        up_send, up_keep, down_send, down_keep = narrow_mlp_sums(
            blocks, second_blocks, piece, core, far, normed_two, other_two, other_two_far, cotangent, w_up, b_up, w_down, pre_grad, hidden
        )
    else:
        up_send, up_keep, down_send, down_keep = call(
            functools.partial(mlp_grads_kernel, **sizes),
            scalars,
            [remote(normed_two), other_two, other_two_far, remote(cotangent), remote(w_up)]
            + [row(b_up), remote(w_down), remote(pre_grad), remote(hidden)],
            [((D // 2, quarter), bf16, kept_far)] * 4,
            scratch=[
                held(2 * seq, D), held(2 * seq, D), held(D, quarter), held(quarter, D), held(2 * seq, quarter),
                held(2 * seq, quarter), held(2, D, quarter),
            ],
            us=15,
            mb=24,
            after=[normed_came, attended_far, per_head_far],
        )
    up_keep, down_keep = by_block(up_keep), by_block(down_keep)
    up_came = swap_stage(by_block(up_send), groups, 0)
    down_came = swap_stage(by_block(down_send), groups, 0, 1)

    class Sum:
        def __init__(self, keep, way, stage, sent=None, came=None):
            self.keep, self.way, self.stage = keep, way, stage
            self.came = swap_stage(sent, groups, stage, way) if came is None else came

    def onward(sums, after):
        results = halved([v for x in sums for v in (x.keep, x.came)], after)
        for n, x in enumerate(sums):
            x.keep, x.stage = results[2 * n], x.stage + 1
            x.came = swap_stage(results[2 * n + 1], groups, x.stage, x.way)
        return results[0]

    def last(sums, after):
        columns = sum(x.keep.shape[2] for x in sums)
        arrays = [v for x in sums for v in (x.keep, x.came)]
        return call(last_kernel, scalars, arrays, [((piece, columns), bf16)], us=600, after=after)[0]

    norm_part, mid_sums, qkv_keep, qkv_send, mid_grad = call(
        attend_back_kernel,
        scalars,
        [
            normed_part, normed_came, remote(mid), remote(cotangent), row(gain_two), remote(qkv), remote(attended),
            remote(lse), remote(w_proj), remote(w_qkv),
        ],
        [
            ((seq, D), bf16), ((8, D), f32), ((seq, 3 * QUARTER), bf16, kept_far), ((seq, 3 * QUARTER), bf16, kept_far),
            ((seq, D), bf16, kept_far),
        ],
        scratch=[
            held(seq, D), held(seq, D), held(seq, 3 * HALF), held(seq, HALF), wide(OWN_HEADS // 2, seq, LANES),
            held(3, D, HALF), held(HALF, D), held(seq, HALF), held(seq, 3 * HALF), held(seq, 3 * QUARTER),
            held(seq, 3 * QUARTER), held(seq, D),
        ],
        mb=22,
        us=14,
        after=[remote(up_send)],
    )
    norm_came = swap_core(norm_part)
    if narrow:
        one_send, one_keep, two_send, two_keep = narrow_head_sums(
            blocks, second_blocks, piece, core, far, normed_one, qkv_keep, qkv_send, attended, attended_far, mid_grad
        )
    else:
        one_send, one_keep, two_send, two_keep = call(
            functools.partial(head_grads_kernel, **sizes),
            scalars,
            [remote(x) for x in (normed_one, qkv_keep, qkv_send, attended, attended_far, mid_grad)],
            [((D, HALF), bf16, kept_far)] * 2 + [((D // 2, D), bf16, kept_far)] * 2,
            scratch=[
                held(seq, D), held(2, seq, 3 * QUARTER), held(2, seq, HALF), held(seq, HALF), held(2, D, HALF), held(D, D),
            ],
            us=4,
            after=[norm_part],
        )
    one_came = swap_y(one_send.reshape(groups, piece, HALF))
    two_came = swap_stage(by_block(two_send), groups, 0)

    outs = [((half // 2, piece, quarter), bf16)] * 4
    up_keep, up_send, down_keep, down_send = call(
        fetched_halves_kernel,
        scalars,
        [remote(up_keep), up_came, remote(down_keep), down_came],
        outs,
        scratch=[held(half, piece, quarter)] * 2,
        us=600,
        after=[remote(one_send)],
    )
    up, down = Sum(up_keep, 0, 1, up_send), Sum(down_keep, 1, 1, down_send)

    pix_kept, pix_sent, start_sides, small = call(
        start_back_kernel,
        scalars,
        [
            norm_part, norm_came, remote(start), lead, row(w_lead), row(b_lead), row(gain_one), remote(mid_grad),
            remote(w_out), remote(pix), remote(mask), coef, remote(tv), mid_sums, up_sums,
        ],
        [
            ((CELLS, rows), f32), ((CELLS, rows), bf16), ((seq, HALF), bf16, kept_far), ((SMALL_ROWS, D), bf16),
        ],
        scratch=[
            wide(CELLS, seq), held(HALF, D), held(seq, D), held(seq, D), held(HALF, PADDED), held(seq, D),
            held(seq, HALF), held(CELLS, seq), pltpu.VMEM((CELLS, seq), jnp.int32),
        ],
        us=7,
        after=[up.keep],
    )

    if narrow:
        side_sent, side_keep = narrow_side_sums(blocks, piece, core, per_head, per_head_far, start_sides, small)
    else:
        side_sent, side_keep = call(
            functools.partial(side_grads_kernel, **sizes),
            scalars,
            [remote(x) for x in (per_head, per_head_far, start_sides)] + [small],
            [((2 * (QUARTER + LANES + SMALL_ROWS), HALF), bf16), ((HALF, 2 * (QUARTER + LANES)), bf16)],
            scratch=[held(2, HALF, seq), held(seq, HALF), wide(seq, HALF)],
            us=4,
            after=[small],
        )
    side_came = swap_stage(side_sent, groups, 0)
    out_sent, out_kept = call(
        out_kernel,
        scalars,
        [remote(hidden), remote(w_down), remote(mid), row(b_down)],
        [((rows, D), bf16), ((rows, D), f32)],
        scratch=[wide(seq, D), held(2, seq, quarter), held(2, quarter, D), held(rows, D)],
        us=4,
        after=[side_keep],
    )


    def summed(kept, arrived, after=()):
        return call(sum_kernel, scalars, [kept, arrived], [(kept.shape, bf16)], us=600, mb=16, after=after)[0]

    head_rows = ((half, piece, HALF), bf16)
    one_keep, one_send, two_keep, two_send = call(
        heads_kernel,
        scalars,
        [one_keep.reshape(groups, piece, HALF), one_came, by_block(two_keep), two_came],
        [head_rows] * 4,
        us=600,
        mb=16,
        after=[out_sent],
    )
    two_came = swap_y(two_send)
    stages = groups.bit_length() - 1

    one = Sum(one_keep, 1, 0, one_send)
    two = Sum(two_keep, 0, 0, came=two_came)
    after = one_keep
    for _ in range(stages - 2):
        after = onward([up, down], [after])

    def side_step(side, small, came, after):
        rows, columns = side.shape
        if columns > QUARTER + LANES:
            columns //= 2
            outs = [((rows, columns), bf16), (small.shape, bf16), ((columns + SMALL_ROWS * D // rows, rows), bf16)]
        elif rows == piece:
            outs = [(side.shape, bf16), (small.shape, bf16)]
        else:
            outs = [((rows // 2, columns), bf16), (small.shape, bf16)]
            outs.append(((columns + SMALL_ROWS * D * 2 // rows, rows // 2), bf16))
        if narrow and rows <= LANES:
            arrived = (unpacked if rows == LANES else unpacked_narrow)(came, columns)
            side, small = added(side, arrived[0]), added(small, arrived[1])
            if rows == piece:
                return side, small
            return side[: rows // 2], small, packed_narrow(side[rows // 2 :], small)
        return call(side_step_kernel, scalars, [side, small, came], outs, us=600, mb=16, after=after)

    side_keep, small, side_send = side_step(side_keep, small, side_came, [after])
    side_came = swap_y(side_send)
    after = onward([one, two], [side_keep])
    mlp_piece = last([up, down], [after])
    after = mlp_piece
    for stage in range(1, stages):
        side_keep, small, side_send = side_step(side_keep, small, side_came, [after])
        side_came = swap_stage(side_send, groups, stage)
        after = onward([one, two], [side_keep]) if stage < stages - 1 else side_keep
    probes = jnp.concatenate([jnp.where(core == c, probe, far_probe)[:OWN_HEADS] for c in range(2)])
    probes, table_late, query_late, _ = lax.optimization_barrier((probes, table, query, mlp_piece))
    my_probe = cut(probes, me * piece, piece, 1)
    my_table = cut(table_late, me * piece, piece, 1)
    my_query = row(cut(query_late, me * piece, piece, 0))
    mlp_held, _ = lax.optimization_barrier((mlp_piece, one.keep))
    mlp_y, mlp_core = swap_y(mlp_held), swap_core(mlp_held)
    heads_piece = last([one, two], [after])
    w_up_grad, w_down_grad = call(
        mlp_final_kernel,
        scalars,
        [mlp_piece, mlp_y, mlp_core, swap_core(mlp_y)],
        [((piece, units), f32, kept_far), ((units, piece), f32, kept_far)],
        scratch=[wide(piece, units), wide(units, piece)],
        us=1,
        after=[heads_piece],
    )
    side_keep, small = side_step(side_keep, small, side_came, [remote(w_up_grad), my_probe, my_query, my_table])
    other_small = swap_core(small)
    attend_piece = call(
        join_kernel, scalars, [heads_piece, side_keep], [((piece, D + QUARTER + LANES), bf16)], us=1, after=[small]
    )[0]
    attend_y, attend_core = swap_y(attend_piece), swap_core(attend_piece)
    embed_grad, var_grad, w_value_grad, w_key_grad, w_query_grad, query_rows, bias_rows = call(
        functools.partial(small_kernel, piece=piece),
        scalars,
        [
            small, other_small, remote(table), probe, far_probe, remote(w_value), remote(w_key), row(query),
            remote(w_query), my_table, my_probe, my_query,
        ],
        [
            ((CELLS, piece), f32), ((VARS, piece), f32), ((piece, D), f32), ((piece, D), f32), ((piece, D), f32),
            ((8, piece), f32), ((8, D), f32),
        ],
        scratch=[held(PADDED, D), held(piece, D), held(D, D), held(piece, D)],
        us=600,
        after=[attend_piece],
    )
    out_late, pix_late, _ = lax.optimization_barrier((out_sent, pix_sent, embed_grad))
    block_out = (out_kept + swap_core(out_late).astype(f32)).astype(bf16)
    pixels_grad = jnp.transpose(pix_kept + swap_core(pix_late).astype(f32))

    query_grad = query_rows[0]
    my_value_bias = cut(bias_rows, me * piece, piece, 1)[0]
    shared = jnp.where(core == 0, small, other_small)[136:145].astype(f32)
    shared = cut(shared, me * piece, piece, 1)
    gain_two_grad, shift_two_grad, b_proj_grad, b_down_grad, gain_one_grad = (shared[n] for n in range(5))
    shift_one_grad, b_lead_grad, w_lead_grad, b_out_grad = (shared[n] for n in range(5, 9))
    up_rows = [jnp.where(core == c, small, other_small)[145:147] for c in range(2)]
    up_bias_grad = jnp.concatenate(up_rows).reshape(-1).astype(f32)
    my_up_bias = cut(up_bias_grad, me * (units // groups), units // groups, 0)

    w_qkv_grad, w_proj_grad, w_out_grad, pos_grad = call(
        attend_final_kernel,
        scalars,
        [attend_piece, attend_y, attend_core, swap_core(attend_y)],
        [((piece, 3 * D), f32), ((piece, D), f32), ((piece, D), f32), ((seq // groups, D), f32)],
        after=[embed_grad, block_out],
    )
    return (
        block_out, pixels_grad, query_grad, w_query_grad, w_key_grad, w_value_grad, my_value_bias, w_out_grad, b_out_grad,
        embed_grad, var_grad, pos_grad, w_lead_grad, b_lead_grad, gain_one_grad, shift_one_grad, w_qkv_grad, w_proj_grad,
        b_proj_grad, gain_two_grad, shift_two_grad, w_up_grad, my_up_bias, w_down_grad, b_down_grad,
    )


def solution(mesh):
    whole = P()
    args = (P("dp", None), P("dp", None), P("dp")) + (whole,) * 23 + (P("dp", None),)
    outs = (
        (P(axes, None),) * 2
        + (P("dp"),)
        + (P("dp", None),) * 3
        + (P("dp"), P("dp", None), P("dp"), P(None, "dp"), P(None, "dp"), P("dp", None))
        + (P("dp"),) * 4
        + (P("dp", None),) * 2
        + (P("dp"),) * 3
        + (P("dp", None), P("dp"), P(None, "dp"), P("dp"))
    )
    return jax.shard_map(local, mesh=mesh, in_specs=args, out_specs=outs, check_vma=False)
```
